32 devices in a mesh: dp: 4 (over z), section: 2 (over core), head: 4 (over y, x).
Axes of the slice: x: 2, y: 2, z: 4, core: 2. Of those that a mesh axis runs over, the one named last changes fastest.
Arguments:
- text_in: bfloat16 [512, 16, 768], P(('dp', 'section')), may hold values from -6 to 6
- lengths: int32 [512], P(('dp', 'section')), may hold values from 4 to 16, as said below
- image_embed: bfloat16 [512, 768], P(('dp', 'section')), may hold values from -6 to 6
- base_gain_one: float32 [768], replicated, may hold values from 0.25 to 1.75
- base_bias_one: float32 [768], replicated, may hold values from -1.75 to 1.75
- base_w_qkv: bfloat16 [768, 3, 768], P(None, None, 'head'), may hold values from -0.21875 to 0.21875
- base_b_qv: float32 [2, 768], P(None, 'head'), may hold values from -1.75 to 1.75
- base_w_out: bfloat16 [768, 768], P('head'), may hold values from -0.4375 to 0.4375
- base_b_out: float32 [768], replicated, may hold values from -1.75 to 1.75
- base_gain_two: float32 [768], replicated, may hold values from 0.25 to 1.75
- base_bias_two: float32 [768], replicated, may hold values from -1.75 to 1.75
- base_w_up: bfloat16 [768, 3072], P(None, 'head'), may hold values from -0.21875 to 0.21875
- base_b_up: float32 [3072], P('head'), may hold values from -1.75 to 1.75
- base_w_down: bfloat16 [3072, 768], P('head'), may hold values from -0.109375 to 0.109375
- base_b_down: float32 [768], replicated, may hold values from -1.75 to 1.75
- gain_one: float32 [768], replicated, may hold values from 0.25 to 1.75
- bias_one: float32 [768], replicated, may hold values from -1.75 to 1.75
- w_qkv: bfloat16 [768, 3, 768], P(None, None, 'head'), may hold values from -0.21875 to 0.21875
- b_qv: float32 [2, 768], P(None, 'head'), may hold values from -1.75 to 1.75
- output_weight: bfloat16 [768, 768], P('head'), may hold values from -0.4375 to 0.4375
- b_out: float32 [768], replicated, may hold values from -1.75 to 1.75
- gain_two: float32 [768], replicated, may hold values from 0.25 to 1.75
- bias_two: float32 [768], replicated, may hold values from -1.75 to 1.75
- w_up: bfloat16 [768, 3072], P(None, 'head'), may hold values from -0.21875 to 0.21875
- b_up: float32 [3072], P('head'), may hold values from -1.75 to 1.75
- w_down: bfloat16 [3072, 768], P('head'), may hold values from -0.109375 to 0.109375
- b_down: float32 [768], replicated, may hold values from -1.75 to 1.75
Outputs:
- loss: float32 [], replicated
- grad_text: float32 [512, 16, 768], P(('dp', 'section'))
- grad_base_gain_one: float32 [768], replicated
- grad_base_bias_one: float32 [768], replicated
- grad_base_w_qkv: float32 [768, 3, 768], P(None, None, 'head')
- grad_base_b_qv: float32 [2, 768], P(None, 'head')
- grad_base_w_out: float32 [768, 768], P('head')
- grad_base_b_out: float32 [768], replicated
- grad_base_gain_two: float32 [768], replicated
- grad_base_bias_two: float32 [768], replicated
- grad_base_w_up: float32 [768, 3072], P(None, 'head')
- grad_base_b_up: float32 [3072], P('head')
- grad_base_w_down: float32 [3072, 768], P('head')
- grad_base_b_down: float32 [768], replicated
- grad_gain_one: float32 [768], replicated
- grad_bias_one: float32 [768], replicated
- grad_w_qkv: float32 [768, 3, 768], P(None, None, 'head')
- grad_b_qv: float32 [2, 768], P(None, 'head')
- grad_w_out: float32 [768, 768], P('head')
- grad_b_out: float32 [768], replicated
- grad_gain_two: float32 [768], replicated
- grad_bias_two: float32 [768], replicated
- grad_w_up: float32 [768, 3072], P(None, 'head')
- grad_b_up: float32 [3072], P('head')
- grad_w_down: float32 [3072, 768], P('head')
- grad_b_down: float32 [768], replicated
The draws below stay inside these ranges and needn't reach their ends.
Inputs may be any that keep to these rules, and one draw needn't show every extreme that they name: `lengths`: slots from a caption's length on are padding; some caption has 16 tokens and some 4.
All inputs are finite; a program needn't handle non-finite values.
Results may differ from the reference program's by a relative error of at most 0.029.
Values may be sent and summed in bfloat16 or wider, within the bound.
A program may use at most 128 MiB of HBM per device.

```python
import math
from functools import partial
import jax
import jax.numpy as jnp
from jax import lax

D = 768
HEADS = 12
HEAD_DIM = 64
FF = 3072
LEN = 16
MIN_LEN = 4
BATCH = 512


def draw_lengths(key, part):
    key = jax.random.fold_in(key, 11)
    first_key, second_key, third_key = jax.random.split(key, 3)
    drawn = jax.random.randint(first_key, (BATCH,), MIN_LEN, LEN + 1)
    longest = jax.random.randint(second_key, (), 0, BATCH)
    offset = jax.random.randint(third_key, (), 1, BATCH)
    shortest = (longest + offset) % BATCH
    drawn = drawn.at[longest].set(LEN)
    drawn = drawn.at[shortest].set(MIN_LEN)
    return drawn.astype(jnp.int32)


def shard_levels(rng, extent, shards, low, top_value):
    def one(axis_at, blocks):
        draws = jax.random.uniform(jax.random.fold_in(jax.random.fold_in(rng, 6), axis_at), (blocks,), jnp.float32, low / len(shards), top_value / len(shards))
        return jnp.repeat(jnp.exp(draws), extent[axis_at] // blocks).reshape((-1,) + (1,) * (len(extent) - axis_at - 1))

    loudness = one(*shards[0])
    for cut in shards[1:]:
        loudness = loudness * one(*cut)
    return loudness


def gaussian(key, extent, scale, limit, shards=(), kind=jnp.bfloat16):
    values = scale * jax.random.normal(key, extent, jnp.float32)
    if shards:
        values = values * shard_levels(key, extent, shards, -0.22, 0.18)
    return jnp.clip(values, -limit, limit).astype(kind)


def setup_inputs(seed: int = 0) -> dict:
    splits = jax.random.split(jax.random.key(seed), 28)
    return {
        "text_in": gaussian(splits[0], (BATCH, LEN, D), 1.0, 6.0, ((0, 8),)),
        "lengths": draw_lengths(jax.random.fold_in(splits[27], 71), 0),
        "image_embed": gaussian(splits[2], (BATCH, D), 1.0, 6.0, ((0, 8),)),
        "base_gain_one": jnp.clip(1.0 + 0.15 * jax.random.normal(splits[3], (D,), jnp.float32), 0.25, 1.75),
        "base_bias_one": gaussian(splits[4], (D,), 0.3, 1.75, (), jnp.float32),
        "base_w_qkv": gaussian(splits[5], (D, 3, D), D ** -0.5, 0.21875, ((2, 4),)),
        "base_b_qv": gaussian(splits[6], (2, D), 0.3, 1.75, ((1, 4),), jnp.float32),
        "base_w_out": gaussian(splits[7], (D, D), (D // 4) ** -0.5, 0.4375, ((0, 4),)),
        "base_b_out": gaussian(splits[8], (D,), 0.3, 1.75, (), jnp.float32),
        "base_gain_two": jnp.clip(1.0 + 0.15 * jax.random.normal(splits[9], (D,), jnp.float32), 0.25, 1.75),
        "base_bias_two": gaussian(splits[10], (D,), 0.3, 1.75, (), jnp.float32),
        "base_w_up": gaussian(splits[11], (D, FF), D ** -0.5, 0.21875, ((1, 4),)),
        "base_b_up": gaussian(splits[12], (FF,), 0.3, 1.75, ((0, 4),), jnp.float32),
        "base_w_down": gaussian(splits[13], (FF, D), FF ** -0.5, 0.109375, ((0, 4),)),
        "base_b_down": gaussian(splits[14], (D,), 0.3, 1.75, (), jnp.float32),
        "gain_one": jnp.clip(1.0 + 0.15 * jax.random.normal(splits[15], (D,), jnp.float32), 0.25, 1.75),
        "bias_one": gaussian(splits[16], (D,), 0.3, 1.75, (), jnp.float32),
        "w_qkv": gaussian(splits[17], (D, 3, D), D ** -0.5, 0.21875, ((2, 4),)),
        "b_qv": gaussian(splits[18], (2, D), 0.3, 1.75, ((1, 4),), jnp.float32),
        "output_weight": gaussian(splits[19], (D, D), (D // 4) ** -0.5, 0.4375, ((0, 4),)),
        "b_out": gaussian(splits[20], (D,), 0.3, 1.75, (), jnp.float32),
        "gain_two": jnp.clip(1.0 + 0.15 * jax.random.normal(splits[21], (D,), jnp.float32), 0.25, 1.75),
        "bias_two": gaussian(splits[22], (D,), 0.3, 1.75, (), jnp.float32),
        "w_up": gaussian(splits[23], (D, FF), D ** -0.5, 0.21875, ((1, 4),)),
        "b_up": gaussian(splits[24], (FF,), 0.3, 1.75, ((0, 4),), jnp.float32),
        "w_down": gaussian(splits[25], (FF, D), FF ** -0.5, 0.109375, ((0, 4),)),
        "b_down": gaussian(splits[26], (D,), 0.3, 1.75, (), jnp.float32),
    }


@jax.custom_vjp
def low(v):
    return lax.optimization_barrier(v.astype(jnp.bfloat16)).astype(jnp.float32)

@jax.custom_vjp
def reduced_backward(v):
    return v

def low_keep(v):
    return (low(v), None)

def low_pass(kept, grad):
    return (grad,)

def back_keep(v):
    return (v, None)

def back_low(kept, grad):
    return (low(grad),)
low.defvjp(low_keep, low_pass)
reduced_backward.defvjp(back_keep, back_low)
norm_eps = 1e-06
logit_scale = 50.0
highest_precision = lax.Precision.HIGHEST

def layer_norm(values, gain_vec, bias_vec):
    center = lax.optimization_barrier(jnp.mean(values, -1, keepdims=True))
    shifted = values - center
    spread = lax.optimization_barrier(jnp.mean(shifted * shifted, -1, keepdims=True))
    return shifted * lax.rsqrt(spread + norm_eps) * gain_vec + bias_vec

def unit_rows(values):
    return values * lax.rsqrt(lax.optimization_barrier(jnp.mean(values * values, -1, keepdims=True)) + norm_eps) * values.shape[-1] ** (-0.5)

def text_layer(weights, inputs, valid):
    gain_one, bias_one, w_qkv, b_qv, output_weight, b_out, gain_two, bias_two, w_up, b_up, w_down, b_down = weights
    groups = inputs.shape[0]
    normed = low(layer_norm(inputs, gain_one, bias_one))
    project = jnp.einsum('gld,dkc->glkc', normed, w_qkv, precision=highest_precision)
    query = low(reduced_backward(project[:, :, 0] + b_qv[0])).reshape(groups, LEN, HEADS, HEAD_DIM)
    keys = low(reduced_backward(project[:, :, 1])).reshape(groups, LEN, HEADS, HEAD_DIM)
    values = low(reduced_backward(project[:, :, 2] + b_qv[1])).reshape(groups, LEN, HEADS, HEAD_DIM)
    scores = reduced_backward(jnp.einsum('gihe,gjhe->ghij', query, keys, precision=highest_precision) * HEAD_DIM ** (-0.5))
    scores = jnp.where(valid[:, None, None, :], scores, -1000000000.0)
    probs = low(jax.nn.softmax(scores, -1))
    mixed_heads = low(reduced_backward(jnp.einsum('ghij,gjhe->gihe', probs, values, precision=highest_precision))).reshape(groups, LEN, D)
    attended_output = reduced_backward(jnp.einsum('ykz,zn->ykn', mixed_heads, output_weight, precision=highest_precision))
    resid_one = inputs + attended_output + b_out
    normed_two = low(layer_norm(resid_one, gain_two, bias_two))
    upper = reduced_backward(jnp.einsum('gld,df->glf', normed_two, w_up, precision=highest_precision) + b_up)
    hidden = low(jax.nn.gelu(upper))
    branch = reduced_backward(jnp.einsum('glf,fd->gld', hidden, w_down, precision=highest_precision))
    return resid_one + branch + b_down

def encode(weights, block):
    inputs, caption_len = block
    base_weights, top_weights = weights
    positions = jnp.arange(LEN, dtype=jnp.int32)
    valid = positions[None, :] < caption_len[:, None]
    picker = (positions[None, :] == caption_len[:, None] - 1).astype(jnp.float32)
    middle = text_layer(base_weights, inputs, valid)
    result = text_layer(top_weights, middle, valid)
    return jnp.einsum('gl,gld->gd', picker, result, precision=highest_precision)

def contrast(pooled, images):
    text_unit = low(unit_rows(pooled))
    image_unit = low(unit_rows(images))
    scores_row = reduced_backward(logit_scale * jnp.dot(text_unit, image_unit.T, precision=highest_precision))
    scores_col = reduced_backward(logit_scale * jnp.dot(text_unit, image_unit.T, precision=highest_precision))
    row_part = jnp.sum(jax.nn.logsumexp(scores_row, 1) - jnp.diagonal(scores_row))
    col_part = jnp.sum(jax.nn.logsumexp(scores_col, 0) - jnp.diagonal(scores_col))
    return (row_part + col_part) / (2 * BATCH)

def reference(text_in, lengths, image_embed, base_gain_one, base_bias_one, base_w_qkv, base_b_qv, base_w_out, base_b_out, base_gain_two, base_bias_two, base_w_up, base_b_up, base_w_down, base_b_down, gain_one, bias_one, w_qkv, b_qv, output_weight, b_out, gain_two, bias_two, w_up, b_up, w_down, b_down):
    base_weights = tuple((entry.astype(jnp.float32) for entry in (base_gain_one, base_bias_one, base_w_qkv, base_b_qv, base_w_out, base_b_out, base_gain_two, base_bias_two, base_w_up, base_b_up, base_w_down, base_b_down)))
    top_weights = tuple((entry.astype(jnp.float32) for entry in (gain_one, bias_one, w_qkv, b_qv, output_weight, b_out, gain_two, bias_two, w_up, b_up, w_down, b_down)))
    block_rows = math.gcd(BATCH, 256)
    count_blocks = BATCH // block_rows
    images = image_embed.astype(jnp.float32)
    length_blocks = lengths.astype(jnp.int32).reshape(count_blocks, block_rows)

    def total(inputs, params):
        encoder = jax.checkpoint(partial(encode, params))

        def advance(carry, block):
            return (carry, encoder(block))
        blocks = inputs.reshape(count_blocks, block_rows, LEN, D)
        unused, pooled = lax.scan(advance, jnp.zeros((), jnp.float32), (blocks, length_blocks))
        return contrast(pooled.reshape(BATCH, D), images)
    loss, pullback = jax.vjp(total, text_in.astype(jnp.float32), (base_weights, top_weights))
    grad_text, grad_pair = pullback(jnp.ones((), jnp.float32))
    return (loss, grad_text) + tuple(grad_pair[0]) + tuple(grad_pair[1])
```

```python
import functools

import jax
import jax.numpy as jnp
from jax import lax
from jax.experimental import pallas as pl
from jax.experimental.pallas import tpu as pltpu
from jax.sharding import PartitionSpec as P

HEAD_DIM = 64
NORM_EPS = 1e-06
LOGIT_SCALE = 50.0
NEG = -1e30
BF = jnp.bfloat16
F32 = jnp.float32
MESH = pl.DeviceIdType.MESH
VMEM_LIMIT = 56 * 2**20


def dot(a, b):
    return lax.dot_general(a, b, (((1,), (0,)), ((), ())), preferred_element_type=F32)


def dot_nt(a, b):
    return lax.dot_general(a, b, (((1,), (1,)), ((), ())), preferred_element_type=F32)


def dot_tn(a, b):
    return lax.dot_general(a, b, (((0,), (0,)), ((), ())), preferred_element_type=F32)


def norm_stats(values):
    center = jnp.mean(values, -1, keepdims=True)
    shifted = values - center
    spread = jnp.mean(shifted * shifted, -1, keepdims=True)
    rstd = lax.rsqrt(spread + NORM_EPS)
    return shifted * rstd, rstd


def norm_back(grad, hat, rstd, gain):
    scaled = grad * gain
    m1 = jnp.mean(scaled, -1, keepdims=True)
    m2 = jnp.mean(scaled * hat, -1, keepdims=True)
    return rstd * (scaled - m1 - hat * m2)


def rows_sum(values):
    return jnp.sum(values, 0, keepdims=True)


def gelu_pair(u):
    c = 0.7978845608028654
    u2 = u * u
    t = jnp.tanh(c * u * (1.0 + 0.044715 * u2))
    half = 0.5 * (1.0 + t)
    value = u * half
    slope = half + 0.5 * u * (1.0 - t * t) * (c * (1.0 + 3.0 * 0.044715 * u2))
    return value, slope


def head_masks(width, kind):
    lane = lax.broadcasted_iota(jnp.int32, (1, width), 1)
    return [
        jnp.where((lane >= i * HEAD_DIM) & (lane < (i + 1) * HEAD_DIM), 1.0, 0.0).astype(kind)
        for i in range(width // HEAD_DIM)
    ]


class Place:
    def __init__(self):
        self.z = lax.axis_index("dp")
        self.s = lax.axis_index("section")
        h = lax.axis_index("head")
        self.h = h
        self.hi = lax.div(h, 2)
        self.lo = lax.rem(h, 2)
        self.hx = self.block(0, 1)
        self.hy = self.block(1, 0)
        self.hd = self.block(1, 1)

    def block(self, flip_hi, flip_lo):
        return lax.rem(self.hi + flip_hi, 2) * 2 + lax.rem(self.lo + flip_lo, 2)

    def head(self, other):
        return (self.z, self.s, other)

    def greet(self, devices):
        barrier = pltpu.get_barrier_semaphore()
        for device in devices:
            pl.semaphore_signal(barrier, inc=1, device_id=device, device_id_type=MESH)
        pl.semaphore_wait(barrier, len(devices))


def remote(src, dst, send_sem, recv_sem, device):
    return pltpu.make_async_remote_copy(
        src_ref=src,
        dst_ref=dst,
        send_sem=send_sem,
        recv_sem=recv_sem,
        device_id=device,
        device_id_type=MESH,
    )


class Gather:
    def __init__(self, at, ref, send, recv, block):
        half = block // 2

        def rows(owner, part):
            return ref.at[pl.ds(pl.multiple_of(owner * block + part * half, half), half)]

        def copy(i, owner, part, target):
            piece = rows(owner, part)
            return remote(piece, piece, send.at[i], recv.at[i], at.head(target))

        self.c = [
            copy(0, at.h, 0, at.hx),
            copy(1, at.h, 1, at.hy),
            copy(2, at.h, 1, at.hx),
            copy(3, at.h, 0, at.hy),
            copy(4, at.hx, 0, at.hy),
            copy(5, at.hy, 1, at.hx),
        ]

    def start(self):
        for i in range(4):
            self.c[i].start()

    def forward(self):
        self.c[0].wait_recv()
        self.c[4].start()
        self.c[1].wait_recv()
        self.c[5].start()

    def wait_x(self):
        self.c[2].wait_recv()

    def wait_y(self):
        self.c[3].wait_recv()

    def wait_d(self):
        self.c[4].wait_recv()
        self.c[5].wait_recv()

    def finish(self):
        for copy in self.c:
            copy.wait_send()


class Scatter:
    def __init__(self, at, part, got, send, recv, block):
        half = block // 2
        self.at, self.part, self.got, self.half = at, part, got, half

        def piece(owner, side):
            return part.at[owner, pl.ds(side * half, half)]

        def copy(i, owner, side, target):
            return remote(piece(owner, side), got.at[i], send.at[i], recv.at[i], at.head(target))

        self.c = [
            copy(0, at.hd, 0, at.hx),
            copy(1, at.hd, 1, at.hy),
            copy(2, at.hx, 0, at.hx),
            copy(3, at.hy, 1, at.hy),
            copy(4, at.hy, 0, at.hy),
            copy(5, at.hx, 1, at.hx),
        ]

    def send_d(self):
        self.c[0].start()
        self.c[1].start()

    def send_x(self):
        self.c[2].start()

    def send_y(self):
        self.c[3].start()

    def second(self):
        half, part, got, at = self.half, self.part, self.got, self.at
        self.c[0].wait_recv()
        part[at.hy, :half] = (part[at.hy, :half].astype(F32) + got[0].astype(F32)).astype(BF)
        self.c[4].start()
        self.c[1].wait_recv()
        part[at.hx, half:] = (part[at.hx, half:].astype(F32) + got[1].astype(F32)).astype(BF)
        self.c[5].start()

    def wait(self):
        for i in (2, 3, 4, 5):
            self.c[i].wait_recv()

    def total(self):
        half, part, got, at = self.half, self.part, self.got, self.at
        top = part[at.h, :half].astype(F32) + got[2].astype(F32) + got[4].astype(F32)
        low = part[at.h, half:].astype(F32) + got[3].astype(F32) + got[5].astype(F32)
        return jnp.concatenate([top, low], 0)

    def finish(self):
        for copy in self.c:
            copy.wait_send()


def first_forward_kernel(
    dp,
    block,
    slots,
    x,
    kbias,
    image,
    g1,
    c1,
    wqkv,
    bqv,
    wo,
    bo,
    g2,
    c2,
    wu,
    bu,
    wd,
    bd,
    w2,
    b2,
    n1,
    q,
    k,
    v,
    p,
    o,
    n2,
    hid,
    slope,
    r1,
    z,
    w2all,
    b2all,
    images,
    part_a,
    got_a,
    part_b,
    got_b,
    unit,
    sa_send,
    sa_recv,
    ag_send,
    ag_recv,
    sb_send,
    sb_recv,
    w_send,
    w_recv,
    b_send,
    b_recv,
    i_send,
    i_recv,
    local_sem,
):
    at = Place()
    local = wo.shape[0]
    heads = local // HEAD_DIM
    sub = 128
    other_core = (at.z, 1 - at.s, at.h)
    zs = [(lax.rem(at.z + j, dp), at.s, at.h) for j in range(1, dp)]
    z_pair = (at.z + 1 - 2 * lax.rem(at.z, 2), at.s, at.h)
    head_peers = [at.hx, at.hy, at.hd]

    own_w = pltpu.make_async_copy(w2, w2all.at[at.h], local_sem.at[0])
    own_w.start()
    own_b = pltpu.make_async_copy(b2, b2all.at[at.h], local_sem.at[1])
    own_b.start()
    pic = image[...].astype(F32)
    width = pic.shape[1]
    pic = pic * lax.rsqrt(jnp.mean(pic * pic, -1, keepdims=True) + NORM_EPS) * width ** (-0.5)
    unit[...] = pic.astype(BF)
    own_i = pltpu.make_async_copy(unit, images.at[at.z, at.s], local_sem.at[2])
    own_i.start()

    at.greet([at.head(j) for j in head_peers] + zs + [other_core])

    quarter = w2.shape[1] // 4
    mine = lax.rem(at.z, 2) * 2 + at.s
    pair = (1 - lax.rem(at.z, 2)) * 2 + at.s

    def span(which):
        return pl.ds(pl.multiple_of(which * quarter, quarter), quarter)

    hop1 = []
    for i, j in enumerate(head_peers):
        hop1.append(
            remote(
                w2.at[:, span(mine)],
                w2all.at[at.h, :, span(mine)],
                w_send.at[i],
                w_recv.at[i],
                at.head(j),
            )
        )
        hop1.append(remote(b2, b2all.at[at.h], b_send.at[i], b_recv.at[i], at.head(j)))
    hop2, hop3 = [], []
    for i, j in enumerate(head_peers):
        piece = w2all.at[j, :, span(mine)]
        hop2.append(remote(piece, piece, w_send.at[3 + i], w_recv.at[3 + i], z_pair))
        hop3.append(remote(piece, piece, w_send.at[6 + i], w_recv.at[6 + i], other_core))
        piece = w2all.at[j, :, span(pair)]
        hop3.append(remote(piece, piece, w_send.at[9 + i], w_recv.at[9 + i], other_core))
    for copy in hop1:
        copy.start()
    pics = [
        remote(unit, images.at[at.z, at.s], i_send.at[i], i_recv.at[i], device)
        for i, device in enumerate(zs)
    ]
    for copy in pics:
        copy.start()
    core_pics = remote(
        images.at[:, at.s], images.at[:, at.s], i_send.at[dp - 1], i_recv.at[dp - 1], other_core
    )

    scatter = Scatter(at, part_a, got_a, sa_send, sa_recv, block)
    masks_low = head_masks(local, BF)
    masks = head_masks(local, F32)
    row_id = lax.broadcasted_iota(jnp.int32, (sub, sub), 0) // slots
    col_id = lax.broadcasted_iota(jnp.int32, (sub, sub), 1) // slots
    same = row_id == col_id

    def attend(t, carry):
        blk = lax.rem(at.hi + lax.rem(t + 1, 2), 2) * 2 + lax.rem(at.lo + lax.div(3 - t, 2), 2)
        first = pl.multiple_of(blk * block, block)
        rows = pl.ds(first, block)
        hat, _ = norm_stats(x[rows].astype(F32))
        normed = (hat * g1[...] + c1[...]).astype(BF)
        n1[rows] = normed
        query = (dot(normed, wqkv[0]) + bqv[0]).astype(BF)
        keys = dot(normed, wqkv[1]).astype(BF)
        values = (dot(normed, wqkv[2]) + bqv[1]).astype(BF)
        q[rows] = query
        k[rows] = keys
        v[rows] = values
        mixed = []
        for m in range(block // sub):
            cut = slice(m * sub, (m + 1) * sub)
            index = blk * (block // sub) + m
            bias = jnp.where(same, kbias[index], NEG)
            total = jnp.zeros((sub, local), F32)
            for i in range(heads):
                scores = dot_nt(query[cut] * masks_low[i], keys[cut]) * HEAD_DIM ** (-0.5) + bias
                scores = jnp.exp(scores - jnp.max(scores, -1, keepdims=True))
                probs = (scores * (1.0 / jnp.sum(scores, -1, keepdims=True))).astype(BF)
                p[index, i] = probs
                total = total + dot(probs, values[cut]) * masks[i]
            mixed.append(total.astype(BF))
        mixed = jnp.concatenate(mixed, 0)
        o[rows] = mixed
        part_a[blk] = dot(mixed, wo[...]).astype(BF)
        pl.when(t == 0)(scatter.send_d)
        pl.when(t == 1)(scatter.send_x)
        pl.when(t == 2)(scatter.send_y)
        return carry

    lax.fori_loop(0, 4, attend, 0)
    scatter.second()
    for i in range(3):
        hop1[2 * i].wait_recv()
        hop2[i].start()
    scatter.wait()
    own = pl.ds(pl.multiple_of(at.h * block, block), block)
    resid = x[own].astype(F32) + scatter.total() + bo[...]
    r1[...] = resid
    hat, _ = norm_stats(resid)
    n2[own] = (hat * g2[...] + c2[...]).astype(BF)

    gather = Gather(at, n2, ag_send, ag_recv, block)
    gather.start()
    spread = Scatter(at, part_b, got_b, sb_send, sb_recv, block)

    def feed(t, carry):
        @pl.when(t == 1)
        def _():
            gather.forward()
            gather.wait_x()

        pl.when(t == 2)(gather.wait_y)
        pl.when(t == 3)(gather.wait_d)
        blk = lax.rem(at.hi + lax.div(t, 2), 2) * 2 + lax.rem(at.lo + lax.rem(t, 2), 2)
        rows = pl.ds(pl.multiple_of(blk * block, block), block)
        value, steep = gelu_pair(dot(n2[rows], wu[...]) + bu[...])
        value = value.astype(BF)
        hid[rows] = value
        slope[rows] = steep.astype(BF)
        part_b[blk] = dot(value, wd[...]).astype(BF)
        pl.when(t == 1)(spread.send_x)
        pl.when(t == 2)(spread.send_y)
        pl.when(t == 3)(spread.send_d)
        return carry

    lax.fori_loop(0, 4, feed, 0)
    for i in range(3):
        hop2[i].wait_recv()
        hop3[2 * i].start()
        hop3[2 * i + 1].start()
    own_i.wait()
    for copy in pics:
        copy.wait_recv()
    core_pics.start()
    spread.second()
    spread.wait()
    z[...] = r1[...] + spread.total() + bd[...]
    own_w.wait()
    own_b.wait()
    for i in range(3):
        hop1[2 * i + 1].wait_recv()
    for copy in hop3:
        copy.wait_recv()
    core_pics.wait_recv()
    for copy in hop1 + hop2 + hop3 + pics + [core_pics]:
        copy.wait_send()
    scatter.finish()
    gather.finish()
    spread.finish()


def first_forward(dp, section, x, kbias, image, base, w2, b2):
    g1, c1, wqkv, bqv, wo, bo, g2, c2, wu, bu, wd, bd = base
    tokens, width = x.shape
    local = wo.shape[0]
    ff = wu.shape[1]
    block = tokens // 4
    heads = local // HEAD_DIM
    captions = image.shape[0]
    slots = tokens // captions
    vmem = pl.BlockSpec(memory_space=pltpu.VMEM)
    hbm = pl.BlockSpec(memory_space=pl.ANY)
    shape = jax.ShapeDtypeStruct
    outs = [
        shape((tokens, width), BF),
        shape((tokens, local), BF),
        shape((tokens, local), BF),
        shape((tokens, local), BF),
        shape((tokens // 128, heads, 128, 128), BF),
        shape((tokens, local), BF),
        shape((tokens, width), BF),
        shape((tokens, ff), BF),
        shape((tokens, ff), BF),
        shape((block, width), F32),
        shape((block, width), F32),
        shape((4,) + w2.shape, BF),
        shape((4,) + b2.shape, F32),
        shape((dp, section, captions, width), BF),
    ]
    sems = pltpu.SemaphoreType.DMA
    return pl.pallas_call(
        functools.partial(first_forward_kernel, dp, block, slots),
        out_shape=outs,
        in_specs=[vmem] * 15 + [hbm] * 2,
        out_specs=[vmem] * 11 + [hbm] * 3,
        scratch_shapes=[
            pltpu.VMEM((4, block, width), BF),
            pltpu.VMEM((6, block // 2, width), BF),
            pltpu.VMEM((4, block, width), BF),
            pltpu.VMEM((6, block // 2, width), BF),
            pltpu.VMEM((captions, width), BF),
            sems((6,)),
            sems((6,)),
            sems((6,)),
            sems((6,)),
            sems((6,)),
            sems((6,)),
            sems((12,)),
            sems((12,)),
            sems((3,)),
            sems((3,)),
            sems((dp,)),
            sems((dp,)),
            sems((3,)),
        ],
        compiler_params=pltpu.CompilerParams(
            collective_id=0, has_side_effects=True, vmem_limit_bytes=VMEM_LIMIT
        ),
        cost_estimate=pl.CostEstimate(
            flops=4 * 10**9, bytes_accessed=20 * 10**6, transcendentals=10**6
        ),
    )(x, kbias, image, g1, c1, wqkv, bqv, wo, bo, g2, c2, wu, bu, wd, bd, w2, b2)


def second_kernel(
    dp,
    section,
    slots,
    z,
    kbias,
    pick,
    pcol,
    images,
    w2,
    b2,
    g1,
    c1,
    bo,
    g2,
    c2,
    wu,
    bu,
    wd,
    bd,
    dz,
    loss,
    g_qkv,
    g_wo,
    g_wu,
    g_wd,
    g_vec,
    g_bqv,
    g_bu,
    ring,
    arb,
    stats,
    dpool,
    dn2b,
    rsb,
    f_out,
    f_in,
    s_out,
    s_in,
    a_in,
    send,
    recv,
    st_send,
    st_recv,
):
    at = Place()
    head_peers = [at.hx, at.hy, at.hd]
    others = []
    for j in range(dp):
        for i in range(section):
            if i or j:
                others.append((lax.rem(at.z + j, dp), lax.rem(at.s + i, section), at.h))
    at.greet([at.head(j) for j in head_peers] + others)

    block, width = z.shape
    own_caps = block // slots
    caps = 4 * own_caps
    local = w2.shape[3]
    heads = local // HEAD_DIM
    scale = HEAD_DIM ** (-0.5)
    low_masks = head_masks(local, BF)
    masks = head_masks(local, F32)

    def stack(values):
        return jnp.concatenate([values * low_masks[i] for i in range(heads)], 0)

    def pick_heads(values):
        total = values[:own_caps] * masks[0]
        for i in range(1, heads):
            total = total + values[i * own_caps : (i + 1) * own_caps] * masks[i]
        return total

    zv = z[...]
    hat1, rstd1 = norm_stats(zv)
    normed = (hat1 * g1[...] + c1[...]).astype(BF)
    pooled_low = dot(pick[...], normed).astype(BF)
    a_in[at.h, 0] = pooled_low
    z_pool = jnp.sum((zv * pcol[...]).reshape(own_caps, slots, width), 1)
    us = []
    for j in range(4):
        query = (dot(pooled_low, w2[j, 0]) + b2[j, 0:1]).astype(BF)
        s_out[j, 0] = query
        us.append(dot_nt(stack(query), w2[j, 1]).astype(BF))
    u_all = jnp.concatenate(us, 0)
    rows_n = 4 * heads * own_caps
    row_cap = lax.rem(lax.broadcasted_iota(jnp.int32, (rows_n, block), 0), own_caps)
    col_cap = lax.broadcasted_iota(jnp.int32, (rows_n, block), 1) // slots
    bias = jnp.where(row_cap == col_cap, kbias[...], NEG)
    scores = dot_nt(u_all, normed) * scale + bias
    scores = jnp.exp(scores - jnp.max(scores, -1, keepdims=True))
    probs = scores * (1.0 / jnp.sum(scores, -1, keepdims=True))
    probs_low = probs.astype(BF)
    mix = dot(probs_low, normed).astype(BF)
    attended = jnp.zeros((own_caps, width), F32)
    per = heads * own_caps
    for j in range(4):
        part = mix[j * per : (j + 1) * per]
        f_out[j, 0] = part
        out = (pick_heads(dot(part, w2[j, 2])) + b2[j, 1:2]).astype(BF)
        s_out[j, 3] = out
        attended = attended + dot_nt(out, w2[j, 3])
    r1 = z_pool + attended + bo[...]
    ring[at.h] = r1
    rings = [
        remote(ring.at[at.h], ring.at[at.h], send.at[i], recv.at[i], at.head(j))
        for i, j in enumerate(head_peers)
    ]
    for copy in rings:
        copy.start()
    for copy in rings:
        copy.wait_recv()

    r1_all = ring[...].reshape(caps, width)
    hat2_all, _ = norm_stats(r1_all)
    n2 = (hat2_all * g2[...] + c2[...]).astype(BF)
    value, slope = gelu_pair(dot(n2, wu[...]) + bu[...])
    value = value.astype(BF)
    arb[at.h] = dot(value, wd[...]).astype(BF)
    sums = [
        remote(arb.at[at.h], arb.at[at.h], send.at[3 + i], recv.at[3 + i], at.head(j))
        for i, j in enumerate(head_peers)
    ]
    for copy in sums:
        copy.start()
    for copy in sums:
        copy.wait_recv()
    pooled = r1_all + bd[...]
    for j in range(4):
        pooled = pooled + arb[j].astype(F32)
    unit_r = lax.rsqrt(jnp.mean(pooled * pooled, -1, keepdims=True) + NORM_EPS)
    text = (pooled * unit_r * width ** (-0.5)).astype(BF)

    everyone = dp * section * caps
    images_all = images[...].reshape(everyone, width)
    logits = LOGIT_SCALE * dot_nt(text, images_all)
    place = at.z * section + at.s
    col = lax.broadcasted_iota(jnp.int32, (caps, everyone), 1)
    row = lax.broadcasted_iota(jnp.int32, (caps, everyone), 0) + place * caps
    diag = col == row
    eye = jnp.where(diag, 1.0, 0.0)
    row_max = jnp.max(logits, 1, keepdims=True)
    row_exp = jnp.exp(logits - row_max)
    row_sum = jnp.sum(row_exp, 1, keepdims=True)
    diagonal = jnp.sum(jnp.where(diag, logits, 0.0), 1, keepdims=True)
    row_loss = jnp.sum(row_max + jnp.log(row_sum) - 2.0 * diagonal, 0, keepdims=True)
    col_max = jnp.max(logits, 0, keepdims=True)
    col_sum = jnp.sum(jnp.exp(logits - col_max), 0, keepdims=True)
    stats[place, 0:1] = col_max
    stats[place, 1:2] = col_sum
    stats[place, 2:3] = jnp.broadcast_to(row_loss, (1, everyone))
    tells = [
        remote(stats.at[place], stats.at[place], st_send.at[i], st_recv.at[i], device)
        for i, device in enumerate(others)
    ]
    for copy in tells:
        copy.start()
    row_grad = ((row_exp * (1.0 / row_sum) - eye) * (0.5 / everyone)).astype(BF)
    text_grad = dot(row_grad, images_all)
    for copy in tells:
        copy.wait_recv()
    told = stats[...]
    top = jnp.max(told[:, 0:1], 0)
    total = jnp.sum(told[:, 1:2] * jnp.exp(told[:, 0:1] - top[None]), 0)
    col_lse = top + jnp.log(total)
    whole_loss = jnp.sum(told[:, 2:3, 0:1], 0) + jnp.sum(col_lse, 1, keepdims=True)
    loss[...] = whole_loss * (0.5 / everyone)
    col_grad = ((jnp.exp(logits - col_lse) - eye) * (0.5 / everyone)).astype(BF)
    text_grad = LOGIT_SCALE * (text_grad + dot(col_grad, images_all))
    inner = jnp.mean(pooled * text_grad, -1, keepdims=True)
    d_pool = (unit_r * width ** (-0.5)) * (text_grad - pooled * (unit_r * unit_r * inner))
    dpool[...] = d_pool

    dm = d_pool.astype(BF)
    du = (dot_nt(dm, wd[...]) * slope).astype(BF)
    dn2b[...] = dot_nt(du, wu[...]).astype(BF)
    own_rows = pl.ds(pl.multiple_of(at.h * own_caps, own_caps), own_caps)
    backs = []
    for i, j in enumerate(head_peers):
        rows = pl.ds(pl.multiple_of(j * own_caps, own_caps), own_caps)
        backs.append(
            remote(dn2b.at[rows], rsb.at[at.h], send.at[6 + i], recv.at[6 + i], at.head(j))
        )
    for copy in backs:
        copy.start()
    g_wd[...] = dot_tn(value, dm).astype(BF)
    g_wu[...] = dot_tn(n2, du).astype(BF)
    g_bu[...] = rows_sum(du.astype(F32))
    rsb[at.h] = dn2b[own_rows]
    for copy in backs:
        copy.wait_recv()
    dn2 = rsb[0].astype(F32)
    for j in range(1, 4):
        dn2 = dn2 + rsb[j].astype(F32)
    hat2, rstd2 = norm_stats(ring[at.h])
    dpool_own = dpool[own_rows]
    dr1 = dpool_own + norm_back(dn2, hat2, rstd2, g2[...])
    g_vec[2:3] = rows_sum(dr1)
    g_vec[3:4] = rows_sum(dn2 * hat2)
    g_vec[4:5] = rows_sum(dn2)
    g_vec[5:6] = rows_sum(dpool_own)
    g_vec[6:8] = jnp.zeros((2, width), F32)

    da = dr1.astype(BF)
    a_in[at.h, 1] = da
    ws = []
    for j in range(4):
        d_out = dot(da, w2[j, 3]).astype(BF)
        s_out[j, 2] = d_out
        ws.append(dot_nt(stack(d_out), w2[j, 2]).astype(BF))
    w_all = jnp.concatenate(ws, 0)
    d_probs = dot_nt(w_all, normed)
    d_scores = probs * (d_probs - jnp.sum(probs * d_probs, -1, keepdims=True))
    scores_low = d_scores.astype(BF)
    g_rows = (dot(scores_low, normed) * scale).astype(BF)
    d_pooled_low = jnp.zeros((own_caps, width), F32)
    for j in range(4):
        part = g_rows[j * per : (j + 1) * per]
        f_out[j, 1] = part
        d_query = pick_heads(dot(part, w2[j, 1])).astype(BF)
        s_out[j, 1] = d_query
        d_pooled_low = d_pooled_low + dot_nt(d_query, w2[j, 0])
    facts = []
    for i, j in enumerate(head_peers):
        facts.append(remote(f_out.at[j], f_in.at[at.h], send.at[9 + i], recv.at[9 + i], at.head(j)))
        facts.append(
            remote(s_out.at[j], s_in.at[at.h], send.at[12 + i], recv.at[12 + i], at.head(j))
        )
        facts.append(
            remote(a_in.at[at.h], a_in.at[at.h], send.at[15 + i], recv.at[15 + i], at.head(j))
        )
    for copy in facts:
        copy.start()
    dn = dot_tn(scores_low, u_all) * scale + dot_tn(probs_low, w_all)
    spread = jnp.broadcast_to(
        jnp.stack([d_pooled_low, dr1], 0)[:, :, None, :], (2, own_caps, slots, width)
    ).reshape(2, block, width)
    dn = dn + pcol[...] * spread[0]
    dz[...] = norm_back(dn, hat1, rstd1, g1[...]) + pcol[...] * spread[1]
    g_vec[0:1] = rows_sum(dn * hat1)
    g_vec[1:2] = rows_sum(dn)

    f_in[at.h] = f_out[at.h]
    s_in[at.h] = s_out[at.h]
    for copy in facts:
        copy.wait_recv()
    pooled_all = jnp.concatenate([a_in[j, 0] for j in range(4)], 0)
    da_all = jnp.concatenate([a_in[j, 1] for j in range(4)], 0)
    dq_all = jnp.concatenate([s_in[j, 1] for j in range(4)], 0)
    do_all = jnp.concatenate([s_in[j, 2] for j in range(4)], 0)
    out_all = jnp.concatenate([s_in[j, 3] for j in range(4)], 0)
    g_qkv[0] = dot_tn(pooled_all, dq_all).astype(BF)
    g_qkv[1] = dot_tn(
        jnp.concatenate([f_in[j, 1] for j in range(4)], 0),
        jnp.concatenate([stack(s_in[j, 0]) for j in range(4)], 0),
    ).astype(BF)
    g_qkv[2] = dot_tn(
        jnp.concatenate([f_in[j, 0] for j in range(4)], 0),
        jnp.concatenate([stack(s_in[j, 2]) for j in range(4)], 0),
    ).astype(BF)
    g_wo[...] = dot_tn(out_all, da_all).astype(BF)
    g_bqv[0:1] = rows_sum(dq_all.astype(F32))
    g_bqv[1:2] = rows_sum(do_all.astype(F32))
    for copy in rings + sums + tells + backs + facts:
        copy.wait_send()


def second_layer(dp, section, slots, z, kbias, pick, pcol, images, w2, b2, top):
    g1, c1, bo, g2, c2, wu, bu, wd, bd = top
    block, width = z.shape
    own_caps = block // slots
    caps = 4 * own_caps
    local = w2.shape[3]
    ff = wu.shape[1]
    heads = local // HEAD_DIM
    per = heads * own_caps
    everyone = dp * section * caps
    vmem = pl.BlockSpec(memory_space=pltpu.VMEM)
    shape = jax.ShapeDtypeStruct
    outs = [
        shape((block, width), F32),
        shape((1, 1), F32),
        shape((3, width, local), BF),
        shape((local, width), BF),
        shape((width, ff), BF),
        shape((ff, width), BF),
        shape((8, width), F32),
        shape((2, local), F32),
        shape((1, ff), F32),
    ]
    sems = pltpu.SemaphoreType.DMA
    others = dp * section - 1
    return pl.pallas_call(
        functools.partial(second_kernel, dp, section, slots),
        out_shape=outs,
        in_specs=[vmem] * 16,
        out_specs=[vmem] * len(outs),
        scratch_shapes=[
            pltpu.VMEM((4, own_caps, width), F32),
            pltpu.VMEM((4, caps, width), BF),
            pltpu.VMEM((dp * section, 8, everyone), F32),
            pltpu.VMEM((caps, width), F32),
            pltpu.VMEM((caps, width), BF),
            pltpu.VMEM((4, own_caps, width), BF),
            pltpu.VMEM((4, 2, per, width), BF),
            pltpu.VMEM((4, 2, per, width), BF),
            pltpu.VMEM((4, 4, own_caps, local), BF),
            pltpu.VMEM((4, 4, own_caps, local), BF),
            pltpu.VMEM((4, 2, own_caps, width), BF),
            sems((18,)),
            sems((18,)),
            sems((others,)),
            sems((others,)),
        ],
        compiler_params=pltpu.CompilerParams(
            collective_id=1, has_side_effects=True, vmem_limit_bytes=VMEM_LIMIT
        ),
        cost_estimate=pl.CostEstimate(
            flops=2 * 10**9, bytes_accessed=20 * 10**6, transcendentals=10**6
        ),
    )(z, kbias, pick, pcol, images, w2, b2, g1, c1, bo, g2, c2, wu, bu, wd, bd)


def first_backward_kernel(
    block,
    dz,
    x,
    n1,
    q,
    k,
    v,
    p,
    o,
    n2,
    hid,
    slope,
    r1,
    g1,
    wqkv,
    wo,
    g2,
    wu,
    wd,
    dy,
    g_qkv,
    g_wo,
    g_wu,
    g_wd,
    g_vec,
    g_bqv,
    g_bu,
    dm,
    du,
    da,
    dqkv,
    dr1,
    part_a,
    got_a,
    part_b,
    got_b,
    ga_send,
    ga_recv,
    sa_send,
    sa_recv,
    gb_send,
    gb_recv,
    sb_send,
    sb_recv,
    gc_send,
    gc_recv,
):
    at = Place()
    at.greet([at.head(j) for j in (at.hx, at.hy, at.hd)])
    local = wo.shape[0]
    heads = local // HEAD_DIM
    width = x.shape[1]
    sub = 128
    own = pl.ds(pl.multiple_of(at.h * block, block), block)
    dm[own] = dz[...].astype(BF)
    gather = Gather(at, dm, ga_send, ga_recv, block)
    gather.start()
    scatter = Scatter(at, part_a, got_a, sa_send, sa_recv, block)

    def waits(t, gather):
        @pl.when(t == 1)
        def _():
            gather.forward()
            gather.wait_x()

        pl.when(t == 2)(gather.wait_y)
        pl.when(t == 3)(gather.wait_d)

    def sends(t, scatter):
        pl.when(t == 1)(scatter.send_x)
        pl.when(t == 2)(scatter.send_y)
        pl.when(t == 3)(scatter.send_d)

    def block_of(t):
        return lax.rem(at.hi + lax.div(t, 2), 2) * 2 + lax.rem(at.lo + lax.rem(t, 2), 2)

    def feed(t, carry):
        waits(t, gather)
        blk = block_of(t)
        rows = pl.ds(pl.multiple_of(blk * block, block), block)
        grad = (dot_nt(dm[rows], wd[...]) * slope[rows].astype(F32)).astype(BF)
        du[rows] = grad
        part_a[blk] = dot_nt(grad, wu[...]).astype(BF)
        sends(t, scatter)
        return carry

    lax.fori_loop(0, 4, feed, 0)
    g_wd[...] = dot_tn(hid[...], dm[...]).astype(BF)
    scatter.second()
    g_wu[...] = dot_tn(n2[...], du[...]).astype(BF)
    g_bu[...] = rows_sum(du[...].astype(F32))
    scatter.wait()
    dn2 = scatter.total()
    hat, rstd = norm_stats(r1[...])
    upper = dz[...]
    back = upper + norm_back(dn2, hat, rstd, g2[...])
    dr1[...] = back
    da[own] = back.astype(BF)
    gather_a = Gather(at, da, gb_send, gb_recv, block)
    gather_a.start()
    g_vec[2:3] = rows_sum(back)
    g_vec[3:4] = rows_sum(dn2 * hat)
    g_vec[4:5] = rows_sum(dn2)
    g_vec[5:6] = rows_sum(upper)
    g_vec[6:8] = jnp.zeros((2, width), F32)

    scatter_b = Scatter(at, part_b, got_b, sb_send, sb_recv, block)
    low_masks = head_masks(local, BF)
    masks = head_masks(local, F32)
    scale = HEAD_DIM ** (-0.5)

    def attend(t, carry):
        waits(t, gather_a)
        blk = block_of(t)
        rows = pl.ds(pl.multiple_of(blk * block, block), block)
        d_out = dot_nt(da[rows], wo[...]).astype(BF)
        query, keys, values = q[rows], k[rows], v[rows]
        parts = [[], [], []]
        for m in range(block // sub):
            cut = slice(m * sub, (m + 1) * sub)
            index = blk * (block // sub) + m
            dq = jnp.zeros((sub, local), F32)
            dk = jnp.zeros((sub, local), F32)
            dv = jnp.zeros((sub, local), F32)
            for i in range(heads):
                probs_low = p[index, i]
                probs = probs_low.astype(F32)
                d_probs = dot_nt(d_out[cut] * low_masks[i], values[cut])
                d_scores = probs * (d_probs - jnp.sum(probs * d_probs, -1, keepdims=True))
                d_scores = d_scores.astype(BF)
                dq = dq + dot(d_scores, keys[cut]) * masks[i]
                dk = dk + dot_tn(d_scores, query[cut]) * masks[i]
                dv = dv + dot_tn(probs_low, d_out[cut]) * masks[i]
            parts[0].append((dq * scale).astype(BF))
            parts[1].append((dk * scale).astype(BF))
            parts[2].append(dv.astype(BF))
        total = None
        for i in range(3):
            whole = jnp.concatenate(parts[i], 0)
            dqkv[i, rows] = whole
            term = dot_nt(whole, wqkv[i])
            total = term if total is None else total + term
        part_b[blk] = total.astype(BF)
        sends(t, scatter_b)
        return carry

    lax.fori_loop(0, 4, attend, 0)
    g_wo[...] = dot_tn(o[...], da[...]).astype(BF)
    g_qkv[0] = dot_tn(n1[...], dqkv[0]).astype(BF)
    scatter_b.second()
    g_qkv[1] = dot_tn(n1[...], dqkv[1]).astype(BF)
    g_qkv[2] = dot_tn(n1[...], dqkv[2]).astype(BF)
    g_bqv[0:1] = rows_sum(dqkv[0].astype(F32))
    g_bqv[1:2] = rows_sum(dqkv[2].astype(F32))
    scatter_b.wait()
    dn1 = scatter_b.total()
    hat, rstd = norm_stats(x[own].astype(F32))
    dy[own] = (dr1[...] + norm_back(dn1, hat, rstd, g1[...])).astype(BF)
    gather_y = Gather(at, dy, gc_send, gc_recv, block)
    gather_y.start()
    g_vec[0:1] = rows_sum(dn1 * hat)
    g_vec[1:2] = rows_sum(dn1)
    gather_y.forward()
    gather_y.wait_x()
    gather_y.wait_y()
    gather_y.wait_d()
    for group in (gather, scatter, gather_a, scatter_b, gather_y):
        group.finish()


def first_backward(dz, x, saved, weights):
    tokens, width = x.shape
    block = tokens // 4
    g1, wqkv, wo, g2, wu, wd = weights
    local = wo.shape[0]
    ff = wu.shape[1]
    vmem = pl.BlockSpec(memory_space=pltpu.VMEM)
    shape = jax.ShapeDtypeStruct
    outs = [
        shape((tokens, width), BF),
        shape((3, width, local), BF),
        shape((local, width), BF),
        shape((width, ff), BF),
        shape((ff, width), BF),
        shape((8, width), F32),
        shape((2, local), F32),
        shape((1, ff), F32),
    ]
    sems = pltpu.SemaphoreType.DMA
    return pl.pallas_call(
        functools.partial(first_backward_kernel, block),
        out_shape=outs,
        in_specs=[vmem] * 18,
        out_specs=[vmem] * len(outs),
        scratch_shapes=[
            pltpu.VMEM((tokens, width), BF),
            pltpu.VMEM((tokens, ff), BF),
            pltpu.VMEM((tokens, width), BF),
            pltpu.VMEM((3, tokens, local), BF),
            pltpu.VMEM((block, width), F32),
            pltpu.VMEM((4, block, width), BF),
            pltpu.VMEM((6, block // 2, width), BF),
            pltpu.VMEM((4, block, width), BF),
            pltpu.VMEM((6, block // 2, width), BF),
        ]
        + [sems((6,))] * 10,
        compiler_params=pltpu.CompilerParams(
            collective_id=2, has_side_effects=True, vmem_limit_bytes=VMEM_LIMIT
        ),
        cost_estimate=pl.CostEstimate(
            flops=8 * 10**9, bytes_accessed=30 * 10**6, transcendentals=10**6
        ),
    )(dz, x, *saved, g1, wqkv, wo, g2, wu, wd)


def on_device(dp, section, text_in, lengths, image_embed, *params):
    base, top = params[:12], params[12:]
    captions, slots, width = text_in.shape
    tokens = captions * slots
    block = tokens // 4
    own_caps = captions // 4

    def line(vector):
        return vector.reshape(1, -1)

    def layout(layer):
        g1, c1, wqkv, bqv, wo, bo, g2, c2, wu, bu, wd, bd = layer
        return (
            line(g1),
            line(c1),
            wqkv.transpose(1, 0, 2),
            bqv,
            wo,
            line(bo),
            line(g2),
            line(c2),
            wu,
            line(bu),
            wd,
            line(bd),
        )

    base, top = layout(base), layout(top)
    x = text_in.reshape(tokens, width)
    positions = jnp.arange(slots, dtype=jnp.int32)
    kbias = jnp.where(positions[None, :] < lengths[:, None], 0.0, NEG).astype(F32)
    head = lax.axis_index("head")
    own_lengths = lax.dynamic_slice_in_dim(lengths, head * own_caps, own_caps)
    kbias_own = lax.dynamic_slice_in_dim(kbias, head * own_caps, own_caps).reshape(1, block)
    picker = positions[None, :] == own_lengths[:, None] - 1
    pick = (
        jnp.where(jnp.eye(own_caps, dtype=bool)[:, :, None], picker[None], False)
        .reshape(own_caps, block)
        .astype(BF)
    )
    pcol = picker.reshape(block, 1).astype(F32)

    w2 = jnp.concatenate([top[2], top[4].T[None]], 0)
    outs = first_forward(
        dp,
        section,
        x,
        kbias.reshape(tokens // 128, 1, 128),
        image_embed,
        base[:3] + (base[3].reshape(2, 1, -1),) + base[4:],
        w2,
        top[3],
    )
    n1, q, k, v, p, o, n2, hid, slope, r1, z, w2all, b2all, images = outs
    seconds = second_layer(
        dp,
        section,
        slots,
        z,
        kbias_own,
        pick,
        pcol,
        images,
        w2all,
        b2all,
        (top[0], top[1], top[5], top[6], top[7], top[8], top[9], top[10], top[11]),
    )
    dz, loss = seconds[0], seconds[1]
    firsts = first_backward(
        dz,
        x,
        (n1, q, k, v, p, o, n2, hid, slope, r1),
        (base[0], base[2], base[4], base[6], base[8], base[10]),
    )
    dy = firsts[0]
    axes = ("dp", "section")
    top_big = lax.psum(tuple(seconds[2:6]), axes)
    base_big = lax.psum(tuple(firsts[1:5]), axes)
    vec = lax.psum(jnp.stack([firsts[5], seconds[6]], 0), axes + ("head",))
    small = lax.psum((firsts[6], firsts[7], seconds[7], seconds[8]), axes)

    def grads(big, vec, bqv, bu):
        g_qkv, g_wo, g_wu, g_wd = (item.astype(F32) for item in big)
        return (
            vec[0],
            vec[1],
            g_qkv.transpose(1, 0, 2),
            bqv,
            g_wo,
            vec[2],
            vec[3],
            vec[4],
            g_wu,
            bu.reshape(-1),
            g_wd,
            vec[5],
        )

    return (
        (loss[0, 0], dy.astype(F32).reshape(captions, slots, width))
        + grads(base_big, vec[0], small[0], small[1])
        + grads(top_big, vec[1], small[2], small[3])
    )


def solution(mesh):
    layer_in = (
        P(),
        P(),
        P(None, None, "head"),
        P(None, "head"),
        P("head", None),
        P(),
        P(),
        P(),
        P(None, "head"),
        P("head"),
        P("head", None),
        P(),
    )
    rows = P(("dp", "section"), None, None)
    return jax.shard_map(
        functools.partial(on_device, mesh.shape["dp"], mesh.shape["section"]),
        mesh=mesh,
        in_specs=(rows, P(("dp", "section")), P(("dp", "section"), None)) + layer_in * 2,
        out_specs=(P(), rows) + layer_in * 2,
        check_vma=False,
    )
```

```python
import functools

import jax
import jax.numpy as jnp
from jax import lax
from jax.experimental import pallas as pl
from jax.experimental.pallas import tpu as pltpu
from jax.sharding import PartitionSpec as P

HEAD_DIM = 64
NORM_EPS = 1e-06
LOGIT_SCALE = 50.0
NEG = -1e30
BF = jnp.bfloat16
F32 = jnp.float32
MESH = pl.DeviceIdType.MESH
VMEM_LIMIT = 63 * 2**20


def dot(a, b):
    return lax.dot_general(a, b, (((1,), (0,)), ((), ())), preferred_element_type=F32)


def dot_nt(a, b):
    return lax.dot_general(a, b, (((1,), (1,)), ((), ())), preferred_element_type=F32)


def dot_tn(a, b):
    return lax.dot_general(a, b, (((0,), (0,)), ((), ())), preferred_element_type=F32)


def norm_stats(values):
    center = jnp.mean(values, -1, keepdims=True)
    shifted = values - center
    spread = jnp.mean(shifted * shifted, -1, keepdims=True)
    rstd = lax.rsqrt(spread + NORM_EPS)
    return shifted * rstd, rstd


def norm_back(grad, hat, rstd, gain):
    scaled = grad * gain
    m1 = jnp.mean(scaled, -1, keepdims=True)
    m2 = jnp.mean(scaled * hat, -1, keepdims=True)
    return rstd * (scaled - m1 - hat * m2)


def rows_sum(values):
    return jnp.sum(values, 0, keepdims=True)


def gelu_pair(u):
    c = 0.7978845608028654
    u2 = u * u
    t = jnp.tanh(c * u * (1.0 + 0.044715 * u2))
    half = 0.5 * (1.0 + t)
    value = u * half
    slope = half + 0.5 * u * (1.0 - t * t) * (c * (1.0 + 3.0 * 0.044715 * u2))
    return value, slope


def head_masks(width, kind):
    lane = lax.broadcasted_iota(jnp.int32, (1, width), 1)
    return [
        jnp.where((lane >= i * HEAD_DIM) & (lane < (i + 1) * HEAD_DIM), 1.0, 0.0).astype(kind)
        for i in range(width // HEAD_DIM)
    ]


class Place:
    def __init__(self):
        self.z = lax.axis_index("dp")
        self.s = lax.axis_index("section")
        h = lax.axis_index("head")
        self.h = h
        self.hi = lax.div(h, 2)
        self.lo = lax.rem(h, 2)
        self.hx = self.block(0, 1)
        self.hy = self.block(1, 0)
        self.hd = self.block(1, 1)

    def block(self, flip_hi, flip_lo):
        return lax.rem(self.hi + flip_hi, 2) * 2 + lax.rem(self.lo + flip_lo, 2)

    def head(self, other):
        return (self.z, self.s, other)

    def greet(self, devices):
        barrier = pltpu.get_barrier_semaphore()
        for device in devices:
            pl.semaphore_signal(barrier, inc=1, device_id=device, device_id_type=MESH)
        pl.semaphore_wait(barrier, len(devices))


def remote(src, dst, send_sem, recv_sem, device):
    return pltpu.make_async_remote_copy(
        src_ref=src,
        dst_ref=dst,
        send_sem=send_sem,
        recv_sem=recv_sem,
        device_id=device,
        device_id_type=MESH,
    )


class Gather:
    def __init__(self, at, ref, send, recv, block):
        half = block // 2

        def rows(owner, part):
            return ref.at[pl.ds(pl.multiple_of(owner * block + part * half, half), half)]

        def copy(i, owner, part, target):
            piece = rows(owner, part)
            return remote(piece, piece, send.at[i], recv.at[i], at.head(target))

        self.c = [
            copy(0, at.h, 0, at.hx),
            copy(1, at.h, 1, at.hy),
            copy(2, at.h, 1, at.hx),
            copy(3, at.h, 0, at.hy),
            copy(4, at.hx, 0, at.hy),
            copy(5, at.hy, 1, at.hx),
        ]

    def start(self):
        for i in range(4):
            self.c[i].start()

    def forward(self):
        self.c[0].wait_recv()
        self.c[4].start()
        self.c[1].wait_recv()
        self.c[5].start()

    def wait_x(self):
        self.c[2].wait_recv()

    def wait_y(self):
        self.c[3].wait_recv()

    def wait_d(self):
        self.c[4].wait_recv()
        self.c[5].wait_recv()

    def finish(self):
        for copy in self.c:
            copy.wait_send()


class Scatter:
    def __init__(self, at, part, got, send, recv, block):
        half = block // 2
        self.at, self.part, self.got, self.half = at, part, got, half

        def piece(owner, side):
            return part.at[owner, pl.ds(side * half, half)]

        def copy(i, owner, side, target):
            return remote(piece(owner, side), got.at[i], send.at[i], recv.at[i], at.head(target))

        self.c = [
            copy(0, at.hd, 0, at.hx),
            copy(1, at.hd, 1, at.hy),
            copy(2, at.hx, 0, at.hx),
            copy(3, at.hy, 1, at.hy),
            copy(4, at.hy, 0, at.hy),
            copy(5, at.hx, 1, at.hx),
        ]

    def send_d(self):
        self.c[0].start()
        self.c[1].start()

    def send_x(self):
        self.c[2].start()

    def send_y(self):
        self.c[3].start()

    def second(self):
        half, part, got, at = self.half, self.part, self.got, self.at
        self.c[0].wait_recv()
        part[at.hy, :half] = (part[at.hy, :half].astype(F32) + got[0].astype(F32)).astype(BF)
        self.c[4].start()
        self.c[1].wait_recv()
        part[at.hx, half:] = (part[at.hx, half:].astype(F32) + got[1].astype(F32)).astype(BF)
        self.c[5].start()

    def wait(self):
        for i in (2, 3, 4, 5):
            self.c[i].wait_recv()

    def total(self):
        half, part, got, at = self.half, self.part, self.got, self.at
        top = part[at.h, :half].astype(F32) + got[2].astype(F32) + got[4].astype(F32)
        low = part[at.h, half:].astype(F32) + got[3].astype(F32) + got[5].astype(F32)
        return jnp.concatenate([top, low], 0)

    def finish(self):
        for copy in self.c:
            copy.wait_send()


class Ledger:
    def __init__(self, at, dp, refs, sems):
        self.at = at
        self.pieces = refs
        self.cs, self.cr, self.ns, self.ar, self.br, self.os, self.fs, self.fr, self.free = sems
        left = at.z < dp // 2
        step = jnp.where(left, 1, -1)
        self.inner = (at.z + step, at.s, at.h)
        self.outer = (at.z - step, at.s, at.h)
        self.core = (at.z, 1 - at.s, at.h)
        self.mid = (at.z == dp // 2 - 1) | (at.z == dp // 2)
        self.outermost = (at.z == 0) | (at.z == dp - 1)

    def rows(self, i, side):
        ref, c, a, b = self.pieces[i]
        half = ref.shape[0] // 2
        return ref.at[pl.ds(pl.multiple_of(side * half, half), half)]

    def swap(self, i):
        c = self.pieces[i][1]
        return remote(self.rows(i, 1 - self.at.s), c, self.cs.at[i], self.cr.at[i], self.core)

    def inward(self, i):
        return remote(
            self.rows(i, self.at.s), self.pieces[i][2], self.ns.at[i], self.ar.at[i], self.inner
        )

    def across(self, i):
        return remote(
            self.rows(i, self.at.s), self.pieces[i][3], self.ns.at[i], self.br.at[i], self.inner
        )

    def outward(self, i):
        return remote(
            self.rows(i, self.at.s), self.pieces[i][3], self.os.at[i], self.br.at[i], self.outer
        )

    def last(self, i):
        mine = self.rows(i, self.at.s)
        return remote(mine, mine, self.fs.at[i], self.fr.at[i], self.core)

    def release(self, i):
        self.swap(i).wait_send()
        pl.semaphore_signal(
            self.free.at[i], inc=1, device_id=self.core, device_id_type=MESH
        )

    def finish(self, i):
        pl.semaphore_wait(self.free.at[i], 1)
        self.last(i).start()

    def add(self, i, *refs):
        mine = self.rows(i, self.at.s)
        total = mine[...].astype(F32)
        for ref in refs:
            total = total + ref[...].astype(F32)
        mine[...] = total.astype(mine.dtype)

    def open(self, *which):
        for i in which:
            self.swap(i).start()

    def step(self, ends=(), middles=(), turns=(), backs=()):
        for i in ends:

            @pl.when(self.outermost)
            def _():
                self.swap(i).wait_recv()
                self.add(i, self.pieces[i][1])
                self.release(i)
                pl.when(self.mid)(lambda: self.across(i).start())
                pl.when(jnp.logical_not(self.mid))(lambda: self.inward(i).start())

        for i in middles:

            @pl.when(jnp.logical_not(self.outermost))
            def _():
                self.swap(i).wait_recv()
                self.inward(i).wait_recv()
                self.add(i, self.pieces[i][1], self.pieces[i][2])
                self.release(i)
                pl.when(self.mid)(lambda: self.across(i).start())
                pl.when(jnp.logical_not(self.mid))(lambda: self.inward(i).start())

        for i in turns:

            @pl.when(self.mid)
            def _():
                self.across(i).wait_recv()
                self.across(i).wait_send()
                self.add(i, self.pieces[i][3])
                pl.when(jnp.logical_not(self.outermost))(lambda: self.outward(i).start())
                self.finish(i)

        for i in backs:

            @pl.when(jnp.logical_not(self.mid))
            def _():
                self.outward(i).wait_recv()
                self.inward(i).wait_send()
                mine = self.rows(i, self.at.s)
                mine[...] = self.pieces[i][3][...]
                pl.when(jnp.logical_not(self.outermost))(lambda: self.outward(i).start())
                self.finish(i)

    def close(self):
        for i in range(len(self.pieces)):
            self.last(i).wait_recv()
            self.last(i).wait_send()
            pl.when(jnp.logical_not(self.outermost))(lambda: self.outward(i).wait_send())


def kernel(dp, section, slots, *refs):
    refs = list(refs)

    def take(count):
        out = refs[:count]
        del refs[:count]
        return out

    x, lens, image = take(3)
    g1, c1, wqkv, bqv, wo, bo, g2, c2, wu, bu, wd, bd = take(12)
    tg1, tc1, tqkv, tbqv, two, tbo, tg2, tc2, twu, tbu, twd, tbd = take(12)
    dy, grads, vec = take(3)
    n1, q, k, v, p, o, n2, hid, slope, r1, z = take(11)
    w2, b2, images = take(3)
    part, got = take(2)
    ring, arb, stats, scored, dpool, dn2b, rsb = take(7)
    f_out, f_in, s_out, s_in, a_in = take(5)
    (da,) = take(1)
    dm = dy
    c_in, l_in, b_in, vh_in, vc_in, vl_in, vb_in = take(7)
    ag_sems, rs_sems, w_sems, h_sems, i_sems, st_sems, sm_sems, v_sems = (
        take(2) for _ in range(8)
    )
    ledger_sems = take(9)
    assert not refs

    at = Place()
    tokens, width = x.shape
    block = tokens // 4
    local = wo.shape[0]
    heads = local // HEAD_DIM
    sub = 128
    captions = tokens // slots
    own_caps = block // slots
    caps = captions
    scale = HEAD_DIM ** (-0.5)
    low_masks = head_masks(local, BF)
    masks = head_masks(local, F32)
    other_core = (at.z, 1 - at.s, at.h)
    zs = [(lax.rem(at.z + j, dp), at.s, at.h) for j in range(1, dp)]
    z_pair = (at.z + 1 - 2 * lax.rem(at.z, 2), at.s, at.h)
    head_peers = [at.hx, at.hy, at.hd]
    others = []
    for j in range(dp):
        for i in range(section):
            if i or j:
                others.append((lax.rem(at.z + j, dp), lax.rem(at.s + i, section), at.h))
    own = pl.ds(pl.multiple_of(at.h * block, block), block)

    def vector(ref):
        return ref[...].reshape(1, -1)

    pic = image[...].astype(F32)
    pic = pic * lax.rsqrt(jnp.mean(pic * pic, -1, keepdims=True) + NORM_EPS) * width ** (-0.5)
    images[at.z, at.s] = pic.astype(BF)
    w2[at.h, 0:3] = tqkv[...]
    w2[at.h, 3] = two[...]
    b2[at.h] = tbqv[...]

    at.greet([at.head(j) for j in head_peers] + others)

    quarter = local // 4
    mine = lax.rem(at.z, 2) * 2 + at.s
    pair = (1 - lax.rem(at.z, 2)) * 2 + at.s

    def shard_part(owner, which):
        return w2.at[owner, :, pl.ds(pl.multiple_of(which * quarter, quarter), quarter)]

    def same_place(ref, sems, i, device):
        return remote(ref, ref, sems[0].at[i], sems[1].at[i], device)

    hop1 = [
        same_place(shard_part(at.h, mine), w_sems, i, at.head(j)) for i, j in enumerate(head_peers)
    ]
    hop_b = [same_place(b2.at[at.h], h_sems, i, at.head(j)) for i, j in enumerate(head_peers)]
    hop2 = [
        same_place(shard_part(j, mine), w_sems, 3 + i, z_pair) for i, j in enumerate(head_peers)
    ]
    hop3 = [
        same_place(shard_part(j, which), w_sems, 6 + 3 * n + i, other_core)
        for i, j in enumerate(head_peers)
        for n, which in enumerate((mine, pair))
    ]
    pics = [
        same_place(images.at[at.z, at.s], i_sems, i, device) for i, device in enumerate(zs)
    ]
    core_pics = same_place(images.at[:, at.s], i_sems, dp - 1, other_core)
    for copy in hop1 + hop_b + pics:
        copy.start()

    scatters = [
        Scatter(at, part, got, rs_sems[0].at[i], rs_sems[1].at[i], block) for i in range(4)
    ]
    gathers = [
        Gather(at, ref, ag_sems[0].at[i], ag_sems[1].at[i], block)
        for i, ref in enumerate((n2, dm, da, dy))
    ]

    def block_of(t):
        return lax.rem(at.hi + lax.div(t, 2), 2) * 2 + lax.rem(at.lo + lax.rem(t, 2), 2)

    def limits(first, count):
        cap = lax.broadcasted_iota(jnp.int32, (captions, count), 0)
        slot = lax.broadcasted_iota(jnp.int32, (captions, count), 1)
        chosen = jnp.where(cap == first + slot // slots, 1.0, 0.0).astype(BF)
        row = jnp.broadcast_to(vector(lens).astype(F32), (8, captions)).astype(BF)
        return dot(row, chosen)[:1]

    def key_bias(first, count):
        slot = lax.broadcasted_iota(jnp.int32, (1, count), 1)
        inside = lax.rem(slot, slots).astype(F32) < limits(first, count)
        return jnp.where(inside, 0.0, NEG)

    row_id = lax.broadcasted_iota(jnp.int32, (sub, sub), 0) // slots
    col_id = lax.broadcasted_iota(jnp.int32, (sub, sub), 1) // slots
    same = row_id == col_id
    scatter = scatters[0]

    def attend(t, carry):
        blk = block_of(3 - t)
        rows = pl.ds(pl.multiple_of(blk * block, block), block)
        hat, _ = norm_stats(x[rows].astype(F32))
        normed = (hat * vector(g1) + vector(c1)).astype(BF)
        n1[rows] = normed
        query = (dot_nt(normed, wqkv[0]) + bqv[0:1]).astype(BF)
        keys = dot_nt(normed, wqkv[1]).astype(BF)
        values = (dot_nt(normed, wqkv[2]) + bqv[1:2]).astype(BF)
        q[rows] = query
        k[rows] = keys
        v[rows] = values
        mixed = []
        for m in range(block // sub):
            cut = slice(m * sub, (m + 1) * sub)
            index = blk * (block // sub) + m
            bias = jnp.where(same, key_bias(index * (sub // slots), sub), NEG)
            total = jnp.zeros((sub, local), F32)
            for i in range(heads):
                scores = dot_nt(query[cut] * low_masks[i], keys[cut]) * scale + bias
                scores = jnp.exp(scores - jnp.max(scores, -1, keepdims=True))
                probs = (scores * (1.0 / jnp.sum(scores, -1, keepdims=True))).astype(BF)
                p[index, i] = probs
                total = total + dot(probs, values[cut]) * masks[i]
            mixed.append(total.astype(BF))
        mixed = jnp.concatenate(mixed, 0)
        o[rows] = mixed
        part[blk] = dot(mixed, wo[...]).astype(BF)
        pl.when(t == 0)(scatter.send_d)
        pl.when(t == 1)(scatter.send_y)
        pl.when(t == 2)(scatter.send_x)
        return carry

    lax.fori_loop(0, 4, attend, 0)
    scatter.second()
    for i in range(3):
        hop1[i].wait_recv()
        hop2[i].start()
    scatter.wait()
    resid = x[own].astype(F32) + scatter.total() + vector(bo)
    scatter.finish()
    r1[...] = resid
    hat, _ = norm_stats(resid)
    n2[own] = (hat * vector(g2) + vector(c2)).astype(BF)

    def waits(t, gather):
        @pl.when(t == 1)
        def _():
            gather.forward()
            gather.wait_x()

        pl.when(t == 2)(gather.wait_y)
        pl.when(t == 3)(gather.wait_d)

    def sends(t, scatter):
        pl.when(t == 1)(scatter.send_x)
        pl.when(t == 2)(scatter.send_y)
        pl.when(t == 3)(scatter.send_d)

    gathers[0].start()

    def feed(t, carry):
        waits(t, gathers[0])
        blk = block_of(t)
        rows = pl.ds(pl.multiple_of(blk * block, block), block)
        value, steep = gelu_pair(dot(n2[rows], wu[...]) + vector(bu))
        value = value.astype(BF)
        hid[rows] = value
        slope[rows] = steep.astype(BF)
        part[blk] = dot(value, wd[...]).astype(BF)
        sends(t, scatters[1])
        return carry

    lax.fori_loop(0, 4, feed, 0)
    for i in range(3):
        hop2[i].wait_recv()
        hop3[2 * i].start()
        hop3[2 * i + 1].start()
    for copy in pics:
        copy.wait_recv()
    core_pics.start()
    scatters[1].second()
    scatters[1].wait()
    zv = r1[...] + scatters[1].total() + vector(bd)
    scatters[1].finish()
    z[...] = zv
    for copy in hop_b + hop3 + [core_pics]:
        copy.wait_recv()

    per = heads * own_caps

    def stack(values):
        return jnp.concatenate([values * low_masks[i] for i in range(heads)], 0)

    def pick_heads(values):
        total = values[:own_caps] * masks[0]
        for i in range(1, heads):
            total = total + values[i * own_caps : (i + 1) * own_caps] * masks[i]
        return total

    first_cap = at.h * own_caps
    last_slot = limits(first_cap, block) - 1.0
    slot_row = lax.broadcasted_iota(jnp.int32, (own_caps, block), 1)
    cap_row = lax.broadcasted_iota(jnp.int32, (own_caps, block), 0)
    picked = (slot_row // slots == cap_row) & (lax.rem(slot_row, slots).astype(F32) == last_slot)
    pick = jnp.where(picked, 1.0, 0.0).astype(BF)
    cap_of = lax.broadcasted_iota(jnp.int32, (block, captions), 0)
    cap_at = lax.broadcasted_iota(jnp.int32, (block, captions), 1)
    length_col = jnp.sum(
        jnp.where(cap_at == first_cap + cap_of // slots, vector(lens).astype(F32), 0.0),
        1,
        keepdims=True,
    )
    slot_col = lax.rem(lax.broadcasted_iota(jnp.int32, (block, 1), 0), slots).astype(F32)
    pcol = jnp.where(slot_col == length_col - 1.0, 1.0, 0.0)

    hat1, rstd1 = norm_stats(zv)
    normed = (hat1 * vector(tg1) + vector(tc1)).astype(BF)
    pooled_low = dot(pick, normed).astype(BF)
    a_in[at.h, 0] = pooled_low
    z_pool = jnp.sum((zv * pcol).reshape(own_caps, slots, width), 1)
    us = []
    for j in range(4):
        query = (dot_nt(pooled_low, w2[j, 0]) + b2[j, 0:1]).astype(BF)
        s_out[j, 0] = query
        us.append(dot(stack(query), w2[j, 1]).astype(BF))
    u_all = jnp.concatenate(us, 0)
    rows_n = 4 * per
    row_cap = lax.rem(lax.broadcasted_iota(jnp.int32, (rows_n, block), 0), own_caps)
    col_cap = lax.broadcasted_iota(jnp.int32, (rows_n, block), 1) // slots
    bias = jnp.where(row_cap == col_cap, key_bias(first_cap, block), NEG)
    scores = dot_nt(u_all, normed) * scale + bias
    scores = jnp.exp(scores - jnp.max(scores, -1, keepdims=True))
    probs = scores * (1.0 / jnp.sum(scores, -1, keepdims=True))
    probs_low = probs.astype(BF)
    mix = dot(probs_low, normed).astype(BF)
    attended = jnp.zeros((own_caps, width), F32)
    for j in range(4):
        piece = mix[j * per : (j + 1) * per]
        f_out[j, 0] = piece
        out = (pick_heads(dot_nt(piece, w2[j, 2])) + b2[j, 1:2]).astype(BF)
        s_out[j, 3] = out
        attended = attended + dot(out, w2[j, 3])
    ring[at.h] = z_pool + attended + vector(tbo)

    def small(ref, i, j, target=None):
        return remote(
            ref,
            ref if target is None else target,
            sm_sems[0].at[i],
            sm_sems[1].at[i],
            at.head(j),
        )

    rings = [small(ring.at[at.h], i, j) for i, j in enumerate(head_peers)]
    for copy in rings:
        copy.start()
    for copy in rings:
        copy.wait_recv()

    r1_all = ring[...].reshape(caps, width)
    hat2_all, _ = norm_stats(r1_all)
    n2_top = (hat2_all * vector(tg2) + vector(tc2)).astype(BF)
    value, steep = gelu_pair(dot(n2_top, twu[...]) + vector(tbu))
    value = value.astype(BF)
    arb[at.h] = dot(value, twd[...]).astype(BF)
    sums = [small(arb.at[at.h], 3 + i, j) for i, j in enumerate(head_peers)]
    for copy in sums:
        copy.start()
    for copy in sums:
        copy.wait_recv()
    pooled = r1_all + vector(tbd)
    for j in range(4):
        pooled = pooled + arb[j].astype(F32)
    unit_r = lax.rsqrt(jnp.mean(pooled * pooled, -1, keepdims=True) + NORM_EPS)
    text = (pooled * unit_r * width ** (-0.5)).astype(BF)

    everyone = dp * section * caps
    batch = min(dp, 4)
    wide = batch * section * caps
    lanes = wide // 4
    place = at.z * section + at.s

    def chunk_images(n):
        return images[n * batch : (n + 1) * batch].reshape(wide, width)

    def own_columns(n):
        col = lax.broadcasted_iota(jnp.int32, (caps, wide), 1) + n * wide
        row = lax.broadcasted_iota(jnp.int32, (caps, wide), 0) + place * caps
        return col == row

    chunks = [slice(n * wide, (n + 1) * wide) for n in range(dp // batch)]
    row_max = diagonal = None
    for n, cols in enumerate(chunks):
        logits = LOGIT_SCALE * dot_nt(text, chunk_images(n))
        scored[:, cols] = logits
        found = jnp.max(logits, 1, keepdims=True)
        row_max = found if row_max is None else jnp.maximum(row_max, found)
        found = jnp.sum(jnp.where(own_columns(n), logits, 0.0), 1, keepdims=True)
        diagonal = found if diagonal is None else diagonal + found
        col_max = jnp.max(logits, 0, keepdims=True)
        col_sum = jnp.sum(jnp.exp(logits - col_max), 0, keepdims=True)
        for i in range(4):
            stats[place, n, i : i + 1] = col_max[:, i * lanes : (i + 1) * lanes]
            stats[place, n, 4 + i : 5 + i] = col_sum[:, i * lanes : (i + 1) * lanes]
    tells = [
        same_place(stats.at[place], st_sems, i, device) for i, device in enumerate(others)
    ]
    for copy in tells:
        copy.start()
    row_sum = None
    for n, cols in enumerate(chunks):
        found = jnp.sum(jnp.exp(scored[:, cols] - row_max), 1, keepdims=True)
        row_sum = found if row_sum is None else row_sum + found
    row_lse = row_max + jnp.log(row_sum)

    def pull(n, cols, lse):
        steep = jnp.exp(scored[:, cols] - lse) - jnp.where(own_columns(n), 1.0, 0.0)
        return dot((steep * (0.5 / everyone)).astype(BF), chunk_images(n))

    text_grad = None
    for n, cols in enumerate(chunks):
        term = pull(n, cols, row_lse)
        text_grad = term if text_grad is None else text_grad + term
    lost = jnp.sum(row_lse - 2.0 * diagonal, 0, keepdims=True)
    for copy in tells:
        copy.wait_recv()
    for n, cols in enumerate(chunks):
        told = stats[:, n]
        top = jnp.max(told[:, 0:4], 0)
        total = jnp.sum(told[:, 4:8] * jnp.exp(told[:, 0:4] - top[None]), 0)
        lse = top + jnp.log(total)
        col_lse = jnp.concatenate([lse[i : i + 1] for i in range(4)], 1)
        text_grad = text_grad + pull(n, cols, col_lse)
        found = jnp.sum(jnp.where(own_columns(n), col_lse, 0.0), 1, keepdims=True)
        lost = lost + jnp.sum(found, 0, keepdims=True)
    text_grad = LOGIT_SCALE * text_grad
    inner = jnp.mean(pooled * text_grad, -1, keepdims=True)
    d_pool = (unit_r * width ** (-0.5)) * (text_grad - pooled * (unit_r * unit_r * inner))
    dpool[...] = d_pool

    per_array = 2
    span = width // per_array
    pieces = []
    for a in range(6):
        for n in range(per_array):
            i = a * per_array + n
            pieces.append(
                (grads.at[a, pl.ds(n * span, span)], c_in.at[i], l_in.at[i], b_in.at[i])
            )
    pieces.append((vec, vc_in, vl_in, vb_in))
    ledger = Ledger(at, dp, pieces, ledger_sems)

    low = d_pool.astype(BF)
    du_top = (dot_nt(low, twd[...]) * steep).astype(BF)
    dn2b[...] = dot_nt(du_top, twu[...]).astype(BF)
    own_rows = pl.ds(pl.multiple_of(at.h * own_caps, own_caps), own_caps)
    backs = []
    for i, j in enumerate(head_peers):
        there = pl.ds(pl.multiple_of(j * own_caps, own_caps), own_caps)
        backs.append(small(dn2b.at[there], 6 + i, j, rsb.at[at.h]))
    for copy in backs:
        copy.start()
    grads[0] = dot_tn(value, low).astype(BF)
    ledger.open(0, 1)
    grads[1] = dot_tn(n2_top, du_top).astype(BF)
    ledger.open(2, 3)
    vec[...] = jnp.zeros_like(vec)
    vec[22:23, 0:128] = jnp.broadcast_to(lost, (1, 128))
    vec[17:18] = rows_sum(du_top.astype(F32))
    rsb[at.h] = dn2b[own_rows]
    ledger.step(ends=(0,))
    for copy in backs:
        copy.wait_recv()
    dn2 = rsb[0].astype(F32)
    for j in range(1, 4):
        dn2 = dn2 + rsb[j].astype(F32)
    hat2, rstd2 = norm_stats(ring[at.h])
    dpool_own = dpool[own_rows]
    dr1_top = dpool_own + norm_back(dn2, hat2, rstd2, vector(tg2))
    vec[8:9] = rows_sum(dr1_top)
    vec[9:10] = rows_sum(dn2 * hat2)
    vec[10:11] = rows_sum(dn2)
    vec[11:12] = rows_sum(dpool_own)

    da_top = dr1_top.astype(BF)
    a_in[at.h, 1] = da_top
    ws = []
    for j in range(4):
        d_out = dot_nt(da_top, w2[j, 3]).astype(BF)
        s_out[j, 2] = d_out
        ws.append(dot(stack(d_out), w2[j, 2]).astype(BF))
    w_all = jnp.concatenate(ws, 0)
    d_probs = dot_nt(w_all, normed)
    d_scores = probs * (d_probs - jnp.sum(probs * d_probs, -1, keepdims=True))
    scores_low = d_scores.astype(BF)
    g_rows = (dot(scores_low, normed) * scale).astype(BF)
    ledger.step(ends=(1,), middles=(0,))
    d_pooled_low = jnp.zeros((own_caps, width), F32)
    for j in range(4):
        piece = g_rows[j * per : (j + 1) * per]
        f_out[j, 1] = piece
        d_query = pick_heads(dot_nt(piece, w2[j, 1])).astype(BF)
        s_out[j, 1] = d_query
        d_pooled_low = d_pooled_low + dot(d_query, w2[j, 0])
    facts = []
    for i, j in enumerate(head_peers):
        facts.append(small(f_out.at[j], 9 + i, j, f_in.at[at.h]))
        facts.append(small(s_out.at[j], 12 + i, j, s_in.at[at.h]))
        facts.append(small(a_in.at[at.h], 15 + i, j))
    dn = dot_tn(scores_low, u_all) * scale + dot_tn(probs_low, w_all)

    def widen(values):
        values = jnp.broadcast_to(values[:, None, :], (own_caps, slots, width))
        return values.reshape(block, width)

    dn = dn + pcol * widen(d_pooled_low)
    dz = norm_back(dn, hat1, rstd1, vector(tg1)) + pcol * widen(dr1_top)
    dm[own] = dz.astype(BF)
    gathers[1].start()
    for copy in facts:
        copy.start()
    z[...] = dz
    vec[6:7] = rows_sum(dn * hat1)
    vec[7:8] = rows_sum(dn)
    vec[5:6] = rows_sum(dz)

    f_in[at.h] = f_out[at.h]
    s_in[at.h] = s_out[at.h]
    ledger.step(ends=(2,), middles=(1,), turns=(0,))
    scatter_a = scatters[2]

    def feed_back(t, carry):
        waits(t, gathers[1])
        blk = block_of(t)
        rows = pl.ds(pl.multiple_of(blk * block, block), block)
        grad = (dot_nt(dm[rows], wd[...]) * slope[rows].astype(F32)).astype(BF)
        slope[rows] = grad
        part[blk] = dot_nt(grad, wu[...]).astype(BF)
        sends(t, scatter_a)
        pl.when(t == 0)(lambda: ledger.step(ends=(3,), middles=(2,), turns=(1,), backs=(0,)))
        return carry

    lax.fori_loop(0, 4, feed_back, 0)
    gathers[1].finish()
    for copy in facts:
        copy.wait_recv()
    pooled_all = jnp.concatenate([a_in[j, 0] for j in range(4)], 0)
    da_all = jnp.concatenate([a_in[j, 1] for j in range(4)], 0)
    dq_all = jnp.concatenate([s_in[j, 1] for j in range(4)], 0)
    do_all = jnp.concatenate([s_in[j, 2] for j in range(4)], 0)
    out_all = jnp.concatenate([s_in[j, 3] for j in range(4)], 0)
    grads[2, 0:local] = dot_tn(dq_all, pooled_all).astype(BF)
    grads[2, local : 2 * local] = dot_tn(
        jnp.concatenate([stack(s_in[j, 0]) for j in range(4)], 0),
        jnp.concatenate([f_in[j, 1] for j in range(4)], 0),
    ).astype(BF)
    grads[2, 2 * local : 3 * local] = dot_tn(
        jnp.concatenate([stack(s_in[j, 2]) for j in range(4)], 0),
        jnp.concatenate([f_in[j, 0] for j in range(4)], 0),
    ).astype(BF)
    grads[2, 3 * local :] = dot_tn(out_all, da_all).astype(BF)
    ledger.open(4, 5)
    vec[20:21, 0:local] = rows_sum(dq_all.astype(F32))
    vec[21:22, 0:local] = rows_sum(do_all.astype(F32))
    ledger.step(middles=(3,), turns=(2,), backs=(1,))
    scatter_a.second()
    grads[3] = dot_tn(hid[...], dm[...]).astype(BF)
    ledger.open(6, 7)
    ledger.step(ends=(4, 5), turns=(3,), backs=(2,))
    grads[4] = dot_tn(n2[...], slope[...]).astype(BF)
    ledger.open(8, 9)
    vec[16:17] = rows_sum(slope[...].astype(F32))
    ledger.step(ends=(6,), middles=(4,), backs=(3,))
    scatter_a.wait()
    dn2 = scatter_a.total()
    scatter_a.finish()
    hat, rstd = norm_stats(r1[...])
    back = z[...] + norm_back(dn2, hat, rstd, vector(g2))
    r1[...] = back
    da[own] = back.astype(BF)
    gathers[2].start()
    vec[2:3] = rows_sum(back)
    vec[3:4] = rows_sum(dn2 * hat)
    vec[4:5] = rows_sum(dn2)

    ledger.step(ends=(7,), middles=(5,), turns=(4,))
    scatter_b = scatters[3]

    def attend_back(t, carry):
        waits(t, gathers[2])
        blk = block_of(t)
        rows = pl.ds(pl.multiple_of(blk * block, block), block)
        d_out = dot_nt(da[rows], wo[...]).astype(BF)
        query, keys, values = q[rows], k[rows], v[rows]
        parts = [[], [], []]
        for m in range(block // sub):
            cut = slice(m * sub, (m + 1) * sub)
            index = blk * (block // sub) + m
            dq = jnp.zeros((sub, local), F32)
            dk = jnp.zeros((sub, local), F32)
            dv = jnp.zeros((sub, local), F32)
            for i in range(heads):
                probs_low = p[index, i]
                probs = probs_low.astype(F32)
                d_probs = dot_nt(d_out[cut] * low_masks[i], values[cut])
                d_scores = probs * (d_probs - jnp.sum(probs * d_probs, -1, keepdims=True))
                d_scores = d_scores.astype(BF)
                dq = dq + dot(d_scores, keys[cut]) * masks[i]
                dk = dk + dot_tn(d_scores, query[cut]) * masks[i]
                dv = dv + dot_tn(probs_low, d_out[cut]) * masks[i]
            parts[0].append((dq * scale).astype(BF))
            parts[1].append((dk * scale).astype(BF))
            parts[2].append(dv.astype(BF))
        total = None
        for i in range(3):
            whole = jnp.concatenate(parts[i], 0)
            (q, k, v)[i][rows] = whole
            term = dot(whole, wqkv[i])
            total = term if total is None else total + term
        part[blk] = total.astype(BF)
        sends(t, scatter_b)
        pl.when(t == 0)(lambda: ledger.step(ends=(8,), middles=(6,), turns=(5,), backs=(4,)))
        pl.when(t == 2)(lambda: ledger.step(ends=(9,), middles=(7,), turns=(6,), backs=(5,)))
        return carry

    lax.fori_loop(0, 4, attend_back, 0)
    for i in range(2):
        grads[5, i * local : (i + 1) * local] = dot_tn((q, k)[i][...], n1[...]).astype(BF)
    ledger.open(10)
    ledger.step(middles=(8,), turns=(7,), backs=(6,))
    scatter_b.second()
    grads[5, 2 * local : 3 * local] = dot_tn(v[...], n1[...]).astype(BF)
    grads[5, 3 * local :] = dot_tn(o[...], da[...]).astype(BF)
    ledger.open(11)
    vec[18:19, 0:local] = rows_sum(q[...].astype(F32))
    vec[19:20, 0:local] = rows_sum(v[...].astype(F32))
    ledger.step(ends=(10, 11), middles=(9,), turns=(8,), backs=(7,))
    scatter_b.wait()
    dn1 = scatter_b.total()
    hat, rstd = norm_stats(x[own].astype(F32))
    dy[own] = (r1[...] + norm_back(dn1, hat, rstd, vector(g1))).astype(BF)
    gathers[3].start()
    vec[0:1] = rows_sum(dn1 * hat)
    vec[1:2] = rows_sum(dn1)

    vh_in[at.h] = vec[0:16]
    tops = [
        same_place(vh_in.at[at.h], v_sems, i, at.head(j)) for i, j in enumerate(head_peers)
    ]
    for copy in tops:
        copy.start()
    ledger.step(middles=(10,), turns=(9,), backs=(8,))
    for copy in tops:
        copy.wait_recv()
    vec[0:16] = vh_in[0] + vh_in[1] + vh_in[2] + vh_in[3]
    ledger.open(12)
    gathers[3].forward()
    ledger.step(ends=(12,), middles=(11, 12), turns=(10,), backs=(9,))
    gathers[3].wait_x()
    gathers[3].wait_y()
    ledger.step(turns=(11, 12), backs=(10,))
    gathers[3].wait_d()
    ledger.step(backs=(11, 12))
    ledger.close()
    scatter_b.finish()
    for i in (0, 2, 3):
        gathers[i].finish()
    for copy in hop1 + hop_b + hop2 + hop3 + pics + [core_pics]:
        copy.wait_send()
    for copy in rings + sums + tells + backs + facts + tops:
        copy.wait_send()


def run_kernel(dp, section, slots, x, lens, image, base, top):
    tokens, width = x.shape
    local = base[4].shape[0]
    ff = base[8].shape[1]
    block = tokens // 4
    heads = local // HEAD_DIM
    captions = image.shape[0]
    own_caps = captions // 4
    per = heads * own_caps
    everyone = dp * section * captions
    batch = min(dp, 4)
    others = dp * section - 1
    vmem = pl.BlockSpec(memory_space=pltpu.VMEM)
    shape = jax.ShapeDtypeStruct
    outs = [
        shape((tokens, width), BF),
        shape((6, width, width), BF),
        shape((32, width), F32),
    ]
    assert ff == width and 4 * local == width
    sems = pltpu.SemaphoreType.DMA
    ram = pltpu.VMEM
    half_piece = width // 4
    scratch = [
        ram((tokens, width), BF),
        ram((tokens, local), BF),
        ram((tokens, local), BF),
        ram((tokens, local), BF),
        ram((tokens // 128, heads, 128, 128), BF),
        ram((tokens, local), BF),
        ram((tokens, width), BF),
        ram((tokens, ff), BF),
        ram((tokens, ff), BF),
        ram((block, width), F32),
        ram((block, width), F32),
        ram((4, 4, local, width), BF),
        ram((4, 2, local), F32),
        ram((dp, section, captions, width), BF),
        ram((4, block, width), BF),
        ram((6, block // 2, width), BF),
        ram((4, own_caps, width), F32),
        ram((4, captions, width), BF),
        ram((dp * section, dp // batch, 8, everyone // (dp // batch) // 4), F32),
        ram((captions, everyone), F32),
        ram((captions, width), F32),
        ram((captions, width), BF),
        ram((4, own_caps, width), BF),
        ram((4, 2, per, width), BF),
        ram((4, 2, per, width), BF),
        ram((4, 4, own_caps, local), BF),
        ram((4, 4, own_caps, local), BF),
        ram((4, 2, own_caps, width), BF),
        ram((tokens, width), BF),
        ram((12, half_piece, width), BF),
        ram((12, half_piece, width), BF),
        ram((12, half_piece, width), BF),
        ram((4, 16, width), F32),
        ram((16, width), F32),
        ram((16, width), F32),
        ram((16, width), F32),
    ]
    for count in ((4, 6), (4, 6), (12,), (3,), (dp,), (others,), (18,), (3,)):
        scratch += [sems(count), sems(count)]
    scratch += [sems((13,))] * 8 + [pltpu.SemaphoreType.REGULAR((13,))]
    return pl.pallas_call(
        functools.partial(kernel, dp, section, slots),
        out_shape=outs,
        in_specs=[vmem] * 27,
        out_specs=[vmem] * 3,
        scratch_shapes=scratch,
        compiler_params=pltpu.CompilerParams(
            collective_id=0, has_side_effects=True, vmem_limit_bytes=VMEM_LIMIT
        ),
        cost_estimate=pl.CostEstimate(
            flops=14 * 10**9, bytes_accessed=40 * 10**6, transcendentals=4 * 10**6
        ),
    )(x, lens, image, *base, *top)


def on_device(dp, section, text_in, lengths, image_embed, *params):
    base, top = params[:12], params[12:]
    captions, slots, width = text_in.shape
    tokens = captions * slots
    local = base[4].shape[0]

    def layout(layer):
        return layer[:2] + (layer[2].transpose(1, 2, 0),) + layer[3:]

    dy, grads, vec = run_kernel(
        dp,
        section,
        slots,
        text_in.reshape(tokens, width),
        lengths,
        image_embed,
        layout(base),
        layout(top),
    )

    def unpack(start, rows, bu, bqv):
        down, up, attention = (grads[start + i] for i in range(3))
        return (
            vec[rows],
            vec[rows + 1],
            attention[: 3 * local].reshape(3, local, width).transpose(2, 0, 1).astype(F32),
            vec[bqv : bqv + 2, :local],
            attention[3 * local :].astype(F32),
            vec[rows + 2],
            vec[rows + 3],
            vec[rows + 4],
            up.astype(F32),
            vec[bu],
            down.astype(F32),
            vec[rows + 5],
        )

    loss = vec[22, 0] * (0.5 / (dp * section * captions))
    return (
        (loss, dy.astype(F32).reshape(captions, slots, width))
        + unpack(3, 0, 16, 18)
        + unpack(0, 6, 17, 20)
    )


def solution(mesh):
    layer_in = (
        P(),
        P(),
        P(None, None, "head"),
        P(None, "head"),
        P("head", None),
        P(),
        P(),
        P(),
        P(None, "head"),
        P("head"),
        P("head", None),
        P(),
    )
    rows = P(("dp", "section"), None, None)
    return jax.shard_map(
        functools.partial(on_device, mesh.shape["dp"], mesh.shape["section"]),
        mesh=mesh,
        in_specs=(rows, P(("dp", "section")), P(("dp", "section"), None)) + layer_in * 2,
        out_specs=(P(), rows) + layer_in * 2,
        check_vma=False,
    )
```

```python
import functools

import jax
import jax.numpy as jnp
from jax import lax
from jax.experimental import pallas as pl
from jax.experimental.pallas import tpu as pltpu
from jax.sharding import PartitionSpec as P

HEAD_DIM = 64
NORM_EPS = 1e-06
LOGIT_SCALE = 50.0
NEG = -1e30
BF = jnp.bfloat16
F32 = jnp.float32
MESH = pl.DeviceIdType.MESH
VMEM_LIMIT = 63 * 2**20


def dot(a, b):
    return lax.dot_general(a, b, (((1,), (0,)), ((), ())), preferred_element_type=F32)


def dot_nt(a, b):
    return lax.dot_general(a, b, (((1,), (1,)), ((), ())), preferred_element_type=F32)


def dot_tn(a, b):
    return lax.dot_general(a, b, (((0,), (0,)), ((), ())), preferred_element_type=F32)


def norm_stats(values):
    center = jnp.mean(values, -1, keepdims=True)
    shifted = values - center
    spread = jnp.mean(shifted * shifted, -1, keepdims=True)
    rstd = lax.rsqrt(spread + NORM_EPS)
    return shifted * rstd, rstd


def norm_back(grad, hat, rstd, gain):
    scaled = grad * gain
    m1 = jnp.mean(scaled, -1, keepdims=True)
    m2 = jnp.mean(scaled * hat, -1, keepdims=True)
    return rstd * (scaled - m1 - hat * m2)


def rows_sum(values):
    return jnp.sum(values, 0, keepdims=True)


def gelu_pair(u):
    c = 0.7978845608028654
    u2 = u * u
    t = jnp.tanh(c * u * (1.0 + 0.044715 * u2))
    half = 0.5 * (1.0 + t)
    value = u * half
    slope = half + 0.5 * u * (1.0 - t * t) * (c * (1.0 + 3.0 * 0.044715 * u2))
    return value, slope


def head_masks(width, kind):
    lane = lax.broadcasted_iota(jnp.int32, (1, width), 1)
    return [
        jnp.where((lane >= i * HEAD_DIM) & (lane < (i + 1) * HEAD_DIM), 1.0, 0.0).astype(kind)
        for i in range(width // HEAD_DIM)
    ]


class Place:
    def __init__(self):
        self.z = lax.axis_index("dp")
        self.s = lax.axis_index("section")
        h = lax.axis_index("head")
        self.h = h
        self.hi = lax.div(h, 2)
        self.lo = lax.rem(h, 2)
        self.hx = self.block(0, 1)
        self.hy = self.block(1, 0)
        self.hd = self.block(1, 1)

    def block(self, flip_hi, flip_lo):
        return lax.rem(self.hi + flip_hi, 2) * 2 + lax.rem(self.lo + flip_lo, 2)

    def head(self, other):
        return (self.z, self.s, other)

    def greet(self, devices):
        barrier = pltpu.get_barrier_semaphore()
        for device in devices:
            pl.semaphore_signal(barrier, inc=1, device_id=device, device_id_type=MESH)
        return lambda: pl.semaphore_wait(barrier, len(devices))


def remote(src, dst, send_sem, recv_sem, device):
    return pltpu.make_async_remote_copy(
        src_ref=src,
        dst_ref=dst,
        send_sem=send_sem,
        recv_sem=recv_sem,
        device_id=device,
        device_id_type=MESH,
    )


class Gather:
    def __init__(self, at, ref, send, recv, block):
        half = block // 2

        def rows(owner, part):
            return ref.at[pl.ds(pl.multiple_of(owner * block + part * half, half), half)]

        def copy(i, owner, part, target):
            piece = rows(owner, part)
            return remote(piece, piece, send.at[i], recv.at[i], at.head(target))

        self.c = [
            copy(0, at.h, 0, at.hx),
            copy(1, at.h, 1, at.hy),
            copy(2, at.h, 1, at.hx),
            copy(3, at.h, 0, at.hy),
            copy(4, at.hx, 0, at.hy),
            copy(5, at.hy, 1, at.hx),
        ]

    def start(self):
        for i in range(4):
            self.c[i].start()

    def forward(self):
        self.c[0].wait_recv()
        self.c[4].start()
        self.c[1].wait_recv()
        self.c[5].start()

    def wait_x(self):
        self.c[2].wait_recv()

    def wait_y(self):
        self.c[3].wait_recv()

    def wait_d(self):
        self.c[4].wait_recv()
        self.c[5].wait_recv()

    def finish(self):
        for copy in self.c:
            copy.wait_send()


class Scatter:
    def __init__(self, at, part, got, send, recv, block):
        half = block // 2
        self.at, self.part, self.got, self.half = at, part, got, half

        def piece(owner, side):
            return part.at[owner, pl.ds(side * half, half)]

        def copy(i, owner, side, target):
            return remote(piece(owner, side), got.at[i], send.at[i], recv.at[i], at.head(target))

        self.c = [
            copy(0, at.hd, 0, at.hx),
            copy(1, at.hd, 1, at.hy),
            copy(2, at.hx, 0, at.hx),
            copy(3, at.hy, 1, at.hy),
            copy(4, at.hy, 0, at.hy),
            copy(5, at.hx, 1, at.hx),
        ]

    def send_d(self):
        self.c[0].start()
        self.c[1].start()

    def send_x(self):
        self.c[2].start()

    def send_y(self):
        self.c[3].start()

    def second(self):
        half, part, got, at = self.half, self.part, self.got, self.at
        self.c[0].wait_recv()
        part[at.hy, :half] = (part[at.hy, :half].astype(F32) + got[0].astype(F32)).astype(BF)
        self.c[4].start()
        self.c[1].wait_recv()
        part[at.hx, half:] = (part[at.hx, half:].astype(F32) + got[1].astype(F32)).astype(BF)
        self.c[5].start()

    def wait(self):
        for i in (2, 3, 4, 5):
            self.c[i].wait_recv()

    def total(self):
        half, part, got, at = self.half, self.part, self.got, self.at
        top = part[at.h, :half].astype(F32) + got[2].astype(F32) + got[4].astype(F32)
        low = part[at.h, half:].astype(F32) + got[3].astype(F32) + got[5].astype(F32)
        return jnp.concatenate([top, low], 0)

    def finish(self):
        for copy in self.c:
            copy.wait_send()


class Ledger:
    def __init__(self, at, dp, refs, sems):
        self.at = at
        self.pieces = refs
        self.cs, self.cr, self.ns, self.ar, self.br, self.os, self.fs, self.fr, self.free = sems
        left = at.z < dp // 2
        step = jnp.where(left, 1, -1)
        self.inner = (at.z + step, at.s, at.h)
        self.outer = (at.z - step, at.s, at.h)
        self.core = (at.z, 1 - at.s, at.h)
        self.mid = (at.z == dp // 2 - 1) | (at.z == dp // 2)
        self.outermost = (at.z == 0) | (at.z == dp - 1)

    def rows(self, i, side):
        ref, c, a, b = self.pieces[i]
        half = ref.shape[0] // 2
        return ref.at[pl.ds(pl.multiple_of(side * half, half), half)]

    def swap(self, i):
        c = self.pieces[i][1]
        return remote(self.rows(i, 1 - self.at.s), c, self.cs.at[i], self.cr.at[i], self.core)

    def inward(self, i):
        return remote(
            self.rows(i, self.at.s), self.pieces[i][2], self.ns.at[i], self.ar.at[i], self.inner
        )

    def across(self, i):
        return remote(
            self.rows(i, self.at.s), self.pieces[i][3], self.ns.at[i], self.br.at[i], self.inner
        )

    def outward(self, i):
        return remote(
            self.rows(i, self.at.s), self.pieces[i][3], self.os.at[i], self.br.at[i], self.outer
        )

    def last(self, i):
        mine = self.rows(i, self.at.s)
        return remote(mine, mine, self.fs.at[i], self.fr.at[i], self.core)

    def release(self, i):
        self.swap(i).wait_send()
        pl.semaphore_signal(
            self.free.at[i], inc=1, device_id=self.core, device_id_type=MESH
        )

    def finish(self, i):
        pl.semaphore_wait(self.free.at[i], 1)
        self.last(i).start()

    def add(self, i, *refs):
        mine = self.rows(i, self.at.s)
        total = mine[...].astype(F32)
        for ref in refs:
            total = total + ref[...].astype(F32)
        mine[...] = total.astype(mine.dtype)

    def open(self, *which):
        for i in which:
            self.swap(i).start()

    def step(self, ends=(), middles=(), turns=(), backs=()):
        for i in ends:

            @pl.when(self.outermost)
            def _():
                self.swap(i).wait_recv()
                self.add(i, self.pieces[i][1])
                self.release(i)
                pl.when(self.mid)(lambda: self.across(i).start())
                pl.when(jnp.logical_not(self.mid))(lambda: self.inward(i).start())

        for i in middles:

            @pl.when(jnp.logical_not(self.outermost))
            def _():
                self.swap(i).wait_recv()
                self.inward(i).wait_recv()
                self.add(i, self.pieces[i][1], self.pieces[i][2])
                self.release(i)
                pl.when(self.mid)(lambda: self.across(i).start())
                pl.when(jnp.logical_not(self.mid))(lambda: self.inward(i).start())

        for i in turns:

            @pl.when(self.mid)
            def _():
                self.across(i).wait_recv()
                self.across(i).wait_send()
                self.add(i, self.pieces[i][3])
                pl.when(jnp.logical_not(self.outermost))(lambda: self.outward(i).start())
                self.finish(i)

        for i in backs:

            @pl.when(jnp.logical_not(self.mid))
            def _():
                self.outward(i).wait_recv()
                self.inward(i).wait_send()
                mine = self.rows(i, self.at.s)
                mine[...] = self.pieces[i][3][...]
                pl.when(jnp.logical_not(self.outermost))(lambda: self.outward(i).start())
                self.finish(i)

    def close(self, i):
        self.last(i).wait_recv()
        self.last(i).wait_send()
        pl.when(jnp.logical_not(self.outermost))(lambda: self.outward(i).wait_send())


PER_ARRAY = 2
SCHEDULE = (
    ((0,), (), (), (), ()),
    ((), (), (), (), ()),
    ((1,), (), (), (), ()),
    ((), (0,), (), (), ()),
    ((2, 3), (1,), (0,), (), ()),
    ((), (), (), (), ()),
    ((), (2,), (1,), (), ()),
    ((), (3,), (), (0,), ()),
    ((4,), (), (), (), ()),
    ((), (), (2,), (), (0,)),
    ((5,), (4,), (), (1,), (1,)),
    ((), (), (3,), (), ()),
    ((6, 7), (5,), (4,), (2, 3), (2,)),
    ((), (6,), (), (), (3,)),
    ((8,), (), (5,), (4,), ()),
    ((9,), (7,), (6,), (), (4,)),
    ((), (), (), (5,), ()),
    ((10,), (8,), (7,), (), (5,)),
    ((11,), (9,), (8,), (6,), (6,)),
    ((), (10,), (9,), (7,), (7,)),
    ((), (), (), (8,), ()),
    ((), (11,), (), (), ()),
    ((), (), (10, 11), (9, 10, 11), (8, 9, 10, 11)),
)


def kernel(dp, section, slots, *refs):
    refs = list(refs)

    def take(count):
        out = refs[:count]
        del refs[:count]
        return out

    far_x, lens, image = take(3)
    g1, c1, far_qkv, bqv, far_o, bo, g2, c2, far_u, bu, far_d, bd = take(12)
    tg1, tc1, tqkv, tbqv, two, tbo, tg2, tc2, far_tu, tbu, far_td, tbd = take(12)
    far_dy, far_grads, vec = take(3)
    x, wqkv, wo, wu, wd, twu, twd, dy, grads = take(9)
    n1, q, k, v, p, o, n2, hid, slope, r1, z = take(11)
    w2, b2, images = take(3)
    part, got = take(2)
    ring, arb, stats, scored, dpool, dn2b, rsb = take(7)
    f_out, f_in, s_out, s_in, a_in = take(5)
    (da,) = take(1)
    dm = dy
    c_in, l_in, b_in, vh_in, vc_in, vl_in, vb_in = take(7)
    ag_sems, rs_sems, w_sems, h_sems, i_sems, st_sems, sm_sems, v_sems = (
        take(2) for _ in range(8)
    )
    ledger_sems = take(9)
    in_sems, out_sems = take(2)
    assert not refs

    at = Place()
    tokens, width = x.shape
    block = tokens // 4
    local = wo.shape[0]
    heads = local // HEAD_DIM
    sub = 128
    captions = tokens // slots
    own_caps = block // slots
    caps = captions
    scale = HEAD_DIM ** (-0.5)
    low_masks = head_masks(local, BF)
    masks = head_masks(local, F32)
    other_core = (at.z, 1 - at.s, at.h)
    zs = [(lax.rem(at.z + j, dp), at.s, at.h) for j in range(1, dp)]
    z_pair = (at.z + 1 - 2 * lax.rem(at.z, 2), at.s, at.h)
    head_peers = [at.hx, at.hy, at.hd]
    others = []
    for j in range(dp):
        for i in range(section):
            if i or j:
                others.append((lax.rem(at.z + j, dp), lax.rem(at.s + i, section), at.h))
    own = pl.ds(pl.multiple_of(at.h * block, block), block)

    def vector(ref):
        return ref[...].reshape(1, -1)

    arrive = at.greet([at.head(j) for j in head_peers] + others)
    loads = [
        pltpu.make_async_copy(source, target, in_sems.at[i])
        for i, (source, target) in enumerate(
            (
                (tqkv, w2.at[at.h, 0:3]),
                (two, w2.at[at.h, 3]),
                (far_x, x),
                (far_qkv, wqkv),
                (far_o, wo),
                (far_u, wu),
                (far_d, wd),
                (far_tu, twu),
                (far_td, twd),
            )
        )
    ]
    for copy in loads:
        copy.start()
    pic = image[...].astype(F32)
    pic = pic * lax.rsqrt(jnp.mean(pic * pic, -1, keepdims=True) + NORM_EPS) * width ** (-0.5)
    images[at.z, at.s] = pic.astype(BF)
    b2[at.h] = tbqv[...]

    quarter = local // 4
    mine = lax.rem(at.z, 2) * 2 + at.s
    pair = (1 - lax.rem(at.z, 2)) * 2 + at.s

    def shard_part(owner, which):
        return w2.at[owner, :, pl.ds(pl.multiple_of(which * quarter, quarter), quarter)]

    def same_place(ref, sems, i, device):
        return remote(ref, ref, sems[0].at[i], sems[1].at[i], device)

    hop1 = [
        same_place(shard_part(at.h, mine), w_sems, i, at.head(j)) for i, j in enumerate(head_peers)
    ]
    hop_b = [same_place(b2.at[at.h], h_sems, i, at.head(j)) for i, j in enumerate(head_peers)]
    hop2 = [
        same_place(shard_part(j, mine), w_sems, 3 + i, z_pair) for i, j in enumerate(head_peers)
    ]
    hop3 = [
        same_place(shard_part(j, which), w_sems, 6 + 3 * n + i, other_core)
        for i, j in enumerate(head_peers)
        for n, which in enumerate((mine, pair))
    ]
    pics = [
        same_place(images.at[at.z, at.s], i_sems, i, device) for i, device in enumerate(zs)
    ]
    core_pics = same_place(images.at[:, at.s], i_sems, dp - 1, other_core)
    for copy in loads[:2]:
        copy.wait()
    arrive()
    for copy in hop1 + hop_b + pics:
        copy.start()

    scatters = [
        Scatter(at, part, got, rs_sems[0].at[i], rs_sems[1].at[i], block) for i in range(4)
    ]
    gathers = [
        Gather(at, ref, ag_sems[0].at[i], ag_sems[1].at[i], block)
        for i, ref in enumerate((n2, dm, da, dy))
    ]

    def block_of(t):
        return lax.rem(at.hi + lax.div(t, 2), 2) * 2 + lax.rem(at.lo + lax.rem(t, 2), 2)

    def limits(first, count):
        cap = lax.broadcasted_iota(jnp.int32, (captions, count), 0)
        slot = lax.broadcasted_iota(jnp.int32, (captions, count), 1)
        chosen = jnp.where(cap == first + slot // slots, 1.0, 0.0).astype(BF)
        row = jnp.broadcast_to(vector(lens).astype(F32), (8, captions)).astype(BF)
        return dot(row, chosen)[:1]

    def key_bias(first, count):
        slot = lax.broadcasted_iota(jnp.int32, (1, count), 1)
        inside = lax.rem(slot, slots).astype(F32) < limits(first, count)
        return jnp.where(inside, 0.0, NEG)

    row_id = lax.broadcasted_iota(jnp.int32, (sub, sub), 0) // slots
    col_id = lax.broadcasted_iota(jnp.int32, (sub, sub), 1) // slots
    same = row_id == col_id
    scatter = scatters[0]

    def attend(t, carry):
        blk = block_of(3 - t)
        rows = pl.ds(pl.multiple_of(blk * block, block), block)
        hat, _ = norm_stats(x[rows].astype(F32))
        normed = (hat * vector(g1) + vector(c1)).astype(BF)
        n1[rows] = normed
        query = (dot_nt(normed, wqkv[0]) + bqv[0:1]).astype(BF)
        keys = dot_nt(normed, wqkv[1]).astype(BF)
        values = (dot_nt(normed, wqkv[2]) + bqv[1:2]).astype(BF)
        q[rows] = query
        k[rows] = keys
        v[rows] = values
        mixed = []
        for m in range(block // sub):
            cut = slice(m * sub, (m + 1) * sub)
            index = blk * (block // sub) + m
            bias = jnp.where(same, key_bias(index * (sub // slots), sub), NEG)
            total = jnp.zeros((sub, local), F32)
            for i in range(heads):
                scores = dot_nt(query[cut] * low_masks[i], keys[cut]) * scale + bias
                scores = jnp.exp(scores - jnp.max(scores, -1, keepdims=True))
                probs = (scores * (1.0 / jnp.sum(scores, -1, keepdims=True))).astype(BF)
                p[index, i] = probs
                total = total + dot(probs, values[cut]) * masks[i]
            mixed.append(total.astype(BF))
        mixed = jnp.concatenate(mixed, 0)
        o[rows] = mixed
        part[blk] = dot(mixed, wo[...]).astype(BF)
        pl.when(t == 0)(scatter.send_d)
        pl.when(t == 1)(scatter.send_y)
        pl.when(t == 2)(scatter.send_x)
        return carry

    for copy in loads[2:5]:
        copy.wait()
    lax.fori_loop(0, 4, attend, 0)
    scatter.second()
    for i in range(3):
        hop1[i].wait_recv()
        hop2[i].start()
    scatter.wait()
    resid = x[own].astype(F32) + scatter.total() + vector(bo)
    scatter.finish()
    r1[...] = resid
    hat, _ = norm_stats(resid)
    n2[own] = (hat * vector(g2) + vector(c2)).astype(BF)

    def waits(t, gather):
        @pl.when(t == 1)
        def _():
            gather.forward()
            gather.wait_x()

        pl.when(t == 2)(gather.wait_y)
        pl.when(t == 3)(gather.wait_d)

    def sends(t, scatter):
        pl.when(t == 1)(scatter.send_x)
        pl.when(t == 2)(scatter.send_y)
        pl.when(t == 3)(scatter.send_d)

    gathers[0].start()
    for copy in loads[5:7]:
        copy.wait()

    def feed(t, carry):
        waits(t, gathers[0])
        blk = block_of(t)
        rows = pl.ds(pl.multiple_of(blk * block, block), block)
        value, steep = gelu_pair(dot(n2[rows], wu[...]) + vector(bu))
        value = value.astype(BF)
        hid[rows] = value
        slope[rows] = steep.astype(BF)
        part[blk] = dot(value, wd[...]).astype(BF)
        sends(t, scatters[1])
        return carry

    lax.fori_loop(0, 4, feed, 0)
    for i in range(3):
        hop2[i].wait_recv()
        hop3[2 * i].start()
        hop3[2 * i + 1].start()
    for copy in pics:
        copy.wait_recv()
    core_pics.start()
    scatters[1].second()
    scatters[1].wait()
    zv = r1[...] + scatters[1].total() + vector(bd)
    scatters[1].finish()
    z[...] = zv
    for copy in hop_b + hop3 + [core_pics]:
        copy.wait_recv()

    per = heads * own_caps

    def stack(values):
        return jnp.concatenate([values * low_masks[i] for i in range(heads)], 0)

    def pick_heads(values):
        total = values[:own_caps] * masks[0]
        for i in range(1, heads):
            total = total + values[i * own_caps : (i + 1) * own_caps] * masks[i]
        return total

    first_cap = at.h * own_caps
    last_slot = limits(first_cap, block) - 1.0
    slot_row = lax.broadcasted_iota(jnp.int32, (own_caps, block), 1)
    cap_row = lax.broadcasted_iota(jnp.int32, (own_caps, block), 0)
    picked = (slot_row // slots == cap_row) & (lax.rem(slot_row, slots).astype(F32) == last_slot)
    pick = jnp.where(picked, 1.0, 0.0).astype(BF)
    cap_of = lax.broadcasted_iota(jnp.int32, (block, captions), 0)
    cap_at = lax.broadcasted_iota(jnp.int32, (block, captions), 1)
    length_col = jnp.sum(
        jnp.where(cap_at == first_cap + cap_of // slots, vector(lens).astype(F32), 0.0),
        1,
        keepdims=True,
    )
    slot_col = lax.rem(lax.broadcasted_iota(jnp.int32, (block, 1), 0), slots).astype(F32)
    pcol = jnp.where(slot_col == length_col - 1.0, 1.0, 0.0)

    hat1, rstd1 = norm_stats(zv)
    normed = (hat1 * vector(tg1) + vector(tc1)).astype(BF)
    pooled_low = dot(pick, normed).astype(BF)
    a_in[at.h, 0] = pooled_low
    z_pool = jnp.sum((zv * pcol).reshape(own_caps, slots, width), 1)
    us = []
    for j in range(4):
        query = (dot_nt(pooled_low, w2[j, 0]) + b2[j, 0:1]).astype(BF)
        s_out[j, 0] = query
        us.append(dot(stack(query), w2[j, 1]).astype(BF))
    u_all = jnp.concatenate(us, 0)
    rows_n = 4 * per
    row_cap = lax.rem(lax.broadcasted_iota(jnp.int32, (rows_n, block), 0), own_caps)
    col_cap = lax.broadcasted_iota(jnp.int32, (rows_n, block), 1) // slots
    bias = jnp.where(row_cap == col_cap, key_bias(first_cap, block), NEG)
    scores = dot_nt(u_all, normed) * scale + bias
    scores = jnp.exp(scores - jnp.max(scores, -1, keepdims=True))
    probs = scores * (1.0 / jnp.sum(scores, -1, keepdims=True))
    probs_low = probs.astype(BF)
    mix = dot(probs_low, normed).astype(BF)
    attended = jnp.zeros((own_caps, width), F32)
    for j in range(4):
        piece = mix[j * per : (j + 1) * per]
        f_out[j, 0] = piece
        out = (pick_heads(dot_nt(piece, w2[j, 2])) + b2[j, 1:2]).astype(BF)
        s_out[j, 3] = out
        attended = attended + dot(out, w2[j, 3])
    ring[at.h] = z_pool + attended + vector(tbo)

    def small(ref, i, j, target=None):
        return remote(
            ref,
            ref if target is None else target,
            sm_sems[0].at[i],
            sm_sems[1].at[i],
            at.head(j),
        )

    for copy in loads[7:]:
        copy.wait()
    rings = [small(ring.at[at.h], i, j) for i, j in enumerate(head_peers)]
    early = [
        small(f_out.at[j, 0], 18 + i, j, f_in.at[at.h, 0]) for i, j in enumerate(head_peers)
    ]
    for copy in rings + early:
        copy.start()
    for copy in rings:
        copy.wait_recv()

    r1_all = ring[...].reshape(caps, width)
    hat2_all, _ = norm_stats(r1_all)
    n2_top = (hat2_all * vector(tg2) + vector(tc2)).astype(BF)
    value, steep = gelu_pair(dot(n2_top, twu[...]) + vector(tbu))
    value = value.astype(BF)
    arb[at.h] = dot(value, twd[...]).astype(BF)
    sums = [small(arb.at[at.h], 3 + i, j) for i, j in enumerate(head_peers)]
    for copy in sums:
        copy.start()
    for copy in sums:
        copy.wait_recv()
    pooled = r1_all + vector(tbd)
    for j in range(4):
        pooled = pooled + arb[j].astype(F32)
    unit_r = lax.rsqrt(jnp.mean(pooled * pooled, -1, keepdims=True) + NORM_EPS)
    text = (pooled * unit_r * width ** (-0.5)).astype(BF)

    everyone = dp * section * caps
    batch = min(dp, 4)
    wide = batch * section * caps
    lanes = wide // 4
    place = at.z * section + at.s

    def chunk_images(n):
        return images[n * batch : (n + 1) * batch].reshape(wide, width)

    def own_columns(n):
        col = lax.broadcasted_iota(jnp.int32, (caps, wide), 1) + n * wide
        row = lax.broadcasted_iota(jnp.int32, (caps, wide), 0) + place * caps
        return col == row

    chunks = [slice(n * wide, (n + 1) * wide) for n in range(dp // batch)]
    row_max = diagonal = None
    for n, cols in enumerate(chunks):
        logits = LOGIT_SCALE * dot_nt(text, chunk_images(n))
        scored[:, cols] = logits
        found = jnp.max(logits, 1, keepdims=True)
        row_max = found if row_max is None else jnp.maximum(row_max, found)
        found = jnp.sum(jnp.where(own_columns(n), logits, 0.0), 1, keepdims=True)
        diagonal = found if diagonal is None else diagonal + found
        col_max = jnp.max(logits, 0, keepdims=True)
        col_sum = jnp.sum(jnp.exp(logits - col_max), 0, keepdims=True)
        for i in range(4):
            stats[place, n, i : i + 1] = col_max[:, i * lanes : (i + 1) * lanes]
            stats[place, n, 4 + i : 5 + i] = col_sum[:, i * lanes : (i + 1) * lanes]
    tells = [
        same_place(stats.at[place], st_sems, i, device) for i, device in enumerate(others)
    ]
    for copy in tells:
        copy.start()
    row_sum = None
    for n, cols in enumerate(chunks):
        found = jnp.sum(jnp.exp(scored[:, cols] - row_max), 1, keepdims=True)
        row_sum = found if row_sum is None else row_sum + found
    row_lse = row_max + jnp.log(row_sum)

    def pull(n, cols, lse):
        steep = jnp.exp(scored[:, cols] - lse) - jnp.where(own_columns(n), 1.0, 0.0)
        return dot((steep * (0.5 / everyone)).astype(BF), chunk_images(n))

    text_grad = None
    for n, cols in enumerate(chunks):
        term = pull(n, cols, row_lse)
        text_grad = term if text_grad is None else text_grad + term
    lost = jnp.sum(row_lse - 2.0 * diagonal, 0, keepdims=True)
    for copy in tells:
        copy.wait_recv()
    for n, cols in enumerate(chunks):
        told = stats[:, n]
        top = jnp.max(told[:, 0:4], 0)
        total = jnp.sum(told[:, 4:8] * jnp.exp(told[:, 0:4] - top[None]), 0)
        lse = top + jnp.log(total)
        col_lse = jnp.concatenate([lse[i : i + 1] for i in range(4)], 1)
        text_grad = text_grad + pull(n, cols, col_lse)
        found = jnp.sum(jnp.where(own_columns(n), col_lse, 0.0), 1, keepdims=True)
        lost = lost + jnp.sum(found, 0, keepdims=True)
    text_grad = LOGIT_SCALE * text_grad
    inner = jnp.mean(pooled * text_grad, -1, keepdims=True)
    d_pool = (unit_r * width ** (-0.5)) * (text_grad - pooled * (unit_r * unit_r * inner))
    dpool[...] = d_pool

    per_array = PER_ARRAY
    span = width // per_array
    pieces = []
    for a in range(6):
        for n in range(per_array):
            i = a * per_array + n
            pieces.append(
                (grads.at[a, pl.ds(n * span, span)], c_in.at[i], l_in.at[i], b_in.at[i])
            )
    count = len(pieces)
    pieces.append((vec, vc_in, vl_in, vb_in))
    ledger = Ledger(at, dp, pieces, ledger_sems)

    def opened(a):
        ledger.open(*range(a * per_array, (a + 1) * per_array))

    def flush(i):
        a, n = divmod(i, per_array)
        rows = pl.ds(n * span, span)
        return pltpu.make_async_copy(grads.at[a, rows], far_grads.at[a, rows], out_sems.at[i])

    def slot(number):
        ends, middles, turns, backs, done = SCHEDULE[number]
        ledger.step(ends, middles, turns, backs)
        for i in done:
            ledger.close(i)
            flush(i).start()

    low = d_pool.astype(BF)
    du_top = (dot_nt(low, twd[...]) * steep).astype(BF)
    dn2b[...] = dot_nt(du_top, twu[...]).astype(BF)
    own_rows = pl.ds(pl.multiple_of(at.h * own_caps, own_caps), own_caps)
    backs = []
    for i, j in enumerate(head_peers):
        there = pl.ds(pl.multiple_of(j * own_caps, own_caps), own_caps)
        backs.append(small(dn2b.at[there], 6 + i, j, rsb.at[at.h]))
    for copy in backs:
        copy.start()
    grads[0] = dot_tn(value, low).astype(BF)
    opened(0)
    grads[1] = dot_tn(n2_top, du_top).astype(BF)
    opened(1)
    vec[...] = jnp.zeros_like(vec)
    vec[22:23, 0:128] = jnp.broadcast_to(lost, (1, 128))
    vec[17:18] = rows_sum(du_top.astype(F32))
    rsb[at.h] = dn2b[own_rows]
    slot(0)
    for copy in backs:
        copy.wait_recv()
    dn2 = rsb[0].astype(F32)
    for j in range(1, 4):
        dn2 = dn2 + rsb[j].astype(F32)
    hat2, rstd2 = norm_stats(ring[at.h])
    dpool_own = dpool[own_rows]
    dr1_top = dpool_own + norm_back(dn2, hat2, rstd2, vector(tg2))
    vec[8:9] = rows_sum(dr1_top)
    vec[9:10] = rows_sum(dn2 * hat2)
    vec[10:11] = rows_sum(dn2)
    vec[11:12] = rows_sum(dpool_own)

    slot(1)

    da_top = dr1_top.astype(BF)
    a_in[at.h, 1] = da_top
    ws = []
    for j in range(4):
        d_out = dot_nt(da_top, w2[j, 3]).astype(BF)
        s_out[j, 2] = d_out
        ws.append(dot(stack(d_out), w2[j, 2]).astype(BF))
    w_all = jnp.concatenate(ws, 0)
    d_probs = dot_nt(w_all, normed)
    d_scores = probs * (d_probs - jnp.sum(probs * d_probs, -1, keepdims=True))
    scores_low = d_scores.astype(BF)
    g_rows = (dot(scores_low, normed) * scale).astype(BF)
    slot(2)
    d_pooled_low = jnp.zeros((own_caps, width), F32)
    for j in range(4):
        piece = g_rows[j * per : (j + 1) * per]
        f_out[j, 1] = piece
        d_query = pick_heads(dot_nt(piece, w2[j, 1])).astype(BF)
        s_out[j, 1] = d_query
        d_pooled_low = d_pooled_low + dot(d_query, w2[j, 0])
    facts = []
    for i, j in enumerate(head_peers):
        facts.append(small(f_out.at[j, 1], 9 + i, j, f_in.at[at.h, 1]))
        facts.append(small(s_out.at[j], 12 + i, j, s_in.at[at.h]))
        facts.append(small(a_in.at[at.h], 15 + i, j))
    dn = dot_tn(scores_low, u_all) * scale + dot_tn(probs_low, w_all)

    def widen(values):
        values = jnp.broadcast_to(values[:, None, :], (own_caps, slots, width))
        return values.reshape(block, width)

    dn = dn + pcol * widen(d_pooled_low)
    dz = norm_back(dn, hat1, rstd1, vector(tg1)) + pcol * widen(dr1_top)
    dm[own] = dz.astype(BF)
    gathers[1].start()
    for copy in facts:
        copy.start()
    z[...] = dz
    vec[6:7] = rows_sum(dn * hat1)
    vec[7:8] = rows_sum(dn)
    vec[5:6] = rows_sum(dz)

    f_in[at.h] = f_out[at.h]
    s_in[at.h] = s_out[at.h]
    slot(3)
    scatter_a = scatters[2]

    def feed_back(t, carry):
        waits(t, gathers[1])
        blk = block_of(t)
        rows = pl.ds(pl.multiple_of(blk * block, block), block)
        grad = (dot_nt(dm[rows], wd[...]) * slope[rows].astype(F32)).astype(BF)
        slope[rows] = grad
        part[blk] = dot_nt(grad, wu[...]).astype(BF)
        sends(t, scatter_a)
        for i in range(3):
            pl.when(t == i)(lambda: slot(4 + i))
        return carry

    lax.fori_loop(0, 4, feed_back, 0)
    gathers[1].finish()
    for copy in early + facts:
        copy.wait_recv()
    pooled_all = jnp.concatenate([a_in[j, 0] for j in range(4)], 0)
    da_all = jnp.concatenate([a_in[j, 1] for j in range(4)], 0)
    dq_all = jnp.concatenate([s_in[j, 1] for j in range(4)], 0)
    do_all = jnp.concatenate([s_in[j, 2] for j in range(4)], 0)
    out_all = jnp.concatenate([s_in[j, 3] for j in range(4)], 0)
    grads[2, 0:local] = dot_tn(dq_all, pooled_all).astype(BF)
    grads[2, local : 2 * local] = dot_tn(
        jnp.concatenate([stack(s_in[j, 0]) for j in range(4)], 0),
        jnp.concatenate([f_in[j, 1] for j in range(4)], 0),
    ).astype(BF)
    grads[2, 2 * local : 3 * local] = dot_tn(
        jnp.concatenate([stack(s_in[j, 2]) for j in range(4)], 0),
        jnp.concatenate([f_in[j, 0] for j in range(4)], 0),
    ).astype(BF)
    grads[2, 3 * local :] = dot_tn(out_all, da_all).astype(BF)
    opened(2)
    vec[20:21, 0:local] = rows_sum(dq_all.astype(F32))
    vec[21:22, 0:local] = rows_sum(do_all.astype(F32))
    slot(7)
    grads[3] = dot_tn(hid[...], dm[...]).astype(BF)
    opened(3)
    slot(8)
    grads[4] = dot_tn(n2[...], slope[...]).astype(BF)
    opened(4)
    slot(9)
    scatter_a.second()
    vec[16:17] = rows_sum(slope[...].astype(F32))
    slot(10)
    scatter_a.wait()
    dn2 = scatter_a.total()
    scatter_a.finish()
    hat, rstd = norm_stats(r1[...])
    back = z[...] + norm_back(dn2, hat, rstd, vector(g2))
    r1[...] = back
    da[own] = back.astype(BF)
    gathers[2].start()
    vec[2:3] = rows_sum(back)
    vec[3:4] = rows_sum(dn2 * hat)
    vec[4:5] = rows_sum(dn2)

    slot(11)
    scatter_b = scatters[3]

    def attend_back(t, carry):
        waits(t, gathers[2])
        blk = block_of(t)
        rows = pl.ds(pl.multiple_of(blk * block, block), block)
        d_out = dot_nt(da[rows], wo[...]).astype(BF)
        query, keys, values = q[rows], k[rows], v[rows]
        parts = [[], [], []]
        for m in range(block // sub):
            cut = slice(m * sub, (m + 1) * sub)
            index = blk * (block // sub) + m
            dq = jnp.zeros((sub, local), F32)
            dk = jnp.zeros((sub, local), F32)
            dv = jnp.zeros((sub, local), F32)
            for i in range(heads):
                probs_low = p[index, i]
                probs = probs_low.astype(F32)
                d_probs = dot_nt(d_out[cut] * low_masks[i], values[cut])
                d_scores = probs * (d_probs - jnp.sum(probs * d_probs, -1, keepdims=True))
                d_scores = d_scores.astype(BF)
                dq = dq + dot(d_scores, keys[cut]) * masks[i]
                dk = dk + dot_tn(d_scores, query[cut]) * masks[i]
                dv = dv + dot_tn(probs_low, d_out[cut]) * masks[i]
            parts[0].append((dq * scale).astype(BF))
            parts[1].append((dk * scale).astype(BF))
            parts[2].append(dv.astype(BF))
        total = None
        for i in range(3):
            whole = jnp.concatenate(parts[i], 0)
            (q, k, v)[i][rows] = whole
            term = dot(whole, wqkv[i])
            total = term if total is None else total + term
        part[blk] = total.astype(BF)
        sends(t, scatter_b)
        for i in range(3):
            pl.when(t == i)(lambda: slot(12 + i))
        return carry

    lax.fori_loop(0, 4, attend_back, 0)
    for i in range(2):
        grads[5, i * local : (i + 1) * local] = dot_tn((q, k)[i][...], n1[...]).astype(BF)
    slot(15)
    grads[5, 2 * local : 3 * local] = dot_tn(v[...], n1[...]).astype(BF)
    grads[5, 3 * local :] = dot_tn(o[...], da[...]).astype(BF)
    opened(5)
    slot(16)
    scatter_b.second()
    vec[18:19, 0:local] = rows_sum(q[...].astype(F32))
    vec[19:20, 0:local] = rows_sum(v[...].astype(F32))
    slot(17)
    scatter_b.wait()
    dn1 = scatter_b.total()
    hat, rstd = norm_stats(x[own].astype(F32))
    dy[own] = (r1[...] + norm_back(dn1, hat, rstd, vector(g1))).astype(BF)
    gathers[3].start()
    vec[0:1] = rows_sum(dn1 * hat)
    vec[1:2] = rows_sum(dn1)

    vh_in[at.h] = vec[0:16]
    tops = [
        same_place(vh_in.at[at.h], v_sems, i, at.head(j)) for i, j in enumerate(head_peers)
    ]
    for copy in tops:
        copy.start()
    slot(18)
    for copy in tops:
        copy.wait_recv()
    vec[0:16] = vh_in[0] + vh_in[1] + vh_in[2] + vh_in[3]
    ledger.open(count)
    gathers[3].forward()
    slot(19)
    ledger.step(ends=(count,), middles=(count,))
    gathers[3].wait_x()
    gathers[3].wait_y()
    slot(20)
    ledger.step(turns=(count,))
    gathers[3].wait_d()
    spill = pltpu.make_async_copy(dy, far_dy, out_sems.at[count])
    spill.start()
    slot(21)
    ledger.step(backs=(count,))
    slot(22)
    ledger.close(count)
    for i in range(count):
        flush(i).wait()
    spill.wait()
    scatter_b.finish()
    for i in (0, 2, 3):
        gathers[i].finish()
    for copy in hop1 + hop_b + hop2 + hop3 + pics + [core_pics]:
        copy.wait_send()
    for copy in rings + early + sums + tells + backs + facts + tops:
        copy.wait_send()


def run_kernel(dp, section, slots, x, lens, image, base, top):
    tokens, width = x.shape
    local = base[4].shape[0]
    ff = base[8].shape[1]
    block = tokens // 4
    heads = local // HEAD_DIM
    captions = image.shape[0]
    own_caps = captions // 4
    per = heads * own_caps
    everyone = dp * section * captions
    batch = min(dp, 4)
    others = dp * section - 1
    vmem = pl.BlockSpec(memory_space=pltpu.VMEM)
    hbm = pl.BlockSpec(memory_space=pl.ANY)
    big = (0, 5, 7, 11, 13, 17, 19, 23, 25)
    shape = jax.ShapeDtypeStruct
    outs = [
        shape((tokens, width), BF),
        shape((6, width, width), BF),
        shape((32, width), F32),
    ]
    assert ff == width and 4 * local == width
    sems = pltpu.SemaphoreType.DMA
    ram = pltpu.VMEM
    half_piece = width // (2 * PER_ARRAY)
    count = 6 * PER_ARRAY
    scratch = [
        ram((tokens, width), BF),
        ram((3, local, width), BF),
        ram((local, width), BF),
        ram((width, ff), BF),
        ram((ff, width), BF),
        ram((width, ff), BF),
        ram((ff, width), BF),
        ram((tokens, width), BF),
        ram((6, width, width), BF),
        ram((tokens, width), BF),
        ram((tokens, local), BF),
        ram((tokens, local), BF),
        ram((tokens, local), BF),
        ram((tokens // 128, heads, 128, 128), BF),
        ram((tokens, local), BF),
        ram((tokens, width), BF),
        ram((tokens, ff), BF),
        ram((tokens, ff), BF),
        ram((block, width), F32),
        ram((block, width), F32),
        ram((4, 4, local, width), BF),
        ram((4, 2, local), F32),
        ram((dp, section, captions, width), BF),
        ram((4, block, width), BF),
        ram((6, block // 2, width), BF),
        ram((4, own_caps, width), F32),
        ram((4, captions, width), BF),
        ram((dp * section, dp // batch, 8, everyone // (dp // batch) // 4), F32),
        ram((captions, everyone), F32),
        ram((captions, width), F32),
        ram((captions, width), BF),
        ram((4, own_caps, width), BF),
        ram((4, 2, per, width), BF),
        ram((4, 2, per, width), BF),
        ram((4, 4, own_caps, local), BF),
        ram((4, 4, own_caps, local), BF),
        ram((4, 2, own_caps, width), BF),
        ram((tokens, width), BF),
        ram((count, half_piece, width), BF),
        ram((count, half_piece, width), BF),
        ram((count, half_piece, width), BF),
        ram((4, 16, width), F32),
        ram((16, width), F32),
        ram((16, width), F32),
        ram((16, width), F32),
    ]
    for many in ((4, 6), (4, 6), (12,), (3,), (dp,), (others,), (21,), (3,)):
        scratch += [sems(many), sems(many)]
    scratch += [sems((count + 1,))] * 8 + [pltpu.SemaphoreType.REGULAR((count + 1,))]
    scratch += [sems((9,)), sems((count + 1,))]
    return pl.pallas_call(
        functools.partial(kernel, dp, section, slots),
        out_shape=outs,
        in_specs=[hbm if i in big else vmem for i in range(27)],
        out_specs=[hbm, hbm, vmem],
        scratch_shapes=scratch,
        compiler_params=pltpu.CompilerParams(
            collective_id=0, has_side_effects=True, vmem_limit_bytes=VMEM_LIMIT
        ),
        cost_estimate=pl.CostEstimate(
            flops=14 * 10**9, bytes_accessed=40 * 10**6, transcendentals=4 * 10**6
        ),
    )(x, lens, image, *base, *top)


def widen_kernel(local, scale, far_dy, far_grads, vec, *refs):
    loss, text, base, top = refs[0], refs[1], refs[2:14], refs[14:26]
    near_dy, near_grads, wide_text, wide_grads, dy_in, dy_out, g_in, g_out = refs[26:]
    rows = wide_text.shape[0] // 4
    width = wide_text.shape[1]
    incoming = []
    for a in (3, 4, 5, 0, 1, 2):
        for n in range(4):
            span = pl.ds(n * local, local)
            incoming.append(
                pltpu.make_async_copy(
                    far_grads.at[a, span], near_grads.at[a, span], g_in.at[4 * a + n]
                )
            )
    texts = []
    for n in range(4):
        span = pl.ds(n * rows, rows)
        texts.append(pltpu.make_async_copy(far_dy.at[span], near_dy.at[span], dy_in.at[n]))
    for copy in incoming + texts:
        copy.start()
    loss[...] = vec[22:23, 0:1] * scale
    for layer, row, bu, bqv in ((base, 0, 16, 18), (top, 6, 17, 20)):
        layer[0][...] = vec[row]
        layer[1][...] = vec[row + 1]
        layer[3][...] = vec[bqv : bqv + 2, 0:local]
        layer[5][...] = vec[row + 2]
        layer[6][...] = vec[row + 3]
        layer[7][...] = vec[row + 4]
        layer[9][...] = vec[bu]
        layer[11][...] = vec[row + 5]
    outgoing = []
    for i, copy in enumerate(incoming):
        a, n = (3, 4, 5, 0, 1, 2)[i // 4], i % 4
        layer = base if a >= 3 else top
        span = pl.ds(n * local, local)
        copy.wait()
        wide_grads[a, span] = near_grads[a, span].astype(F32)
        if a % 3 == 2:
            target = layer[2].at[n] if n < 3 else layer[4]
        else:
            target = layer[10 if a % 3 == 0 else 8].at[span]
        outgoing.append(
            pltpu.make_async_copy(wide_grads.at[a, span], target, g_out.at[4 * a + n])
        )
        outgoing[-1].start()
    for n, copy in enumerate(texts):
        span = pl.ds(n * rows, rows)
        copy.wait()
        wide_text[span] = near_dy[span].astype(F32)
        outgoing.append(pltpu.make_async_copy(wide_text.at[span], text.at[span], dy_out.at[n]))
        outgoing[-1].start()
    for copy in outgoing:
        copy.wait()


def widen(local, scale, dy, grads, vec):
    tokens, width = dy.shape
    vmem = pl.BlockSpec(memory_space=pltpu.VMEM)
    hbm = pl.BlockSpec(memory_space=pl.ANY)
    shape = jax.ShapeDtypeStruct
    line = (shape((width,), F32), vmem)
    square = (shape((width, width), F32), hbm)
    layer = [
        line,
        line,
        (shape((3, local, width), F32), hbm),
        (shape((2, local), F32), vmem),
        (shape((local, width), F32), hbm),
        line,
        line,
        line,
        square,
        line,
        square,
        line,
    ]
    outs = [(shape((1, 1), F32), vmem), (shape((tokens, width), F32), hbm)] + layer * 2
    sems = pltpu.SemaphoreType.DMA
    return pl.pallas_call(
        functools.partial(widen_kernel, local, scale),
        out_shape=[item[0] for item in outs],
        in_specs=[hbm, hbm, vmem],
        out_specs=[item[1] for item in outs],
        scratch_shapes=[
            pltpu.VMEM((tokens, width), BF),
            pltpu.VMEM((6, width, width), BF),
            pltpu.VMEM((tokens, width), F32),
            pltpu.VMEM((6, width, width), F32),
            sems((4,)),
            sems((4,)),
            sems((24,)),
            sems((24,)),
        ],
        compiler_params=pltpu.CompilerParams(vmem_limit_bytes=VMEM_LIMIT),
        cost_estimate=pl.CostEstimate(
            flops=10**7, bytes_accessed=26 * 10**6, transcendentals=0
        ),
    )(dy, grads, vec)


def on_device(dp, section, text_in, lengths, image_embed, *params):
    base, top = params[:12], params[12:]
    captions, slots, width = text_in.shape
    tokens = captions * slots
    local = base[4].shape[0]

    def layout(layer):
        return layer[:2] + (layer[2].transpose(1, 2, 0),) + layer[3:]

    dy, grads, vec = run_kernel(
        dp,
        section,
        slots,
        text_in.reshape(tokens, width),
        lengths,
        image_embed,
        layout(base),
        layout(top),
    )
    outs = list(widen(local, 0.5 / (dp * section * captions), dy, grads, vec))
    for i in (4, 16):
        outs[i] = outs[i].transpose(2, 0, 1)
    return (outs[0][0, 0], outs[1].reshape(captions, slots, width)) + tuple(outs[2:])


def solution(mesh):
    layer_in = (
        P(),
        P(),
        P(None, None, "head"),
        P(None, "head"),
        P("head", None),
        P(),
        P(),
        P(),
        P(None, "head"),
        P("head"),
        P("head", None),
        P(),
    )
    rows = P(("dp", "section"), None, None)
    return jax.shard_map(
        functools.partial(on_device, mesh.shape["dp"], mesh.shape["section"]),
        mesh=mesh,
        in_specs=(rows, P(("dp", "section")), P(("dp", "section"), None)) + layer_in * 2,
        out_specs=(P(), rows) + layer_in * 2,
        check_vma=False,
    )
```

```python
import functools

import jax
import jax.numpy as jnp
from jax import lax
from jax.experimental import pallas as pl
from jax.experimental.pallas import tpu as pltpu
from jax.sharding import PartitionSpec as P

HEAD_DIM = 64
NORM_EPS = 1e-06
LOGIT_SCALE = 50.0
NEG = -1e30
BF = jnp.bfloat16
F32 = jnp.float32
MESH = pl.DeviceIdType.MESH
VMEM_LIMIT = 63 * 2**20


def dot(a, b):
    return lax.dot_general(a, b, (((1,), (0,)), ((), ())), preferred_element_type=F32)


def dot_nt(a, b):
    return lax.dot_general(a, b, (((1,), (1,)), ((), ())), preferred_element_type=F32)


def dot_tn(a, b):
    return lax.dot_general(a, b, (((0,), (0,)), ((), ())), preferred_element_type=F32)


def norm_stats(values):
    center = jnp.mean(values, -1, keepdims=True)
    shifted = values - center
    spread = jnp.mean(shifted * shifted, -1, keepdims=True)
    rstd = lax.rsqrt(spread + NORM_EPS)
    return shifted * rstd, rstd


def norm_back(grad, hat, rstd, gain):
    scaled = grad * gain
    m1 = jnp.mean(scaled, -1, keepdims=True)
    m2 = jnp.mean(scaled * hat, -1, keepdims=True)
    return rstd * (scaled - m1 - hat * m2)


def rows_sum(values):
    return jnp.sum(values, 0, keepdims=True)


def gelu_pair(u):
    c = 0.7978845608028654
    u2 = u * u
    t = jnp.tanh(c * u * (1.0 + 0.044715 * u2))
    half = 0.5 * (1.0 + t)
    value = u * half
    slope = half + 0.5 * u * (1.0 - t * t) * (c * (1.0 + 3.0 * 0.044715 * u2))
    return value, slope


def head_masks(width, kind):
    lane = lax.broadcasted_iota(jnp.int32, (1, width), 1)
    return [
        jnp.where((lane >= i * HEAD_DIM) & (lane < (i + 1) * HEAD_DIM), 1.0, 0.0).astype(kind)
        for i in range(width // HEAD_DIM)
    ]


class Place:
    def __init__(self):
        self.z = lax.axis_index("dp")
        self.s = lax.axis_index("section")
        h = lax.axis_index("head")
        self.h = h
        self.hi = lax.div(h, 2)
        self.lo = lax.rem(h, 2)
        self.hx = self.block(0, 1)
        self.hy = self.block(1, 0)
        self.hd = self.block(1, 1)

    def block(self, flip_hi, flip_lo):
        return lax.rem(self.hi + flip_hi, 2) * 2 + lax.rem(self.lo + flip_lo, 2)

    def head(self, other):
        return (self.z, self.s, other)

    def greet(self, devices):
        barrier = pltpu.get_barrier_semaphore()
        for device in devices:
            pl.semaphore_signal(barrier, inc=1, device_id=device, device_id_type=MESH)
        return lambda: pl.semaphore_wait(barrier, len(devices))


def remote(src, dst, send_sem, recv_sem, device):
    return pltpu.make_async_remote_copy(
        src_ref=src,
        dst_ref=dst,
        send_sem=send_sem,
        recv_sem=recv_sem,
        device_id=device,
        device_id_type=MESH,
    )


class Gather:
    def __init__(self, at, ref, send, recv, block):
        half = block // 2

        def rows(owner, part):
            return ref.at[pl.ds(pl.multiple_of(owner * block + part * half, half), half)]

        def copy(i, owner, part, target):
            piece = rows(owner, part)
            return remote(piece, piece, send.at[i], recv.at[i], at.head(target))

        self.c = [
            copy(0, at.h, 0, at.hx),
            copy(1, at.h, 1, at.hy),
            copy(2, at.h, 1, at.hx),
            copy(3, at.h, 0, at.hy),
            copy(4, at.hx, 0, at.hy),
            copy(5, at.hy, 1, at.hx),
        ]

    def start(self):
        for i in range(4):
            self.c[i].start()

    def forward(self):
        self.c[0].wait_recv()
        self.c[4].start()
        self.c[1].wait_recv()
        self.c[5].start()

    def wait_x(self):
        self.c[2].wait_recv()

    def wait_y(self):
        self.c[3].wait_recv()

    def wait_d(self):
        self.c[4].wait_recv()
        self.c[5].wait_recv()

    def finish(self):
        for copy in self.c:
            copy.wait_send()


class Scatter:
    def __init__(self, at, part, got, send, recv, block):
        half = block // 2
        self.at, self.part, self.got, self.half = at, part, got, half

        def piece(owner, side):
            return part.at[owner, pl.ds(side * half, half)]

        def copy(i, owner, side, target):
            return remote(piece(owner, side), got.at[i], send.at[i], recv.at[i], at.head(target))

        self.c = [
            copy(0, at.hd, 0, at.hx),
            copy(1, at.hd, 1, at.hy),
            copy(2, at.hx, 0, at.hx),
            copy(3, at.hy, 1, at.hy),
            copy(4, at.hy, 0, at.hy),
            copy(5, at.hx, 1, at.hx),
        ]

    def send_d(self):
        self.c[0].start()
        self.c[1].start()

    def send_x(self):
        self.c[2].start()

    def send_y(self):
        self.c[3].start()

    def second(self):
        half, part, got, at = self.half, self.part, self.got, self.at
        self.c[0].wait_recv()
        part[at.hy, :half] = (part[at.hy, :half].astype(F32) + got[0].astype(F32)).astype(BF)
        self.c[4].start()
        self.c[1].wait_recv()
        part[at.hx, half:] = (part[at.hx, half:].astype(F32) + got[1].astype(F32)).astype(BF)
        self.c[5].start()

    def wait(self):
        for i in (2, 3, 4, 5):
            self.c[i].wait_recv()

    def total(self):
        half, part, got, at = self.half, self.part, self.got, self.at
        top = part[at.h, :half].astype(F32) + got[2].astype(F32) + got[4].astype(F32)
        low = part[at.h, half:].astype(F32) + got[3].astype(F32) + got[5].astype(F32)
        return jnp.concatenate([top, low], 0)

    def finish(self):
        for copy in self.c:
            copy.wait_send()


class Ledger:
    def __init__(self, at, dp, refs, sems):
        self.at = at
        self.pieces = refs
        self.cs, self.cr, self.ns, self.ar, self.br, self.os, self.fs, self.fr, self.free = sems
        left = at.z < dp // 2
        step = jnp.where(left, 1, -1)
        self.inner = (at.z + step, at.s, at.h)
        self.outer = (at.z - step, at.s, at.h)
        self.core = (at.z, 1 - at.s, at.h)
        self.mid = (at.z == dp // 2 - 1) | (at.z == dp // 2)
        self.outermost = (at.z == 0) | (at.z == dp - 1)

    def rows(self, i, side):
        ref, c, a, b = self.pieces[i]
        half = ref.shape[0] // 2
        return ref.at[pl.ds(pl.multiple_of(side * half, half), half)]

    def swap(self, i):
        c = self.pieces[i][1]
        return remote(self.rows(i, 1 - self.at.s), c, self.cs.at[i], self.cr.at[i], self.core)

    def inward(self, i):
        return remote(
            self.rows(i, self.at.s), self.pieces[i][2], self.ns.at[i], self.ar.at[i], self.inner
        )

    def across(self, i):
        return remote(
            self.rows(i, self.at.s), self.pieces[i][3], self.ns.at[i], self.br.at[i], self.inner
        )

    def outward(self, i):
        return remote(
            self.rows(i, self.at.s), self.pieces[i][3], self.os.at[i], self.br.at[i], self.outer
        )

    def last(self, i):
        mine = self.rows(i, self.at.s)
        return remote(mine, mine, self.fs.at[i], self.fr.at[i], self.core)

    def release(self, i):
        self.swap(i).wait_send()
        pl.semaphore_signal(
            self.free.at[i], inc=1, device_id=self.core, device_id_type=MESH
        )

    def finish(self, i):
        pl.semaphore_wait(self.free.at[i], 1)
        self.last(i).start()

    def add(self, i, *refs):
        mine = self.rows(i, self.at.s)
        total = mine[...].astype(F32)
        for ref in refs:
            total = total + ref[...].astype(F32)
        mine[...] = total.astype(mine.dtype)

    def open(self, *which):
        for i in which:
            self.swap(i).start()

    def step(self, ends=(), middles=(), turns=(), backs=()):
        for i in ends:

            @pl.when(self.outermost)
            def _():
                self.swap(i).wait_recv()
                self.add(i, self.pieces[i][1])
                self.release(i)
                pl.when(self.mid)(lambda: self.across(i).start())
                pl.when(jnp.logical_not(self.mid))(lambda: self.inward(i).start())

        for i in middles:

            @pl.when(jnp.logical_not(self.outermost))
            def _():
                self.swap(i).wait_recv()
                self.inward(i).wait_recv()
                self.add(i, self.pieces[i][1], self.pieces[i][2])
                self.release(i)
                pl.when(self.mid)(lambda: self.across(i).start())
                pl.when(jnp.logical_not(self.mid))(lambda: self.inward(i).start())

        for i in turns:

            @pl.when(self.mid)
            def _():
                self.across(i).wait_recv()
                self.across(i).wait_send()
                self.add(i, self.pieces[i][3])
                pl.when(jnp.logical_not(self.outermost))(lambda: self.outward(i).start())
                self.finish(i)

        for i in backs:

            @pl.when(jnp.logical_not(self.mid))
            def _():
                self.outward(i).wait_recv()
                self.inward(i).wait_send()
                mine = self.rows(i, self.at.s)
                mine[...] = self.pieces[i][3][...]
                pl.when(jnp.logical_not(self.outermost))(lambda: self.outward(i).start())
                self.finish(i)

    def close(self, i):
        self.last(i).wait_recv()
        self.last(i).wait_send()
        pl.when(jnp.logical_not(self.outermost))(lambda: self.outward(i).wait_send())


PIECES = ((0, 0, 2), (0, 2, 2), (1, 0, 2), (1, 2, 2), (2, 0, 2), (2, 2, 2), (3, 0, 2), (3, 2, 2), (4, 0, 2), (4, 2, 2), (5, 0, 1), (5, 1, 1), (5, 2, 1), (5, 3, 1))
RING = 8
HOP_AT, CORE_AT = 3, 2
VECTORS = (14, 15, 18, 19)
SCHEDULE = (
    ((0,), (), (), (), ()),
    ((), (), (), (), ()),
    ((1,), (), (), (), ()),
    ((), (0,), (), (), ()),
    ((2, 3), (1,), (0,), (), ()),
    ((), (), (), (), ()),
    ((), (2,), (1,), (), ()),
    ((), (3,), (), (0,), ()),
    ((4,), (), (), (), ()),
    ((), (), (2,), (), (0,)),
    ((5,), (4,), (), (1,), (1,)),
    ((), (), (3,), (), ()),
    ((6, 7), (5,), (4,), (2, 3), (2,)),
    ((), (6,), (), (), (3,)),
    ((8,), (), (5,), (4,), ()),
    ((9,), (7,), (6,), (), (4,)),
    ((10,), (), (), (5,), ()),
    ((11,), (), (), (), ()),
    ((12, 13), (8, 9), (7,), (), (5,)),
    ((), (10,), (8,), (6,), (6,)),
    ((), (11, 12), (9, 10), (7, 8), (7,)),
    ((), (13,), (11, 12), (9, 10), (8, 9)),
    ((), (), (13,), (11, 12), (10,)),
    ((), (), (), (13,), (11, 12, 13)),
)


def kernel(dp, section, slots, *refs):
    refs = list(refs)

    def take(count):
        out = refs[:count]
        del refs[:count]
        return out

    far_x, lens, image = take(3)
    g1, c1, far_qkv, bqv, far_o, bo, g2, c2, far_u, bu, far_d, bd = take(12)
    tg1, tc1, tqkv, tbqv, two, tbo, tg2, tc2, far_tu, tbu, far_td, tbd = take(12)
    far_dy, far_grads, vec = take(3)
    x, wqkv, wo_all, wu, wd, twu, twd, dy, grads, o_all = take(10)
    n1, q, k, v, p, o, n2, hid, slope, r1, z = take(11)
    w2, b2, images = take(3)
    part, got = take(2)
    ring, arb, stats, scored, dn2b, rsb = take(6)
    f_out, f_in, s_out, s_in, a_in = take(5)
    (da,) = take(1)
    dm = dy
    c_in, l_in, b_in, vh_in, vc_in, vl_in, vb_in, late, late_in, late_all = take(10)
    ag_sems, rs_sems, w_sems, h_sems, i_sems, st_sems, sm_sems, v_sems, sp_sems, o_sems, wo_sems = (
        take(2) for _ in range(11)
    )
    ledger_sems = take(9)
    in_sems, out_sems = take(2)
    assert not refs

    at = Place()
    tokens, width = x.shape
    block = tokens // 4
    local = far_o.shape[0]
    heads = local // HEAD_DIM
    sub = 128
    captions = tokens // slots
    own_caps = block // slots
    caps = captions
    scale = HEAD_DIM ** (-0.5)
    low_masks = head_masks(local, BF)
    masks = head_masks(local, F32)
    other_core = (at.z, 1 - at.s, at.h)
    zs = [(lax.rem(at.z + j, dp), at.s, at.h) for j in range(1, dp)]
    z_pair = (at.z + 1 - 2 * lax.rem(at.z, 2), at.s, at.h)
    head_peers = [at.hx, at.hy, at.hd]
    others = []
    for j in range(dp):
        for i in range(section):
            if i or j:
                others.append((lax.rem(at.z + j, dp), lax.rem(at.s + i, section), at.h))
    own = pl.ds(pl.multiple_of(at.h * block, block), block)

    def vector(ref):
        return ref[...].reshape(1, -1)

    arrive = at.greet([at.head(j) for j in head_peers] + others)
    loads = [
        pltpu.make_async_copy(source, target, in_sems.at[i])
        for i, (source, target) in enumerate(
            (
                (tqkv, w2.at[at.h, 0:3]),
                (two, w2.at[at.h, 3]),
                (far_x, x),
                (far_qkv, wqkv),
                (far_o, wo_all.at[at.h]),
                (far_u, wu),
                (far_d, wd),
                (far_tu, twu),
                (far_td, twd),
            )
        )
    ]
    for copy in loads:
        copy.start()
    pic = image[...].astype(F32)
    pic = pic * lax.rsqrt(jnp.mean(pic * pic, -1, keepdims=True) + NORM_EPS) * width ** (-0.5)
    images[at.z, at.s] = pic.astype(BF)
    b2[at.h] = tbqv[...]

    quarter = local // 4
    mine = lax.rem(at.z, 2) * 2 + at.s
    pair = (1 - lax.rem(at.z, 2)) * 2 + at.s

    def shard_part(owner, which):
        return w2.at[owner, :, pl.ds(pl.multiple_of(which * quarter, quarter), quarter)]

    def same_place(ref, sems, i, device):
        return remote(ref, ref, sems[0].at[i], sems[1].at[i], device)

    hop1 = [
        same_place(shard_part(at.h, mine), w_sems, i, at.head(j)) for i, j in enumerate(head_peers)
    ]
    hop_b = [same_place(b2.at[at.h], h_sems, i, at.head(j)) for i, j in enumerate(head_peers)]
    hop2 = [
        same_place(shard_part(j, mine), w_sems, 3 + i, z_pair) for i, j in enumerate(head_peers)
    ]
    hop3 = [
        same_place(shard_part(j, which), w_sems, 6 + 3 * n + i, other_core)
        for i, j in enumerate(head_peers)
        for n, which in enumerate((mine, pair))
    ]
    pics = [
        same_place(images.at[at.z, at.s], i_sems, i, device) for i, device in enumerate(zs)
    ]
    core_pics = same_place(images.at[:, at.s], i_sems, dp - 1, other_core)
    half = pl.ds(pl.multiple_of(at.s * (local // 2), local // 2), local // 2)
    wo_hop = [
        same_place(wo_all.at[at.h, half], wo_sems, i, at.head(j)) for i, j in enumerate(head_peers)
    ]
    wo_core = [
        same_place(wo_all.at[j, half], wo_sems, 3 + i, other_core)
        for i, j in enumerate(head_peers)
    ]
    loads[4].wait()
    arrive()
    for copy in wo_hop + hop_b + pics:
        copy.start()
    for copy in loads[:4]:
        copy.wait()

    scatters = [
        Scatter(at, part, got, rs_sems[0].at[i], rs_sems[1].at[i], block) for i in range(3)
    ]
    gathers = [
        Gather(at, ref, ag_sems[0].at[i], ag_sems[1].at[i], block)
        for i, ref in enumerate((n2, dm, da, dy))
    ]

    def block_of(t):
        return lax.rem(at.hi + lax.div(t, 2), 2) * 2 + lax.rem(at.lo + lax.rem(t, 2), 2)

    def limits(first, count):
        cap = lax.broadcasted_iota(jnp.int32, (captions, count), 0)
        slot = lax.broadcasted_iota(jnp.int32, (captions, count), 1)
        chosen = jnp.where(cap == first + slot // slots, 1.0, 0.0).astype(BF)
        row = jnp.broadcast_to(vector(lens).astype(F32), (8, captions)).astype(BF)
        return dot(row, chosen)[:1]

    def key_bias(first, count):
        slot = lax.broadcasted_iota(jnp.int32, (1, count), 1)
        inside = lax.rem(slot, slots).astype(F32) < limits(first, count)
        return jnp.where(inside, 0.0, NEG)

    row_id = lax.broadcasted_iota(jnp.int32, (sub, sub), 0) // slots
    col_id = lax.broadcasted_iota(jnp.int32, (sub, sub), 1) // slots
    same = row_id == col_id
    mixes = [
        remote(
            o.at[pl.ds(pl.multiple_of(j * block, block), block)],
            o_all.at[at.h],
            o_sems[0].at[i],
            o_sems[1].at[i],
            at.head(j),
        )
        for i, j in enumerate((at.hd, at.hy, at.hx))
    ]

    def attend(t, carry):
        blk = block_of(3 - t)
        rows = pl.ds(pl.multiple_of(blk * block, block), block)
        hat, _ = norm_stats(x[rows].astype(F32))
        normed = (hat * vector(g1) + vector(c1)).astype(BF)
        n1[rows] = normed
        query = (dot_nt(normed, wqkv[0]) + bqv[0:1]).astype(BF)
        keys = dot_nt(normed, wqkv[1]).astype(BF)
        values = (dot_nt(normed, wqkv[2]) + bqv[1:2]).astype(BF)
        q[rows] = query
        k[rows] = keys
        v[rows] = values
        mixed = []
        for m in range(block // sub):
            cut = slice(m * sub, (m + 1) * sub)
            index = blk * (block // sub) + m
            bias = jnp.where(same, key_bias(index * (sub // slots), sub), NEG)
            total = jnp.zeros((sub, local), F32)
            for i in range(heads):
                scores = dot_nt(query[cut] * low_masks[i], keys[cut]) * scale + bias
                scores = jnp.exp(scores - jnp.max(scores, -1, keepdims=True))
                probs = (scores * (1.0 / jnp.sum(scores, -1, keepdims=True))).astype(BF)
                p[index, i] = probs
                total = total + dot(probs, values[cut]) * masks[i]
            mixed.append(total.astype(BF))
        mixed = jnp.concatenate(mixed, 0)
        o[rows] = mixed
        for i in range(3):
            pl.when(t == i)(mixes[i].start)

        @pl.when(t == HOP_AT)
        def _():
            for copy in hop1:
                copy.start()

        @pl.when(t == CORE_AT)
        def _():
            for copy in wo_hop:
                copy.wait_recv()
            for copy in wo_core:
                copy.start()

        @pl.when(t == 3)
        def _():
            o_all[at.h] = mixed

        return carry

    lax.fori_loop(0, 4, attend, 0)
    for copy in mixes + wo_core:
        copy.wait_recv()
    resid = x[own].astype(F32) + vector(bo)
    for j in range(4):
        resid = resid + dot(o_all[j], wo_all[j])
    r1[...] = resid
    hat, _ = norm_stats(resid)
    n2[own] = (hat * vector(g2) + vector(c2)).astype(BF)

    def waits(t, gather):
        @pl.when(t == 1)
        def _():
            gather.forward()
            gather.wait_x()

        pl.when(t == 2)(gather.wait_y)
        pl.when(t == 3)(gather.wait_d)

    def sends(t, scatter):
        pl.when(t == 1)(scatter.send_x)
        pl.when(t == 2)(scatter.send_y)
        pl.when(t == 3)(scatter.send_d)

    gathers[0].start()
    for i in range(3):
        hop1[i].wait_recv()
        hop2[i].start()
    for copy in loads[5:7]:
        copy.wait()

    def feed(t, carry):
        waits(t, gathers[0])
        blk = block_of(t)
        rows = pl.ds(pl.multiple_of(blk * block, block), block)
        value, steep = gelu_pair(dot(n2[rows], wu[...]) + vector(bu))
        value = value.astype(BF)
        hid[rows] = value
        slope[rows] = steep.astype(BF)
        part[blk] = dot(value, wd[...]).astype(BF)
        sends(t, scatters[0])
        return carry

    lax.fori_loop(0, 4, feed, 0)
    for i in range(3):
        hop2[i].wait_recv()
        hop3[2 * i].start()
        hop3[2 * i + 1].start()
    for copy in pics:
        copy.wait_recv()
    core_pics.start()
    scatters[0].second()
    scatters[0].wait()
    zv = r1[...] + scatters[0].total() + vector(bd)
    scatters[0].finish()
    z[...] = zv
    for copy in hop_b + hop3 + [core_pics]:
        copy.wait_recv()

    per = heads * own_caps

    def stack(values):
        return jnp.concatenate([values * low_masks[i] for i in range(heads)], 0)

    def pick_heads(values):
        total = values[:own_caps] * masks[0]
        for i in range(1, heads):
            total = total + values[i * own_caps : (i + 1) * own_caps] * masks[i]
        return total

    first_cap = at.h * own_caps
    last_slot = limits(first_cap, block) - 1.0
    slot_row = lax.broadcasted_iota(jnp.int32, (own_caps, block), 1)
    cap_row = lax.broadcasted_iota(jnp.int32, (own_caps, block), 0)
    picked = (slot_row // slots == cap_row) & (lax.rem(slot_row, slots).astype(F32) == last_slot)
    pick = jnp.where(picked, 1.0, 0.0).astype(BF)
    cap_of = lax.broadcasted_iota(jnp.int32, (block, captions), 0)
    cap_at = lax.broadcasted_iota(jnp.int32, (block, captions), 1)
    length_col = jnp.sum(
        jnp.where(cap_at == first_cap + cap_of // slots, vector(lens).astype(F32), 0.0),
        1,
        keepdims=True,
    )
    slot_col = lax.rem(lax.broadcasted_iota(jnp.int32, (block, 1), 0), slots).astype(F32)
    pcol = jnp.where(slot_col == length_col - 1.0, 1.0, 0.0)

    hat1, rstd1 = norm_stats(zv)
    normed = (hat1 * vector(tg1) + vector(tc1)).astype(BF)
    pooled_low = dot(pick, normed).astype(BF)
    a_in[at.h, 0] = pooled_low
    z_pool = jnp.sum((zv * pcol).reshape(own_caps, slots, width), 1)
    us = []
    for j in range(4):
        query = (dot_nt(pooled_low, w2[j, 0]) + b2[j, 0:1]).astype(BF)
        s_out[j, 0] = query
        us.append(dot(stack(query), w2[j, 1]).astype(BF))
    u_all = jnp.concatenate(us, 0)
    rows_n = 4 * per
    row_cap = lax.rem(lax.broadcasted_iota(jnp.int32, (rows_n, block), 0), own_caps)
    col_cap = lax.broadcasted_iota(jnp.int32, (rows_n, block), 1) // slots
    bias = jnp.where(row_cap == col_cap, key_bias(first_cap, block), NEG)
    scores = dot_nt(u_all, normed) * scale + bias
    scores = jnp.exp(scores - jnp.max(scores, -1, keepdims=True))
    probs = scores * (1.0 / jnp.sum(scores, -1, keepdims=True))
    probs_low = probs.astype(BF)
    mix = dot(probs_low, normed).astype(BF)
    attended = jnp.zeros((own_caps, width), F32)
    for j in range(4):
        piece = mix[j * per : (j + 1) * per]
        f_out[j, 0] = piece
        out = (pick_heads(dot_nt(piece, w2[j, 2])) + b2[j, 1:2]).astype(BF)
        s_out[j, 3] = out
        attended = attended + dot(out, w2[j, 3])
    ring[at.h] = z_pool + attended + vector(tbo)

    def small(ref, i, j, target=None):
        return remote(
            ref,
            ref if target is None else target,
            sm_sems[0].at[i],
            sm_sems[1].at[i],
            at.head(j),
        )

    for copy in loads[7:]:
        copy.wait()
    rings = [small(ring.at[at.h], i, j) for i, j in enumerate(head_peers)]
    early = [
        small(f_out.at[j, 0], 18 + i, j, f_in.at[at.h, 0]) for i, j in enumerate(head_peers)
    ]
    for copy in rings + early:
        copy.start()
    for copy in rings:
        copy.wait_recv()

    r1_all = ring[...].reshape(caps, width)
    hat2_all, _ = norm_stats(r1_all)
    n2_top = (hat2_all * vector(tg2) + vector(tc2)).astype(BF)
    value, steep = gelu_pair(dot(n2_top, twu[...]) + vector(tbu))
    value = value.astype(BF)
    arb[at.h] = dot(value, twd[...]).astype(BF)
    sums = [small(arb.at[at.h], 3 + i, j) for i, j in enumerate(head_peers)]
    for copy in sums:
        copy.start()
    for copy in sums:
        copy.wait_recv()
    pooled = r1_all + vector(tbd)
    for j in range(4):
        pooled = pooled + arb[j].astype(F32)
    unit_r = lax.rsqrt(jnp.mean(pooled * pooled, -1, keepdims=True) + NORM_EPS)
    text = (pooled * unit_r * width ** (-0.5)).astype(BF)

    everyone = dp * section * caps
    batch = min(dp, 4)
    wide = batch * section * caps
    lanes = wide // 4
    place = at.z * section + at.s

    def chunk_images(n):
        return images[n * batch : (n + 1) * batch].reshape(wide, width)

    def own_columns(n):
        col = lax.broadcasted_iota(jnp.int32, (caps, wide), 1) + n * wide
        row = lax.broadcasted_iota(jnp.int32, (caps, wide), 0) + place * caps
        return col == row

    chunks = [slice(n * wide, (n + 1) * wide) for n in range(dp // batch)]
    row_max = diagonal = None
    for n, cols in enumerate(chunks):
        logits = LOGIT_SCALE * dot_nt(text, chunk_images(n))
        scored[:, cols] = logits
        found = jnp.max(logits, 1, keepdims=True)
        row_max = found if row_max is None else jnp.maximum(row_max, found)
        found = jnp.sum(jnp.where(own_columns(n), logits, 0.0), 1, keepdims=True)
        diagonal = found if diagonal is None else diagonal + found
        col_max = jnp.max(logits, 0, keepdims=True)
        col_sum = jnp.sum(jnp.exp(logits - col_max), 0, keepdims=True)
        for i in range(4):
            stats[place, n, i : i + 1] = col_max[:, i * lanes : (i + 1) * lanes]
            stats[place, n, 4 + i : 5 + i] = col_sum[:, i * lanes : (i + 1) * lanes]
    tells = [
        same_place(stats.at[place], st_sems, i, device) for i, device in enumerate(others)
    ]
    for copy in tells:
        copy.start()
    row_sum = None
    for n, cols in enumerate(chunks):
        found = jnp.sum(jnp.exp(scored[:, cols] - row_max), 1, keepdims=True)
        row_sum = found if row_sum is None else row_sum + found
    row_lse = row_max + jnp.log(row_sum)

    def pull(n, cols, lse):
        steep = jnp.exp(scored[:, cols] - lse) - jnp.where(own_columns(n), 1.0, 0.0)
        return dot((steep * (0.5 / everyone)).astype(BF), chunk_images(n))

    text_grad = None
    for n, cols in enumerate(chunks):
        term = pull(n, cols, row_lse)
        text_grad = term if text_grad is None else text_grad + term
    lost = jnp.sum(row_lse - 2.0 * diagonal, 0, keepdims=True)
    for copy in tells:
        copy.wait_recv()
    for n, cols in enumerate(chunks):
        told = stats[:, n]
        top = jnp.max(told[:, 0:4], 0)
        total = jnp.sum(told[:, 4:8] * jnp.exp(told[:, 0:4] - top[None]), 0)
        lse = top + jnp.log(total)
        col_lse = jnp.concatenate([lse[i : i + 1] for i in range(4)], 1)
        text_grad = text_grad + pull(n, cols, col_lse)
        found = jnp.sum(jnp.where(own_columns(n), col_lse, 0.0), 1, keepdims=True)
        lost = lost + jnp.sum(found, 0, keepdims=True)
    text_grad = LOGIT_SCALE * text_grad
    inner = jnp.mean(pooled * text_grad, -1, keepdims=True)
    d_pool = (unit_r * width ** (-0.5)) * (text_grad - pooled * (unit_r * unit_r * inner))
    z[:caps] = d_pool

    pieces = []
    taken = 0
    for i, (a, first, many) in enumerate(PIECES):
        first, many = first * width // 4, many * width // 4
        here = pl.ds(taken, many // 2)
        lane = pl.ds(0, many // 2)
        pieces.append(
            (grads.at[a, pl.ds(first, many)], c_in.at[here], l_in.at[i % RING, lane], b_in.at[here])
        )
        taken += many // 2
    count = len(pieces)
    pieces.append((vec, vc_in, vl_in, vb_in))
    ledger = Ledger(at, dp, pieces, ledger_sems)

    def flush(i):
        a, first, many = PIECES[i]
        rows = pl.ds(first * width // 4, many * width // 4)
        return pltpu.make_async_copy(grads.at[a, rows], far_grads.at[a, rows], out_sems.at[i])

    def slot(number):
        ends, middles, turns, backs, done = SCHEDULE[number]
        if number in VECTORS:
            chosen = [()] * 4
            chosen[VECTORS.index(number)] = (count,)
            ledger.step(*chosen)
        ledger.step(ends, middles, turns, backs)
        for i in done:
            ledger.close(i)
            flush(i).start()

    low = d_pool.astype(BF)
    du_top = (dot_nt(low, twd[...]) * steep).astype(BF)
    dn2b[...] = dot_nt(du_top, twu[...]).astype(BF)
    own_rows = pl.ds(pl.multiple_of(at.h * own_caps, own_caps), own_caps)
    backs = []
    for i, j in enumerate(head_peers):
        there = pl.ds(pl.multiple_of(j * own_caps, own_caps), own_caps)
        backs.append(small(dn2b.at[there], 6 + i, j, rsb.at[at.h]))
    for copy in backs:
        copy.start()
    grads[0] = dot_tn(value, low).astype(BF)
    ledger.open(0, 1)
    grads[1] = dot_tn(n2_top, du_top).astype(BF)
    ledger.open(2, 3)
    vec[...] = jnp.zeros_like(vec)
    vec[22:23, 0:128] = jnp.broadcast_to(lost, (1, 128))
    vec[17:18] = rows_sum(du_top.astype(F32))
    rsb[at.h] = dn2b[own_rows]
    slot(0)
    for copy in backs:
        copy.wait_recv()
    dn2 = rsb[0].astype(F32)
    for j in range(1, 4):
        dn2 = dn2 + rsb[j].astype(F32)
    hat2, rstd2 = norm_stats(ring[at.h])
    dpool_own = z[own_rows]
    dr1_top = dpool_own + norm_back(dn2, hat2, rstd2, vector(tg2))
    vec[8:9] = rows_sum(dr1_top)
    vec[9:10] = rows_sum(dn2 * hat2)
    vec[10:11] = rows_sum(dn2)
    vec[11:12] = rows_sum(dpool_own)

    slot(1)

    da_top = dr1_top.astype(BF)
    a_in[at.h, 1] = da_top
    ws = []
    for j in range(4):
        d_out = dot_nt(da_top, w2[j, 3]).astype(BF)
        s_out[j, 2] = d_out
        ws.append(dot(stack(d_out), w2[j, 2]).astype(BF))
    w_all = jnp.concatenate(ws, 0)
    d_probs = dot_nt(w_all, normed)
    d_scores = probs * (d_probs - jnp.sum(probs * d_probs, -1, keepdims=True))
    scores_low = d_scores.astype(BF)
    g_rows = (dot(scores_low, normed) * scale).astype(BF)
    slot(2)
    d_pooled_low = jnp.zeros((own_caps, width), F32)
    for j in range(4):
        piece = g_rows[j * per : (j + 1) * per]
        f_out[j, 1] = piece
        d_query = pick_heads(dot_nt(piece, w2[j, 1])).astype(BF)
        s_out[j, 1] = d_query
        d_pooled_low = d_pooled_low + dot(d_query, w2[j, 0])
    facts = []
    for i, j in enumerate(head_peers):
        facts.append(small(f_out.at[j, 1], 9 + i, j, f_in.at[at.h, 1]))
        facts.append(small(s_out.at[j], 12 + i, j, s_in.at[at.h]))
        facts.append(small(a_in.at[at.h], 15 + i, j))
    dn = dot_tn(scores_low, u_all) * scale + dot_tn(probs_low, w_all)

    def widen(values):
        values = jnp.broadcast_to(values[:, None, :], (own_caps, slots, width))
        return values.reshape(block, width)

    dn = dn + pcol * widen(d_pooled_low)
    dz = norm_back(dn, hat1, rstd1, vector(tg1)) + pcol * widen(dr1_top)
    dm[own] = dz.astype(BF)
    gathers[1].start()
    for copy in facts:
        copy.start()
    z[...] = dz
    vec[6:7] = rows_sum(dn * hat1)
    vec[7:8] = rows_sum(dn)
    vec[5:6] = rows_sum(dz)

    f_in[at.h] = f_out[at.h]
    s_in[at.h] = s_out[at.h]
    slot(3)
    scatter_a = scatters[1]

    def feed_back(t, carry):
        waits(t, gathers[1])
        blk = block_of(t)
        rows = pl.ds(pl.multiple_of(blk * block, block), block)
        grad = (dot_nt(dm[rows], wd[...]) * slope[rows].astype(F32)).astype(BF)
        slope[rows] = grad
        part[blk] = dot_nt(grad, wu[...]).astype(BF)
        sends(t, scatter_a)
        for i in range(3):
            pl.when(t == i)(lambda: slot(4 + i))
        return carry

    lax.fori_loop(0, 4, feed_back, 0)
    gathers[1].finish()
    for copy in early + facts:
        copy.wait_recv()
    pooled_all = jnp.concatenate([a_in[j, 0] for j in range(4)], 0)
    da_all = jnp.concatenate([a_in[j, 1] for j in range(4)], 0)
    dq_all = jnp.concatenate([s_in[j, 1] for j in range(4)], 0)
    do_all = jnp.concatenate([s_in[j, 2] for j in range(4)], 0)
    out_all = jnp.concatenate([s_in[j, 3] for j in range(4)], 0)
    grads[2, 0:local] = dot_tn(dq_all, pooled_all).astype(BF)
    grads[2, local : 2 * local] = dot_tn(
        jnp.concatenate([stack(s_in[j, 0]) for j in range(4)], 0),
        jnp.concatenate([f_in[j, 1] for j in range(4)], 0),
    ).astype(BF)
    grads[2, 2 * local : 3 * local] = dot_tn(
        jnp.concatenate([stack(s_in[j, 2]) for j in range(4)], 0),
        jnp.concatenate([f_in[j, 0] for j in range(4)], 0),
    ).astype(BF)
    grads[2, 3 * local :] = dot_tn(out_all, da_all).astype(BF)
    ledger.open(4, 5)
    vec[20:21, 0:local] = rows_sum(dq_all.astype(F32))
    vec[21:22, 0:local] = rows_sum(do_all.astype(F32))
    slot(7)
    grads[3] = dot_tn(hid[...], dm[...]).astype(BF)
    ledger.open(6, 7)
    slot(8)
    grads[4] = dot_tn(n2[...], slope[...]).astype(BF)
    ledger.open(8, 9)
    slot(9)
    scatter_a.second()
    vec[16:17] = rows_sum(slope[...].astype(F32))
    slot(10)
    scatter_a.wait()
    dn2 = scatter_a.total()
    scatter_a.finish()
    hat, rstd = norm_stats(r1[...])
    back = z[...] + norm_back(dn2, hat, rstd, vector(g2))
    r1[...] = back
    da[own] = back.astype(BF)
    gathers[2].start()
    vec[2:3] = rows_sum(back)
    vec[3:4] = rows_sum(dn2 * hat)
    vec[4:5] = rows_sum(dn2)

    vh_in[at.h] = vec[0:16]
    tops = [same_place(vh_in.at[at.h], v_sems, i, at.head(j)) for i, j in enumerate(head_peers)]
    for copy in tops:
        copy.start()
    slot(11)
    scatter_b = scatters[2]

    def attend_back(t, carry):
        waits(t, gathers[2])
        blk = block_of(t)
        rows = pl.ds(pl.multiple_of(blk * block, block), block)
        d_out = dot_nt(da[rows], wo_all[at.h]).astype(BF)
        query, keys, values = q[rows], k[rows], v[rows]
        parts = [[], [], []]
        for m in range(block // sub):
            cut = slice(m * sub, (m + 1) * sub)
            index = blk * (block // sub) + m
            dq = jnp.zeros((sub, local), F32)
            dk = jnp.zeros((sub, local), F32)
            dv = jnp.zeros((sub, local), F32)
            for i in range(heads):
                probs_low = p[index, i]
                probs = probs_low.astype(F32)
                d_probs = dot_nt(d_out[cut] * low_masks[i], values[cut])
                d_scores = probs * (d_probs - jnp.sum(probs * d_probs, -1, keepdims=True))
                d_scores = d_scores.astype(BF)
                dq = dq + dot(d_scores, keys[cut]) * masks[i]
                dk = dk + dot_tn(d_scores, query[cut]) * masks[i]
                dv = dv + dot_tn(probs_low, d_out[cut]) * masks[i]
            parts[0].append((dq * scale).astype(BF))
            parts[1].append((dk * scale).astype(BF))
            parts[2].append(dv.astype(BF))
        total = None
        for i in range(3):
            whole = jnp.concatenate(parts[i], 0)
            (q, k, v)[i][rows] = whole
            term = dot(whole, wqkv[i])
            total = term if total is None else total + term
        part[blk] = total.astype(BF)
        sends(t, scatter_b)
        for i in range(3):
            pl.when(t == i)(lambda: slot(12 + i))

        @pl.when(t == 1)
        def _():
            for copy in tops:
                copy.wait_recv()
            vec[0:16] = vh_in[0] + vh_in[1] + vh_in[2] + vh_in[3]
            ledger.open(count)

        return carry

    lax.fori_loop(0, 4, attend_back, 0)
    grads[5, 0:local] = dot_tn(q[...], n1[...]).astype(BF)
    ledger.open(10)
    grads[5, local : 2 * local] = dot_tn(k[...], n1[...]).astype(BF)
    ledger.open(11)
    slot(15)
    grads[5, 2 * local : 3 * local] = dot_tn(v[...], n1[...]).astype(BF)
    ledger.open(12)
    slot(16)
    grads[5, 3 * local :] = dot_tn(o[...], da[...]).astype(BF)
    ledger.open(13)
    slot(17)
    scatter_b.second()
    late[...] = jnp.zeros_like(late)
    late[2:3, 0:local] = rows_sum(q[...].astype(F32))
    late[3:4, 0:local] = rows_sum(v[...].astype(F32))
    slot(18)
    scatter_b.wait()
    dn1 = scatter_b.total()
    hat, rstd = norm_stats(x[own].astype(F32))
    dy[own] = (r1[...] + norm_back(dn1, hat, rstd, vector(g1))).astype(BF)
    gathers[3].start()
    late[0:1] = rows_sum(dn1 * hat)
    late[1:2] = rows_sum(dn1)

    late_in[at.h] = late[...]
    lates = [
        same_place(late_in.at[at.h], v_sems, 3 + i, at.head(j)) for i, j in enumerate(head_peers)
    ]
    for copy in lates:
        copy.start()
    slot(19)
    for copy in lates:
        copy.wait_recv()
    late_all[place, 0:2] = late_in[0, 0:2] + late_in[1, 0:2] + late_in[2, 0:2] + late_in[3, 0:2]
    late_all[place, 2:8] = late[2:8]
    spreads = [
        same_place(late_all.at[place], sp_sems, i, device) for i, device in enumerate(others)
    ]
    for copy in spreads:
        copy.start()
    slot(20)
    gathers[3].forward()
    slot(21)
    gathers[3].wait_x()
    gathers[3].wait_y()
    slot(22)
    gathers[3].wait_d()
    spill = pltpu.make_async_copy(dy, far_dy, out_sems.at[count])
    spill.start()
    slot(23)
    for copy in spreads:
        copy.wait_recv()
    total = late_all[0]
    for i in range(1, dp * section):
        total = total + late_all[i]
    ledger.close(count)
    vec[0:2] = total[0:2]
    vec[18:20] = total[2:4]
    for i in range(count):
        flush(i).wait()
    spill.wait()
    scatter_b.finish()
    for i in (0, 2, 3):
        gathers[i].finish()
    for copy in hop1 + hop_b + hop2 + hop3 + pics + [core_pics] + wo_hop + wo_core + mixes:
        copy.wait_send()
    for copy in rings + early + sums + tells + backs + facts + tops + lates + spreads:
        copy.wait_send()


def run_kernel(dp, section, slots, x, lens, image, base, top):
    tokens, width = x.shape
    local = base[4].shape[0]
    ff = base[8].shape[1]
    block = tokens // 4
    heads = local // HEAD_DIM
    captions = image.shape[0]
    own_caps = captions // 4
    per = heads * own_caps
    everyone = dp * section * captions
    batch = min(dp, 4)
    others = dp * section - 1
    vmem = pl.BlockSpec(memory_space=pltpu.VMEM)
    hbm = pl.BlockSpec(memory_space=pl.ANY)
    big = (0, 5, 7, 11, 13, 17, 19, 23, 25)
    shape = jax.ShapeDtypeStruct
    outs = [
        shape((tokens, width), BF),
        shape((6, width, width), BF),
        shape((32, width), F32),
    ]
    assert ff == width and 4 * local == width
    sems = pltpu.SemaphoreType.DMA
    ram = pltpu.VMEM
    count = len(PIECES)
    rows = sum(piece[2] for piece in PIECES) * width // 8
    scratch = [
        ram((tokens, width), BF),
        ram((3, local, width), BF),
        ram((4, local, width), BF),
        ram((width, ff), BF),
        ram((ff, width), BF),
        ram((width, ff), BF),
        ram((ff, width), BF),
        ram((tokens, width), BF),
        ram((6, width, width), BF),
        ram((4, block, local), BF),
        ram((tokens, width), BF),
        ram((tokens, local), BF),
        ram((tokens, local), BF),
        ram((tokens, local), BF),
        ram((tokens // 128, heads, 128, 128), BF),
        ram((tokens, local), BF),
        ram((tokens, width), BF),
        ram((tokens, ff), BF),
        ram((tokens, ff), BF),
        ram((block, width), F32),
        ram((block, width), F32),
        ram((4, 4, local, width), BF),
        ram((4, 2, local), F32),
        ram((dp, section, captions, width), BF),
        ram((4, block, width), BF),
        ram((6, block // 2, width), BF),
        ram((4, own_caps, width), F32),
        ram((4, captions, width), BF),
        ram((dp * section, dp // batch, 8, everyone // (dp // batch) // 4), F32),
        ram((captions, everyone), F32),
        ram((captions, width), BF),
        ram((4, own_caps, width), BF),
        ram((4, 2, per, width), BF),
        ram((4, 2, per, width), BF),
        ram((4, 4, own_caps, local), BF),
        ram((4, 4, own_caps, local), BF),
        ram((4, 2, own_caps, width), BF),
        ram((tokens, width), BF),
        ram((rows, width), BF),
        ram((RING, width // 4, width), BF),
        ram((rows, width), BF),
        ram((4, 16, width), F32),
        ram((16, width), F32),
        ram((16, width), F32),
        ram((16, width), F32),
        ram((8, width), F32),
        ram((4, 8, width), F32),
        ram((dp * section, 8, width), F32),
    ]
    for many in ((4, 6), (3, 6), (12,), (3,), (dp,), (others,), (21,), (6,), (others,), (3,), (6,)):
        scratch += [sems(many), sems(many)]
    scratch += [sems((count + 1,))] * 8 + [pltpu.SemaphoreType.REGULAR((count + 1,))]
    scratch += [sems((9,)), sems((count + 1,))]
    return pl.pallas_call(
        functools.partial(kernel, dp, section, slots),
        out_shape=outs,
        in_specs=[hbm if i in big else vmem for i in range(27)],
        out_specs=[hbm, hbm, vmem],
        scratch_shapes=scratch,
        compiler_params=pltpu.CompilerParams(
            collective_id=0, has_side_effects=True, vmem_limit_bytes=VMEM_LIMIT
        ),
        cost_estimate=pl.CostEstimate(
            flops=14 * 10**9, bytes_accessed=40 * 10**6, transcendentals=4 * 10**6
        ),
    )(x, lens, image, *base, *top)


def widen_kernel(local, scale, far_dy, far_grads, vec, *refs):
    loss, text, base, top = refs[0], refs[1], refs[2:14], refs[14:26]
    near_dy, near_grads, wide_text, wide_grads, dy_in, dy_out, g_in, g_out = refs[26:]
    rows = wide_text.shape[0] // 4
    width = wide_text.shape[1]
    incoming = []
    for a in (3, 4, 5, 0, 1, 2):
        for n in range(4):
            span = pl.ds(n * local, local)
            incoming.append(
                pltpu.make_async_copy(
                    far_grads.at[a, span], near_grads.at[a, span], g_in.at[4 * a + n]
                )
            )
    texts = []
    for n in range(4):
        span = pl.ds(n * rows, rows)
        texts.append(pltpu.make_async_copy(far_dy.at[span], near_dy.at[span], dy_in.at[n]))
    for copy in incoming + texts:
        copy.start()
    loss[...] = vec[22:23, 0:1] * scale
    for layer, row, bu, bqv in ((base, 0, 16, 18), (top, 6, 17, 20)):
        layer[0][...] = vec[row]
        layer[1][...] = vec[row + 1]
        layer[3][...] = vec[bqv : bqv + 2, 0:local]
        layer[5][...] = vec[row + 2]
        layer[6][...] = vec[row + 3]
        layer[7][...] = vec[row + 4]
        layer[9][...] = vec[bu]
        layer[11][...] = vec[row + 5]
    outgoing = []
    for i, copy in enumerate(incoming):
        a, n = (3, 4, 5, 0, 1, 2)[i // 4], i % 4
        layer = base if a >= 3 else top
        span = pl.ds(n * local, local)
        copy.wait()
        wide_grads[a, span] = near_grads[a, span].astype(F32)
        if a % 3 == 2:
            target = layer[2].at[n] if n < 3 else layer[4]
        else:
            target = layer[10 if a % 3 == 0 else 8].at[span]
        outgoing.append(
            pltpu.make_async_copy(wide_grads.at[a, span], target, g_out.at[4 * a + n])
        )
        outgoing[-1].start()
    for n, copy in enumerate(texts):
        span = pl.ds(n * rows, rows)
        copy.wait()
        wide_text[span] = near_dy[span].astype(F32)
        outgoing.append(pltpu.make_async_copy(wide_text.at[span], text.at[span], dy_out.at[n]))
        outgoing[-1].start()
    for copy in outgoing:
        copy.wait()


def widen(local, scale, dy, grads, vec):
    tokens, width = dy.shape
    vmem = pl.BlockSpec(memory_space=pltpu.VMEM)
    hbm = pl.BlockSpec(memory_space=pl.ANY)
    shape = jax.ShapeDtypeStruct
    line = (shape((width,), F32), vmem)
    square = (shape((width, width), F32), hbm)
    layer = [
        line,
        line,
        (shape((3, local, width), F32), hbm),
        (shape((2, local), F32), vmem),
        (shape((local, width), F32), hbm),
        line,
        line,
        line,
        square,
        line,
        square,
        line,
    ]
    outs = [(shape((1, 1), F32), vmem), (shape((tokens, width), F32), hbm)] + layer * 2
    sems = pltpu.SemaphoreType.DMA
    return pl.pallas_call(
        functools.partial(widen_kernel, local, scale),
        out_shape=[item[0] for item in outs],
        in_specs=[hbm, hbm, vmem],
        out_specs=[item[1] for item in outs],
        scratch_shapes=[
            pltpu.VMEM((tokens, width), BF),
            pltpu.VMEM((6, width, width), BF),
            pltpu.VMEM((tokens, width), F32),
            pltpu.VMEM((6, width, width), F32),
            sems((4,)),
            sems((4,)),
            sems((24,)),
            sems((24,)),
        ],
        compiler_params=pltpu.CompilerParams(vmem_limit_bytes=VMEM_LIMIT),
        cost_estimate=pl.CostEstimate(
            flops=10**7, bytes_accessed=26 * 10**6, transcendentals=0
        ),
    )(dy, grads, vec)


def on_device(dp, section, text_in, lengths, image_embed, *params):
    base, top = params[:12], params[12:]
    captions, slots, width = text_in.shape
    tokens = captions * slots
    local = base[4].shape[0]

    def layout(layer):
        return layer[:2] + (layer[2].transpose(1, 2, 0),) + layer[3:]

    dy, grads, vec = run_kernel(
        dp,
        section,
        slots,
        text_in.reshape(tokens, width),
        lengths,
        image_embed,
        layout(base),
        layout(top),
    )
    outs = list(widen(local, 0.5 / (dp * section * captions), dy, grads, vec))
    for i in (4, 16):
        outs[i] = outs[i].transpose(2, 0, 1)
    return (outs[0][0, 0], outs[1].reshape(captions, slots, width)) + tuple(outs[2:])


def solution(mesh):
    layer_in = (
        P(),
        P(),
        P(None, None, "head"),
        P(None, "head"),
        P("head", None),
        P(),
        P(),
        P(),
        P(None, "head"),
        P("head"),
        P("head", None),
        P(),
    )
    rows = P(("dp", "section"), None, None)
    return jax.shard_map(
        functools.partial(on_device, mesh.shape["dp"], mesh.shape["section"]),
        mesh=mesh,
        in_specs=(rows, P(("dp", "section")), P(("dp", "section"), None)) + layer_in * 2,
        out_specs=(P(), rows) + layer_in * 2,
        check_vma=False,
    )
```

```python
import functools

import jax
import jax.numpy as jnp
from jax import lax
from jax.experimental import pallas as pl
from jax.experimental.pallas import tpu as pltpu
from jax.sharding import PartitionSpec as P

HEAD_DIM = 64
NORM_EPS = 1e-06
LOGIT_SCALE = 50.0
NEG = -1e30
BF = jnp.bfloat16
F32 = jnp.float32
MESH = pl.DeviceIdType.MESH
VMEM_LIMIT = 63 * 2**20


def dot(a, b):
    return lax.dot_general(a, b, (((1,), (0,)), ((), ())), preferred_element_type=F32)


def dot_nt(a, b):
    return lax.dot_general(a, b, (((1,), (1,)), ((), ())), preferred_element_type=F32)


def dot_tn(a, b):
    return lax.dot_general(a, b, (((0,), (0,)), ((), ())), preferred_element_type=F32)


def norm_stats(values):
    center = jnp.mean(values, -1, keepdims=True)
    shifted = values - center
    spread = jnp.mean(shifted * shifted, -1, keepdims=True)
    rstd = lax.rsqrt(spread + NORM_EPS)
    return shifted * rstd, rstd


def norm_back(grad, hat, rstd, gain):
    scaled = grad * gain
    m1 = jnp.mean(scaled, -1, keepdims=True)
    m2 = jnp.mean(scaled * hat, -1, keepdims=True)
    return rstd * (scaled - m1 - hat * m2)


def rows_sum(values):
    return jnp.sum(values, 0, keepdims=True)


def gelu_pair(u):
    c = 0.7978845608028654
    u2 = u * u
    t = jnp.tanh(c * u * (1.0 + 0.044715 * u2))
    half = 0.5 * (1.0 + t)
    value = u * half
    slope = half + 0.5 * u * (1.0 - t * t) * (c * (1.0 + 3.0 * 0.044715 * u2))
    return value, slope


def head_masks(width, kind):
    lane = lax.broadcasted_iota(jnp.int32, (1, width), 1)
    return [
        jnp.where((lane >= i * HEAD_DIM) & (lane < (i + 1) * HEAD_DIM), 1.0, 0.0).astype(kind)
        for i in range(width // HEAD_DIM)
    ]


class Place:
    def __init__(self):
        self.z = lax.axis_index("dp")
        self.s = lax.axis_index("section")
        h = lax.axis_index("head")
        self.h = h
        self.hi = lax.div(h, 2)
        self.lo = lax.rem(h, 2)
        self.hx = self.block(0, 1)
        self.hy = self.block(1, 0)
        self.hd = self.block(1, 1)

    def block(self, flip_hi, flip_lo):
        return lax.rem(self.hi + flip_hi, 2) * 2 + lax.rem(self.lo + flip_lo, 2)

    def head(self, other):
        return (self.z, self.s, other)

    def greet(self, devices):
        barrier = pltpu.get_barrier_semaphore()
        for device in devices:
            pl.semaphore_signal(barrier, inc=1, device_id=device, device_id_type=MESH)
        return lambda: pl.semaphore_wait(barrier, len(devices))


def remote(src, dst, send_sem, recv_sem, device):
    return pltpu.make_async_remote_copy(
        src_ref=src,
        dst_ref=dst,
        send_sem=send_sem,
        recv_sem=recv_sem,
        device_id=device,
        device_id_type=MESH,
    )


class Gather:
    def __init__(self, at, ref, send, recv, block):
        half = block // 2

        def rows(owner, part):
            return ref.at[pl.ds(pl.multiple_of(owner * block + part * half, half), half)]

        def copy(i, owner, part, target):
            piece = rows(owner, part)
            return remote(piece, piece, send.at[i], recv.at[i], at.head(target))

        self.c = [
            copy(0, at.h, 0, at.hx),
            copy(1, at.h, 1, at.hy),
            copy(2, at.h, 1, at.hx),
            copy(3, at.h, 0, at.hy),
            copy(4, at.hx, 0, at.hy),
            copy(5, at.hy, 1, at.hx),
        ]

    def start(self):
        for i in range(4):
            self.c[i].start()

    def forward(self):
        self.c[0].wait_recv()
        self.c[4].start()
        self.c[1].wait_recv()
        self.c[5].start()

    def wait_x(self):
        self.c[2].wait_recv()

    def wait_y(self):
        self.c[3].wait_recv()

    def wait_d(self):
        self.c[4].wait_recv()
        self.c[5].wait_recv()

    def finish(self):
        for copy in self.c:
            copy.wait_send()


class Scatter:
    def __init__(self, at, part, got, send, recv, block):
        half = block // 2
        self.at, self.part, self.got, self.half = at, part, got, half

        def piece(owner, side):
            return part.at[owner, pl.ds(side * half, half)]

        def copy(i, owner, side, target):
            return remote(piece(owner, side), got.at[i], send.at[i], recv.at[i], at.head(target))

        self.c = [
            copy(0, at.hd, 0, at.hx),
            copy(1, at.hd, 1, at.hy),
            copy(2, at.hx, 0, at.hx),
            copy(3, at.hy, 1, at.hy),
            copy(4, at.hy, 0, at.hy),
            copy(5, at.hx, 1, at.hx),
        ]

    def send_d(self):
        self.c[0].start()
        self.c[1].start()

    def send_x(self):
        self.c[2].start()

    def send_y(self):
        self.c[3].start()

    def second(self):
        half, part, got, at = self.half, self.part, self.got, self.at
        self.c[0].wait_recv()
        part[at.hy, :half] = (part[at.hy, :half].astype(F32) + got[0].astype(F32)).astype(BF)
        self.c[4].start()
        self.c[1].wait_recv()
        part[at.hx, half:] = (part[at.hx, half:].astype(F32) + got[1].astype(F32)).astype(BF)
        self.c[5].start()

    def wait(self):
        for i in (2, 3, 4, 5):
            self.c[i].wait_recv()

    def total(self):
        half, part, got, at = self.half, self.part, self.got, self.at
        top = part[at.h, :half].astype(F32) + got[2].astype(F32) + got[4].astype(F32)
        low = part[at.h, half:].astype(F32) + got[3].astype(F32) + got[5].astype(F32)
        return jnp.concatenate([top, low], 0)

    def finish(self):
        for copy in self.c:
            copy.wait_send()


class Ledger:
    def __init__(self, at, dp, refs, sems):
        self.at = at
        self.pieces = refs
        self.cs, self.cr, self.ns, self.ar, self.br, self.os, self.fs, self.fr, self.free = sems
        left = at.z < dp // 2
        step = jnp.where(left, 1, -1)
        self.inner = (at.z + step, at.s, at.h)
        self.outer = (at.z - step, at.s, at.h)
        self.core = (at.z, 1 - at.s, at.h)
        self.mid = (at.z == dp // 2 - 1) | (at.z == dp // 2)
        self.outermost = (at.z == 0) | (at.z == dp - 1)

    def rows(self, i, side):
        ref, c, a, b = self.pieces[i]
        half = ref.shape[0] // 2
        return ref.at[pl.ds(pl.multiple_of(side * half, half), half)]

    def swap(self, i):
        c = self.pieces[i][1]
        return remote(self.rows(i, 1 - self.at.s), c, self.cs.at[i], self.cr.at[i], self.core)

    def inward(self, i):
        return remote(
            self.rows(i, self.at.s), self.pieces[i][2], self.ns.at[i], self.ar.at[i], self.inner
        )

    def across(self, i):
        return remote(
            self.rows(i, self.at.s), self.pieces[i][3], self.ns.at[i], self.br.at[i], self.inner
        )

    def outward(self, i):
        return remote(
            self.rows(i, self.at.s), self.pieces[i][3], self.os.at[i], self.br.at[i], self.outer
        )

    def last(self, i):
        mine = self.rows(i, self.at.s)
        return remote(mine, mine, self.fs.at[i], self.fr.at[i], self.core)

    def release(self, i):
        self.swap(i).wait_send()
        pl.semaphore_signal(
            self.free.at[i], inc=1, device_id=self.core, device_id_type=MESH
        )

    def finish(self, i):
        pl.semaphore_wait(self.free.at[i], 1)
        self.last(i).start()

    def add(self, i, *refs):
        mine = self.rows(i, self.at.s)
        total = mine[...].astype(F32)
        for ref in refs:
            total = total + ref[...].astype(F32)
        mine[...] = total.astype(mine.dtype)

    def open(self, *which):
        for i in which:
            self.swap(i).start()

    def step(self, ends=(), middles=(), turns=(), backs=()):
        for i in ends:

            @pl.when(self.outermost)
            def _():
                self.swap(i).wait_recv()
                self.add(i, self.pieces[i][1])
                self.release(i)
                pl.when(self.mid)(lambda: self.across(i).start())
                pl.when(jnp.logical_not(self.mid))(lambda: self.inward(i).start())

        for i in middles:

            @pl.when(jnp.logical_not(self.outermost))
            def _():
                self.swap(i).wait_recv()
                self.inward(i).wait_recv()
                self.add(i, self.pieces[i][1], self.pieces[i][2])
                self.release(i)
                pl.when(self.mid)(lambda: self.across(i).start())
                pl.when(jnp.logical_not(self.mid))(lambda: self.inward(i).start())

        for i in turns:

            @pl.when(self.mid)
            def _():
                self.across(i).wait_recv()
                self.across(i).wait_send()
                self.add(i, self.pieces[i][3])
                pl.when(jnp.logical_not(self.outermost))(lambda: self.outward(i).start())
                self.finish(i)

        for i in backs:

            @pl.when(jnp.logical_not(self.mid))
            def _():
                self.outward(i).wait_recv()
                self.inward(i).wait_send()
                mine = self.rows(i, self.at.s)
                mine[...] = self.pieces[i][3][...]
                pl.when(jnp.logical_not(self.outermost))(lambda: self.outward(i).start())
                self.finish(i)

    def close(self, i):
        self.last(i).wait_recv()
        self.last(i).wait_send()
        pl.when(jnp.logical_not(self.outermost))(lambda: self.outward(i).wait_send())


PIECES = ((0, 0, 2), (0, 2, 2), (1, 0, 2), (1, 2, 2), (2, 0, 2), (2, 2, 2), (3, 0, 2), (3, 2, 2), (4, 0, 2), (4, 2, 2), (5, 0, 1), (5, 1, 1), (5, 2, 1), (5, 3, 1))
RING = 8
HOP_AT, PASS_AT = 2, 2
VECTORS = (14, 15, 18, 19)
SCHEDULE = (
    ((0,), (), (), (), ()),
    ((), (), (), (), ()),
    ((1,), (), (), (), ()),
    ((), (0,), (), (), ()),
    ((2, 3), (1,), (0,), (), ()),
    ((), (), (), (), ()),
    ((), (2,), (1,), (), ()),
    ((), (3,), (), (0,), ()),
    ((4,), (), (), (), ()),
    ((), (), (2,), (), (0,)),
    ((5,), (4,), (), (1,), (1,)),
    ((), (), (3,), (), ()),
    ((6, 7), (5,), (4,), (2, 3), (2,)),
    ((), (6,), (), (), (3,)),
    ((8,), (), (5,), (4,), ()),
    ((9,), (7,), (6,), (), (4,)),
    ((10,), (), (), (5,), ()),
    ((11,), (), (), (), ()),
    ((12, 13), (8, 9), (7,), (), (5,)),
    ((), (10,), (8,), (6,), (6,)),
    ((), (11, 12), (9, 10), (7, 8), (7,)),
    ((), (13,), (11, 12), (9, 10), (8, 9)),
    ((), (), (13,), (11, 12), (10,)),
    ((), (), (), (13,), (11, 12, 13)),
)


def kernel(dp, section, slots, *refs):
    refs = list(refs)

    def take(count):
        out = refs[:count]
        del refs[:count]
        return out

    far_x, lens, image = take(3)
    g1, c1, far_qkv, bqv, far_o, bo, g2, c2, far_u, bu, far_d, bd = take(12)
    tg1, tc1, tqkv, tbqv, two, tbo, tg2, tc2, far_tu, tbu, far_td, tbd = take(12)
    far_dy, far_grads, vec = take(3)
    x, wqkv, wo_all, wu, wd, twu, twd, dy, grads, o_all = take(10)
    n1, q, k, v, p, o, n2, hid, slope, r1, z = take(11)
    w2, b2, images = take(3)
    part, got = take(2)
    ring, arb, stats, scored, dn2b, rsb = take(6)
    f_out, f_in, s_out, s_in, a_in = take(5)
    (da,) = take(1)
    dm = dy
    c_in, l_in, b_in, vh_in, vc_in, vl_in, vb_in, late, late_in, late_all = take(10)
    ag_sems, rs_sems, w_sems, h_sems, i_sems, st_sems, sm_sems, v_sems, sp_sems, o_sems, wo_sems = (
        take(2) for _ in range(11)
    )
    ledger_sems = take(9)
    in_sems, out_sems = take(2)
    assert not refs

    at = Place()
    tokens, width = x.shape
    block = tokens // 4
    local = far_o.shape[0]
    heads = local // HEAD_DIM
    sub = 128
    captions = tokens // slots
    own_caps = block // slots
    caps = captions
    scale = HEAD_DIM ** (-0.5)
    low_masks = head_masks(local, BF)
    masks = head_masks(local, F32)
    other_core = (at.z, 1 - at.s, at.h)
    zs = [(lax.rem(at.z + j, dp), at.s, at.h) for j in range(1, dp)]
    z_pair = (at.z + 1 - 2 * lax.rem(at.z, 2), at.s, at.h)
    head_peers = [at.hx, at.hy, at.hd]
    others = []
    for j in range(dp):
        for i in range(section):
            if i or j:
                others.append((lax.rem(at.z + j, dp), lax.rem(at.s + i, section), at.h))
    own = pl.ds(pl.multiple_of(at.h * block, block), block)

    def vector(ref):
        return ref[...].reshape(1, -1)

    arrive = at.greet([at.head(j) for j in head_peers] + others)
    loads = [
        pltpu.make_async_copy(source, target, in_sems.at[i])
        for i, (source, target) in enumerate(
            (
                (tqkv, w2.at[at.h, 0:3]),
                (two, w2.at[at.h, 3]),
                (far_x, x),
                (far_qkv, wqkv),
                (far_o, wo_all.at[at.h]),
                (far_u, wu),
                (far_d, wd),
                (far_tu, twu),
                (far_td, twd),
            )
        )
    ]
    for copy in loads:
        copy.start()
    pic = image[...].astype(F32)
    pic = pic * lax.rsqrt(jnp.mean(pic * pic, -1, keepdims=True) + NORM_EPS) * width ** (-0.5)
    images[at.z, at.s] = pic.astype(BF)
    b2[at.h] = tbqv[...]

    quarter = local // 4
    mine = lax.rem(at.z, 2) * 2 + at.s
    pair = (1 - lax.rem(at.z, 2)) * 2 + at.s

    def shard_part(owner, which, first=0, many=4):
        rows = pl.ds(pl.multiple_of(which * quarter, quarter), quarter)
        return w2.at[owner, pl.ds(first, many), rows]

    def same_place(ref, sems, i, device):
        return remote(ref, ref, sems[0].at[i], sems[1].at[i], device)

    hop1 = [
        same_place(shard_part(at.h, mine), w_sems, i, at.head(j))
        for i, j in enumerate((at.hx, at.hy))
    ]
    pass1 = [
        same_place(shard_part(at.hx, mine, 0, 2), w_sems, 2, at.head(at.hy)),
        same_place(shard_part(at.hy, mine, 2, 2), w_sems, 3, at.head(at.hx)),
    ]
    hop_b = [same_place(b2.at[at.h], h_sems, i, at.head(j)) for i, j in enumerate(head_peers)]
    hop2 = [
        same_place(shard_part(j, mine), w_sems, 4 + i, z_pair) for i, j in enumerate(head_peers)
    ]
    hop3 = [
        same_place(shard_part(j, which), w_sems, 7 + 3 * n + i, other_core)
        for i, j in enumerate(head_peers)
        for n, which in enumerate((mine, pair))
    ]
    pics = [
        same_place(images.at[at.z, at.s], i_sems, i, device) for i, device in enumerate(zs)
    ]
    core_pics = same_place(images.at[:, at.s], i_sems, dp - 1, other_core)
    half = pl.ds(pl.multiple_of(at.s * (local // 2), local // 2), local // 2)
    wo_hop = [
        same_place(wo_all.at[at.h, half], wo_sems, i, at.head(j))
        for i, j in enumerate((at.hx, at.hy))
    ]

    def wo_part(owner, which):
        piece = local // 4
        first = pl.multiple_of(at.s * (local // 2) + which * piece, piece)
        return wo_all.at[owner, pl.ds(first, piece)]

    wo_pass = [
        same_place(wo_part(at.hx, 0), wo_sems, 2, at.head(at.hy)),
        same_place(wo_part(at.hy, 1), wo_sems, 3, at.head(at.hx)),
    ]
    wo_core = [
        same_place(wo_all.at[j, half], wo_sems, 4 + i, other_core)
        for i, j in enumerate(head_peers)
    ]
    loads[4].wait()
    arrive()
    for copy in wo_hop + hop_b + pics:
        copy.start()
    for copy in loads[:4]:
        copy.wait()

    scatters = [
        Scatter(at, part, got, rs_sems[0].at[i], rs_sems[1].at[i], block) for i in range(3)
    ]
    gathers = [
        Gather(at, ref, ag_sems[0].at[i], ag_sems[1].at[i], block)
        for i, ref in enumerate((n2, dm, da, dy))
    ]

    def block_of(t):
        return lax.rem(at.hi + lax.div(t, 2), 2) * 2 + lax.rem(at.lo + lax.rem(t, 2), 2)

    def limits(first, count):
        cap = lax.broadcasted_iota(jnp.int32, (captions, count), 0)
        slot = lax.broadcasted_iota(jnp.int32, (captions, count), 1)
        chosen = jnp.where(cap == first + slot // slots, 1.0, 0.0).astype(BF)
        row = jnp.broadcast_to(vector(lens).astype(F32), (8, captions)).astype(BF)
        return dot(row, chosen)[:1]

    def key_bias(first, count):
        slot = lax.broadcasted_iota(jnp.int32, (1, count), 1)
        inside = lax.rem(slot, slots).astype(F32) < limits(first, count)
        return jnp.where(inside, 0.0, NEG)

    row_id = lax.broadcasted_iota(jnp.int32, (sub, sub), 0) // slots
    col_id = lax.broadcasted_iota(jnp.int32, (sub, sub), 1) // slots
    same = row_id == col_id
    mixes = [
        remote(
            o.at[pl.ds(pl.multiple_of(j * block, block), block)],
            o_all.at[at.h],
            o_sems[0].at[i],
            o_sems[1].at[i],
            at.head(j),
        )
        for i, j in enumerate((at.hd, at.hy, at.hx))
    ]

    def attend(t, carry):
        blk = block_of(3 - t)
        rows = pl.ds(pl.multiple_of(blk * block, block), block)
        hat, _ = norm_stats(x[rows].astype(F32))
        normed = (hat * vector(g1) + vector(c1)).astype(BF)
        n1[rows] = normed
        query = (dot_nt(normed, wqkv[0]) + bqv[0:1]).astype(BF)
        keys = dot_nt(normed, wqkv[1]).astype(BF)
        values = (dot_nt(normed, wqkv[2]) + bqv[1:2]).astype(BF)
        q[rows] = query
        k[rows] = keys
        v[rows] = values
        mixed = []
        for m in range(block // sub):
            cut = slice(m * sub, (m + 1) * sub)
            index = blk * (block // sub) + m
            bias = jnp.where(same, key_bias(index * (sub // slots), sub), NEG)
            total = jnp.zeros((sub, local), F32)
            for i in range(heads):
                scores = dot_nt(query[cut] * low_masks[i], keys[cut]) * scale + bias
                scores = jnp.exp(scores - jnp.max(scores, -1, keepdims=True))
                probs = (scores * (1.0 / jnp.sum(scores, -1, keepdims=True))).astype(BF)
                p[index, i] = probs
                total = total + dot(probs, values[cut]) * masks[i]
            mixed.append(total.astype(BF))
        mixed = jnp.concatenate(mixed, 0)
        o[rows] = mixed
        for i in range(3):
            pl.when(t == i)(mixes[i].start)

        @pl.when(t == HOP_AT)
        def _():
            for copy in hop1:
                copy.start()

        @pl.when(t == 1)
        def _():
            for copy in wo_hop:
                copy.wait_recv()
            for copy in wo_pass + wo_core[:2]:
                copy.start()

        @pl.when(t == 2)
        def _():
            for copy in wo_pass:
                copy.wait_recv()
            wo_core[2].start()

        @pl.when(t == 3)
        def _():
            o_all[at.h] = mixed

        return carry

    lax.fori_loop(0, 4, attend, 0)
    for copy in mixes + wo_core:
        copy.wait_recv()
    resid = x[own].astype(F32) + vector(bo)
    for j in range(4):
        resid = resid + dot(o_all[j], wo_all[j])
    r1[...] = resid
    hat, _ = norm_stats(resid)
    n2[own] = (hat * vector(g2) + vector(c2)).astype(BF)

    def waits(t, gather):
        @pl.when(t == 1)
        def _():
            gather.forward()
            gather.wait_x()

        pl.when(t == 2)(gather.wait_y)
        pl.when(t == 3)(gather.wait_d)

    def sends(t, scatter):
        pl.when(t == 1)(scatter.send_x)
        pl.when(t == 2)(scatter.send_y)
        pl.when(t == 3)(scatter.send_d)

    gathers[0].start()
    for copy in hop1:
        copy.wait_recv()
    for copy in pass1 + hop2[:2]:
        copy.start()
    for copy in loads[5:7]:
        copy.wait()

    def feed(t, carry):
        waits(t, gathers[0])
        blk = block_of(t)
        rows = pl.ds(pl.multiple_of(blk * block, block), block)
        value, steep = gelu_pair(dot(n2[rows], wu[...]) + vector(bu))
        value = value.astype(BF)
        hid[rows] = value
        slope[rows] = steep.astype(BF)
        part[blk] = dot(value, wd[...]).astype(BF)
        sends(t, scatters[0])

        @pl.when(t == PASS_AT)
        def _():
            for copy in pass1:
                copy.wait_recv()
            hop2[2].start()

        return carry

    lax.fori_loop(0, 4, feed, 0)
    for i in range(3):
        hop2[i].wait_recv()
        hop3[2 * i].start()
        hop3[2 * i + 1].start()
    for copy in pics:
        copy.wait_recv()
    core_pics.start()
    scatters[0].second()
    scatters[0].wait()
    zv = r1[...] + scatters[0].total() + vector(bd)
    scatters[0].finish()
    z[...] = zv
    for copy in hop_b + hop3 + [core_pics]:
        copy.wait_recv()

    per = heads * own_caps

    def stack(values):
        return jnp.concatenate([values * low_masks[i] for i in range(heads)], 0)

    def pick_heads(values):
        total = values[:own_caps] * masks[0]
        for i in range(1, heads):
            total = total + values[i * own_caps : (i + 1) * own_caps] * masks[i]
        return total

    first_cap = at.h * own_caps
    last_slot = limits(first_cap, block) - 1.0
    slot_row = lax.broadcasted_iota(jnp.int32, (own_caps, block), 1)
    cap_row = lax.broadcasted_iota(jnp.int32, (own_caps, block), 0)
    picked = (slot_row // slots == cap_row) & (lax.rem(slot_row, slots).astype(F32) == last_slot)
    pick = jnp.where(picked, 1.0, 0.0).astype(BF)
    cap_of = lax.broadcasted_iota(jnp.int32, (block, captions), 0)
    cap_at = lax.broadcasted_iota(jnp.int32, (block, captions), 1)
    length_col = jnp.sum(
        jnp.where(cap_at == first_cap + cap_of // slots, vector(lens).astype(F32), 0.0),
        1,
        keepdims=True,
    )
    slot_col = lax.rem(lax.broadcasted_iota(jnp.int32, (block, 1), 0), slots).astype(F32)
    pcol = jnp.where(slot_col == length_col - 1.0, 1.0, 0.0)

    hat1, rstd1 = norm_stats(zv)
    normed = (hat1 * vector(tg1) + vector(tc1)).astype(BF)
    pooled_low = dot(pick, normed).astype(BF)
    a_in[at.h, 0] = pooled_low
    z_pool = jnp.sum((zv * pcol).reshape(own_caps, slots, width), 1)
    us = []
    for j in range(4):
        query = (dot_nt(pooled_low, w2[j, 0]) + b2[j, 0:1]).astype(BF)
        s_out[j, 0] = query
        us.append(dot(stack(query), w2[j, 1]).astype(BF))
    u_all = jnp.concatenate(us, 0)
    rows_n = 4 * per
    row_cap = lax.rem(lax.broadcasted_iota(jnp.int32, (rows_n, block), 0), own_caps)
    col_cap = lax.broadcasted_iota(jnp.int32, (rows_n, block), 1) // slots
    bias = jnp.where(row_cap == col_cap, key_bias(first_cap, block), NEG)
    scores = dot_nt(u_all, normed) * scale + bias
    scores = jnp.exp(scores - jnp.max(scores, -1, keepdims=True))
    probs = scores * (1.0 / jnp.sum(scores, -1, keepdims=True))
    probs_low = probs.astype(BF)
    mix = dot(probs_low, normed).astype(BF)
    attended = jnp.zeros((own_caps, width), F32)
    for j in range(4):
        piece = mix[j * per : (j + 1) * per]
        f_out[j, 0] = piece
        out = (pick_heads(dot_nt(piece, w2[j, 2])) + b2[j, 1:2]).astype(BF)
        s_out[j, 3] = out
        attended = attended + dot(out, w2[j, 3])
    ring[at.h] = z_pool + attended + vector(tbo)

    def small(ref, i, j, target=None):
        return remote(
            ref,
            ref if target is None else target,
            sm_sems[0].at[i],
            sm_sems[1].at[i],
            at.head(j),
        )

    for copy in loads[7:]:
        copy.wait()
    rings = [small(ring.at[at.h], i, j) for i, j in enumerate(head_peers)]
    early = [
        small(f_out.at[j, 0], 18 + i, j, f_in.at[at.h, 0]) for i, j in enumerate(head_peers)
    ]
    for copy in rings + early:
        copy.start()
    for copy in rings:
        copy.wait_recv()

    r1_all = ring[...].reshape(caps, width)
    hat2_all, _ = norm_stats(r1_all)
    n2_top = (hat2_all * vector(tg2) + vector(tc2)).astype(BF)
    value, steep = gelu_pair(dot(n2_top, twu[...]) + vector(tbu))
    value = value.astype(BF)
    arb[at.h] = dot(value, twd[...]).astype(BF)
    sums = [small(arb.at[at.h], 3 + i, j) for i, j in enumerate(head_peers)]
    for copy in sums:
        copy.start()
    for copy in sums:
        copy.wait_recv()
    pooled = r1_all + vector(tbd)
    for j in range(4):
        pooled = pooled + arb[j].astype(F32)
    unit_r = lax.rsqrt(jnp.mean(pooled * pooled, -1, keepdims=True) + NORM_EPS)
    text = (pooled * unit_r * width ** (-0.5)).astype(BF)

    everyone = dp * section * caps
    batch = min(dp, 4)
    wide = batch * section * caps
    lanes = wide // 4
    place = at.z * section + at.s

    def chunk_images(n):
        return images[n * batch : (n + 1) * batch].reshape(wide, width)

    def own_columns(n):
        col = lax.broadcasted_iota(jnp.int32, (caps, wide), 1) + n * wide
        row = lax.broadcasted_iota(jnp.int32, (caps, wide), 0) + place * caps
        return col == row

    chunks = [slice(n * wide, (n + 1) * wide) for n in range(dp // batch)]
    row_max = diagonal = None
    for n, cols in enumerate(chunks):
        logits = LOGIT_SCALE * dot_nt(text, chunk_images(n))
        scored[:, cols] = logits
        found = jnp.max(logits, 1, keepdims=True)
        row_max = found if row_max is None else jnp.maximum(row_max, found)
        found = jnp.sum(jnp.where(own_columns(n), logits, 0.0), 1, keepdims=True)
        diagonal = found if diagonal is None else diagonal + found
        col_max = jnp.max(logits, 0, keepdims=True)
        col_sum = jnp.sum(jnp.exp(logits - col_max), 0, keepdims=True)
        for i in range(4):
            stats[place, n, i : i + 1] = col_max[:, i * lanes : (i + 1) * lanes]
            stats[place, n, 4 + i : 5 + i] = col_sum[:, i * lanes : (i + 1) * lanes]
    tells = [
        same_place(stats.at[place], st_sems, i, device) for i, device in enumerate(others)
    ]
    for copy in tells:
        copy.start()
    row_sum = None
    for n, cols in enumerate(chunks):
        found = jnp.sum(jnp.exp(scored[:, cols] - row_max), 1, keepdims=True)
        row_sum = found if row_sum is None else row_sum + found
    row_lse = row_max + jnp.log(row_sum)

    def pull(n, cols, lse):
        steep = jnp.exp(scored[:, cols] - lse) - jnp.where(own_columns(n), 1.0, 0.0)
        return dot((steep * (0.5 / everyone)).astype(BF), chunk_images(n))

    text_grad = None
    for n, cols in enumerate(chunks):
        term = pull(n, cols, row_lse)
        text_grad = term if text_grad is None else text_grad + term
    lost = jnp.sum(row_lse - 2.0 * diagonal, 0, keepdims=True)
    for copy in tells:
        copy.wait_recv()
    for n, cols in enumerate(chunks):
        told = stats[:, n]
        top = jnp.max(told[:, 0:4], 0)
        total = jnp.sum(told[:, 4:8] * jnp.exp(told[:, 0:4] - top[None]), 0)
        lse = top + jnp.log(total)
        col_lse = jnp.concatenate([lse[i : i + 1] for i in range(4)], 1)
        text_grad = text_grad + pull(n, cols, col_lse)
        found = jnp.sum(jnp.where(own_columns(n), col_lse, 0.0), 1, keepdims=True)
        lost = lost + jnp.sum(found, 0, keepdims=True)
    text_grad = LOGIT_SCALE * text_grad
    inner = jnp.mean(pooled * text_grad, -1, keepdims=True)
    d_pool = (unit_r * width ** (-0.5)) * (text_grad - pooled * (unit_r * unit_r * inner))
    z[:caps] = d_pool

    pieces = []
    taken = 0
    for i, (a, first, many) in enumerate(PIECES):
        first, many = first * width // 4, many * width // 4
        here = pl.ds(taken, many // 2)
        lane = pl.ds(0, many // 2)
        pieces.append(
            (grads.at[a, pl.ds(first, many)], c_in.at[here], l_in.at[i % RING, lane], b_in.at[here])
        )
        taken += many // 2
    count = len(pieces)
    pieces.append((vec, vc_in, vl_in, vb_in))
    ledger = Ledger(at, dp, pieces, ledger_sems)

    def flush(i):
        a, first, many = PIECES[i]
        rows = pl.ds(first * width // 4, many * width // 4)
        return pltpu.make_async_copy(grads.at[a, rows], far_grads.at[a, rows], out_sems.at[i])

    def slot(number):
        ends, middles, turns, backs, done = SCHEDULE[number]
        if number in VECTORS:
            chosen = [()] * 4
            chosen[VECTORS.index(number)] = (count,)
            ledger.step(*chosen)
        ledger.step(ends, middles, turns, backs)
        for i in done:
            ledger.close(i)
            flush(i).start()

    low = d_pool.astype(BF)
    du_top = (dot_nt(low, twd[...]) * steep).astype(BF)
    dn2b[...] = dot_nt(du_top, twu[...]).astype(BF)
    own_rows = pl.ds(pl.multiple_of(at.h * own_caps, own_caps), own_caps)
    backs = []
    for i, j in enumerate(head_peers):
        there = pl.ds(pl.multiple_of(j * own_caps, own_caps), own_caps)
        backs.append(small(dn2b.at[there], 6 + i, j, rsb.at[at.h]))
    for copy in backs:
        copy.start()
    grads[0] = dot_tn(value, low).astype(BF)
    ledger.open(0, 1)
    grads[1] = dot_tn(n2_top, du_top).astype(BF)
    ledger.open(2, 3)
    vec[...] = jnp.zeros_like(vec)
    vec[22:23, 0:128] = jnp.broadcast_to(lost, (1, 128))
    vec[17:18] = rows_sum(du_top.astype(F32))
    rsb[at.h] = dn2b[own_rows]
    slot(0)
    for copy in backs:
        copy.wait_recv()
    dn2 = rsb[0].astype(F32)
    for j in range(1, 4):
        dn2 = dn2 + rsb[j].astype(F32)
    hat2, rstd2 = norm_stats(ring[at.h])
    dpool_own = z[own_rows]
    dr1_top = dpool_own + norm_back(dn2, hat2, rstd2, vector(tg2))
    vec[8:9] = rows_sum(dr1_top)
    vec[9:10] = rows_sum(dn2 * hat2)
    vec[10:11] = rows_sum(dn2)
    vec[11:12] = rows_sum(dpool_own)

    slot(1)

    da_top = dr1_top.astype(BF)
    a_in[at.h, 1] = da_top
    ws = []
    for j in range(4):
        d_out = dot_nt(da_top, w2[j, 3]).astype(BF)
        s_out[j, 2] = d_out
        ws.append(dot(stack(d_out), w2[j, 2]).astype(BF))
    w_all = jnp.concatenate(ws, 0)
    d_probs = dot_nt(w_all, normed)
    d_scores = probs * (d_probs - jnp.sum(probs * d_probs, -1, keepdims=True))
    scores_low = d_scores.astype(BF)
    g_rows = (dot(scores_low, normed) * scale).astype(BF)
    slot(2)
    d_pooled_low = jnp.zeros((own_caps, width), F32)
    for j in range(4):
        piece = g_rows[j * per : (j + 1) * per]
        f_out[j, 1] = piece
        d_query = pick_heads(dot_nt(piece, w2[j, 1])).astype(BF)
        s_out[j, 1] = d_query
        d_pooled_low = d_pooled_low + dot(d_query, w2[j, 0])
    facts = []
    for i, j in enumerate(head_peers):
        facts.append(small(f_out.at[j, 1], 9 + i, j, f_in.at[at.h, 1]))
        facts.append(small(s_out.at[j], 12 + i, j, s_in.at[at.h]))
        facts.append(small(a_in.at[at.h], 15 + i, j))
    dn = dot_tn(scores_low, u_all) * scale + dot_tn(probs_low, w_all)

    def widen(values):
        values = jnp.broadcast_to(values[:, None, :], (own_caps, slots, width))
        return values.reshape(block, width)

    dn = dn + pcol * widen(d_pooled_low)
    dz = norm_back(dn, hat1, rstd1, vector(tg1)) + pcol * widen(dr1_top)
    dm[own] = dz.astype(BF)
    gathers[1].start()
    for copy in facts:
        copy.start()
    z[...] = dz
    vec[6:7] = rows_sum(dn * hat1)
    vec[7:8] = rows_sum(dn)
    vec[5:6] = rows_sum(dz)

    f_in[at.h] = f_out[at.h]
    s_in[at.h] = s_out[at.h]
    slot(3)
    scatter_a = scatters[1]

    def feed_back(t, carry):
        waits(t, gathers[1])
        blk = block_of(t)
        rows = pl.ds(pl.multiple_of(blk * block, block), block)
        grad = (dot_nt(dm[rows], wd[...]) * slope[rows].astype(F32)).astype(BF)
        slope[rows] = grad
        part[blk] = dot_nt(grad, wu[...]).astype(BF)
        sends(t, scatter_a)
        for i in range(3):
            pl.when(t == i)(lambda: slot(4 + i))
        return carry

    lax.fori_loop(0, 4, feed_back, 0)
    gathers[1].finish()
    for copy in early + facts:
        copy.wait_recv()
    pooled_all = jnp.concatenate([a_in[j, 0] for j in range(4)], 0)
    da_all = jnp.concatenate([a_in[j, 1] for j in range(4)], 0)
    dq_all = jnp.concatenate([s_in[j, 1] for j in range(4)], 0)
    do_all = jnp.concatenate([s_in[j, 2] for j in range(4)], 0)
    out_all = jnp.concatenate([s_in[j, 3] for j in range(4)], 0)
    grads[2, 0:local] = dot_tn(dq_all, pooled_all).astype(BF)
    grads[2, local : 2 * local] = dot_tn(
        jnp.concatenate([stack(s_in[j, 0]) for j in range(4)], 0),
        jnp.concatenate([f_in[j, 1] for j in range(4)], 0),
    ).astype(BF)
    grads[2, 2 * local : 3 * local] = dot_tn(
        jnp.concatenate([stack(s_in[j, 2]) for j in range(4)], 0),
        jnp.concatenate([f_in[j, 0] for j in range(4)], 0),
    ).astype(BF)
    grads[2, 3 * local :] = dot_tn(out_all, da_all).astype(BF)
    ledger.open(4, 5)
    vec[20:21, 0:local] = rows_sum(dq_all.astype(F32))
    vec[21:22, 0:local] = rows_sum(do_all.astype(F32))
    slot(7)
    grads[3] = dot_tn(hid[...], dm[...]).astype(BF)
    ledger.open(6, 7)
    slot(8)
    grads[4] = dot_tn(n2[...], slope[...]).astype(BF)
    ledger.open(8, 9)
    slot(9)
    scatter_a.second()
    vec[16:17] = rows_sum(slope[...].astype(F32))
    slot(10)
    scatter_a.wait()
    dn2 = scatter_a.total()
    scatter_a.finish()
    hat, rstd = norm_stats(r1[...])
    back = z[...] + norm_back(dn2, hat, rstd, vector(g2))
    r1[...] = back
    da[own] = back.astype(BF)
    gathers[2].start()
    vec[2:3] = rows_sum(back)
    vec[3:4] = rows_sum(dn2 * hat)
    vec[4:5] = rows_sum(dn2)

    vh_in[at.h] = vec[0:16]
    tops = [same_place(vh_in.at[at.h], v_sems, i, at.head(j)) for i, j in enumerate(head_peers)]
    for copy in tops:
        copy.start()
    slot(11)
    scatter_b = scatters[2]

    def attend_back(t, carry):
        waits(t, gathers[2])
        blk = block_of(t)
        rows = pl.ds(pl.multiple_of(blk * block, block), block)
        d_out = dot_nt(da[rows], wo_all[at.h]).astype(BF)
        query, keys, values = q[rows], k[rows], v[rows]
        parts = [[], [], []]
        for m in range(block // sub):
            cut = slice(m * sub, (m + 1) * sub)
            index = blk * (block // sub) + m
            dq = jnp.zeros((sub, local), F32)
            dk = jnp.zeros((sub, local), F32)
            dv = jnp.zeros((sub, local), F32)
            for i in range(heads):
                probs_low = p[index, i]
                probs = probs_low.astype(F32)
                d_probs = dot_nt(d_out[cut] * low_masks[i], values[cut])
                d_scores = probs * (d_probs - jnp.sum(probs * d_probs, -1, keepdims=True))
                d_scores = d_scores.astype(BF)
                dq = dq + dot(d_scores, keys[cut]) * masks[i]
                dk = dk + dot_tn(d_scores, query[cut]) * masks[i]
                dv = dv + dot_tn(probs_low, d_out[cut]) * masks[i]
            parts[0].append((dq * scale).astype(BF))
            parts[1].append((dk * scale).astype(BF))
            parts[2].append(dv.astype(BF))
        total = None
        for i in range(3):
            whole = jnp.concatenate(parts[i], 0)
            (q, k, v)[i][rows] = whole
            term = dot(whole, wqkv[i])
            total = term if total is None else total + term
        part[blk] = total.astype(BF)
        sends(t, scatter_b)
        for i in range(3):
            pl.when(t == i)(lambda: slot(12 + i))

        @pl.when(t == 1)
        def _():
            for copy in tops:
                copy.wait_recv()
            vec[0:16] = vh_in[0] + vh_in[1] + vh_in[2] + vh_in[3]
            ledger.open(count)

        return carry

    lax.fori_loop(0, 4, attend_back, 0)
    grads[5, 0:local] = dot_tn(q[...], n1[...]).astype(BF)
    ledger.open(10)
    grads[5, local : 2 * local] = dot_tn(k[...], n1[...]).astype(BF)
    ledger.open(11)
    slot(15)
    grads[5, 2 * local : 3 * local] = dot_tn(v[...], n1[...]).astype(BF)
    ledger.open(12)
    slot(16)
    grads[5, 3 * local :] = dot_tn(o[...], da[...]).astype(BF)
    ledger.open(13)
    slot(17)
    scatter_b.second()
    late[...] = jnp.zeros_like(late)
    late[2:3, 0:local] = rows_sum(q[...].astype(F32))
    late[3:4, 0:local] = rows_sum(v[...].astype(F32))
    slot(18)
    scatter_b.wait()
    dn1 = scatter_b.total()
    hat, rstd = norm_stats(x[own].astype(F32))
    dy[own] = (r1[...] + norm_back(dn1, hat, rstd, vector(g1))).astype(BF)
    gathers[3].start()
    late[0:1] = rows_sum(dn1 * hat)
    late[1:2] = rows_sum(dn1)

    late_in[at.h] = late[...]
    lates = [
        same_place(late_in.at[at.h], v_sems, 3 + i, at.head(j)) for i, j in enumerate(head_peers)
    ]
    for copy in lates:
        copy.start()
    slot(19)
    for copy in lates:
        copy.wait_recv()
    late_all[place, 0:2] = late_in[0, 0:2] + late_in[1, 0:2] + late_in[2, 0:2] + late_in[3, 0:2]
    late_all[place, 2:8] = late[2:8]
    spreads = [
        same_place(late_all.at[place], sp_sems, i, device) for i, device in enumerate(others)
    ]
    for copy in spreads:
        copy.start()
    slot(20)
    gathers[3].forward()
    slot(21)
    gathers[3].wait_x()
    gathers[3].wait_y()
    slot(22)
    gathers[3].wait_d()
    spill = pltpu.make_async_copy(dy, far_dy, out_sems.at[count])
    spill.start()
    slot(23)
    for copy in spreads:
        copy.wait_recv()
    total = late_all[0]
    for i in range(1, dp * section):
        total = total + late_all[i]
    ledger.close(count)
    vec[0:2] = total[0:2]
    vec[18:20] = total[2:4]
    for i in range(count):
        flush(i).wait()
    spill.wait()
    scatter_b.finish()
    for i in (0, 2, 3):
        gathers[i].finish()
    for copy in hop1 + pass1 + hop_b + hop2 + hop3 + pics + [core_pics]:
        copy.wait_send()
    for copy in wo_hop + wo_pass + wo_core + mixes:
        copy.wait_send()
    for copy in rings + early + sums + tells + backs + facts + tops + lates + spreads:
        copy.wait_send()


def run_kernel(dp, section, slots, x, lens, image, base, top):
    tokens, width = x.shape
    local = base[4].shape[0]
    ff = base[8].shape[1]
    block = tokens // 4
    heads = local // HEAD_DIM
    captions = image.shape[0]
    own_caps = captions // 4
    per = heads * own_caps
    everyone = dp * section * captions
    batch = min(dp, 4)
    others = dp * section - 1
    vmem = pl.BlockSpec(memory_space=pltpu.VMEM)
    hbm = pl.BlockSpec(memory_space=pl.ANY)
    big = (0, 5, 7, 11, 13, 17, 19, 23, 25)
    shape = jax.ShapeDtypeStruct
    outs = [
        shape((tokens, width), BF),
        shape((6, width, width), BF),
        shape((32, width), F32),
    ]
    assert ff == width and 4 * local == width
    sems = pltpu.SemaphoreType.DMA
    ram = pltpu.VMEM
    count = len(PIECES)
    rows = sum(piece[2] for piece in PIECES) * width // 8
    scratch = [
        ram((tokens, width), BF),
        ram((3, local, width), BF),
        ram((4, local, width), BF),
        ram((width, ff), BF),
        ram((ff, width), BF),
        ram((width, ff), BF),
        ram((ff, width), BF),
        ram((tokens, width), BF),
        ram((6, width, width), BF),
        ram((4, block, local), BF),
        ram((tokens, width), BF),
        ram((tokens, local), BF),
        ram((tokens, local), BF),
        ram((tokens, local), BF),
        ram((tokens // 128, heads, 128, 128), BF),
        ram((tokens, local), BF),
        ram((tokens, width), BF),
        ram((tokens, ff), BF),
        ram((tokens, ff), BF),
        ram((block, width), F32),
        ram((block, width), F32),
        ram((4, 4, local, width), BF),
        ram((4, 2, local), F32),
        ram((dp, section, captions, width), BF),
        ram((4, block, width), BF),
        ram((6, block // 2, width), BF),
        ram((4, own_caps, width), F32),
        ram((4, captions, width), BF),
        ram((dp * section, dp // batch, 8, everyone // (dp // batch) // 4), F32),
        ram((captions, everyone), F32),
        ram((captions, width), BF),
        ram((4, own_caps, width), BF),
        ram((4, 2, per, width), BF),
        ram((4, 2, per, width), BF),
        ram((4, 4, own_caps, local), BF),
        ram((4, 4, own_caps, local), BF),
        ram((4, 2, own_caps, width), BF),
        ram((tokens, width), BF),
        ram((rows, width), BF),
        ram((RING, width // 4, width), BF),
        ram((rows, width), BF),
        ram((4, 16, width), F32),
        ram((16, width), F32),
        ram((16, width), F32),
        ram((16, width), F32),
        ram((8, width), F32),
        ram((4, 8, width), F32),
        ram((dp * section, 8, width), F32),
    ]
    for many in ((4, 6), (3, 6), (13,), (3,), (dp,), (others,), (21,), (6,), (others,), (3,), (7,)):
        scratch += [sems(many), sems(many)]
    scratch += [sems((count + 1,))] * 8 + [pltpu.SemaphoreType.REGULAR((count + 1,))]
    scratch += [sems((9,)), sems((count + 1,))]
    return pl.pallas_call(
        functools.partial(kernel, dp, section, slots),
        out_shape=outs,
        in_specs=[hbm if i in big else vmem for i in range(27)],
        out_specs=[hbm, hbm, vmem],
        scratch_shapes=scratch,
        compiler_params=pltpu.CompilerParams(
            collective_id=0, has_side_effects=True, vmem_limit_bytes=VMEM_LIMIT
        ),
        cost_estimate=pl.CostEstimate(
            flops=14 * 10**9, bytes_accessed=40 * 10**6, transcendentals=4 * 10**6
        ),
    )(x, lens, image, *base, *top)


def widen_kernel(local, scale, far_dy, far_grads, vec, *refs):
    loss, text, base, top = refs[0], refs[1], refs[2:14], refs[14:26]
    near_dy, near_grads, wide_text, wide_grads, dy_in, dy_out, g_in, g_out = refs[26:]
    rows = wide_text.shape[0] // 4
    width = wide_text.shape[1]
    incoming = []
    for a in (3, 4, 5, 0, 1, 2):
        for n in range(4):
            span = pl.ds(n * local, local)
            incoming.append(
                pltpu.make_async_copy(
                    far_grads.at[a, span], near_grads.at[a, span], g_in.at[4 * a + n]
                )
            )
    texts = []
    for n in range(4):
        span = pl.ds(n * rows, rows)
        texts.append(pltpu.make_async_copy(far_dy.at[span], near_dy.at[span], dy_in.at[n]))
    for copy in incoming + texts:
        copy.start()
    loss[...] = vec[22:23, 0:1] * scale
    for layer, row, bu, bqv in ((base, 0, 16, 18), (top, 6, 17, 20)):
        layer[0][...] = vec[row]
        layer[1][...] = vec[row + 1]
        layer[3][...] = vec[bqv : bqv + 2, 0:local]
        layer[5][...] = vec[row + 2]
        layer[6][...] = vec[row + 3]
        layer[7][...] = vec[row + 4]
        layer[9][...] = vec[bu]
        layer[11][...] = vec[row + 5]
    outgoing = []
    for i, copy in enumerate(incoming):
        a, n = (3, 4, 5, 0, 1, 2)[i // 4], i % 4
        layer = base if a >= 3 else top
        span = pl.ds(n * local, local)
        copy.wait()
        wide_grads[a, span] = near_grads[a, span].astype(F32)
        if a % 3 == 2:
            target = layer[2].at[n] if n < 3 else layer[4]
        else:
            target = layer[10 if a % 3 == 0 else 8].at[span]
        outgoing.append(
            pltpu.make_async_copy(wide_grads.at[a, span], target, g_out.at[4 * a + n])
        )
        outgoing[-1].start()
    for n, copy in enumerate(texts):
        span = pl.ds(n * rows, rows)
        copy.wait()
        wide_text[span] = near_dy[span].astype(F32)
        outgoing.append(pltpu.make_async_copy(wide_text.at[span], text.at[span], dy_out.at[n]))
        outgoing[-1].start()
    for copy in outgoing:
        copy.wait()


def widen(local, scale, dy, grads, vec):
    tokens, width = dy.shape
    vmem = pl.BlockSpec(memory_space=pltpu.VMEM)
    hbm = pl.BlockSpec(memory_space=pl.ANY)
    shape = jax.ShapeDtypeStruct
    line = (shape((width,), F32), vmem)
    square = (shape((width, width), F32), hbm)
    layer = [
        line,
        line,
        (shape((3, local, width), F32), hbm),
        (shape((2, local), F32), vmem),
        (shape((local, width), F32), hbm),
        line,
        line,
        line,
        square,
        line,
        square,
        line,
    ]
    outs = [(shape((1, 1), F32), vmem), (shape((tokens, width), F32), hbm)] + layer * 2
    sems = pltpu.SemaphoreType.DMA
    return pl.pallas_call(
        functools.partial(widen_kernel, local, scale),
        out_shape=[item[0] for item in outs],
        in_specs=[hbm, hbm, vmem],
        out_specs=[item[1] for item in outs],
        scratch_shapes=[
            pltpu.VMEM((tokens, width), BF),
            pltpu.VMEM((6, width, width), BF),
            pltpu.VMEM((tokens, width), F32),
            pltpu.VMEM((6, width, width), F32),
            sems((4,)),
            sems((4,)),
            sems((24,)),
            sems((24,)),
        ],
        compiler_params=pltpu.CompilerParams(vmem_limit_bytes=VMEM_LIMIT),
        cost_estimate=pl.CostEstimate(
            flops=10**7, bytes_accessed=26 * 10**6, transcendentals=0
        ),
    )(dy, grads, vec)


def on_device(dp, section, text_in, lengths, image_embed, *params):
    base, top = params[:12], params[12:]
    captions, slots, width = text_in.shape
    tokens = captions * slots
    local = base[4].shape[0]

    def layout(layer):
        return layer[:2] + (layer[2].transpose(1, 2, 0),) + layer[3:]

    dy, grads, vec = run_kernel(
        dp,
        section,
        slots,
        text_in.reshape(tokens, width),
        lengths,
        image_embed,
        layout(base),
        layout(top),
    )
    outs = list(widen(local, 0.5 / (dp * section * captions), dy, grads, vec))
    for i in (4, 16):
        outs[i] = outs[i].transpose(2, 0, 1)
    return (outs[0][0, 0], outs[1].reshape(captions, slots, width)) + tuple(outs[2:])


def solution(mesh):
    layer_in = (
        P(),
        P(),
        P(None, None, "head"),
        P(None, "head"),
        P("head", None),
        P(),
        P(),
        P(),
        P(None, "head"),
        P("head"),
        P("head", None),
        P(),
    )
    rows = P(("dp", "section"), None, None)
    return jax.shard_map(
        functools.partial(on_device, mesh.shape["dp"], mesh.shape["section"]),
        mesh=mesh,
        in_specs=(rows, P(("dp", "section")), P(("dp", "section"), None)) + layer_in * 2,
        out_specs=(P(), rows) + layer_in * 2,
        check_vma=False,
    )
```

```python
import functools

import jax
import jax.numpy as jnp
from jax import lax
from jax.experimental import pallas as pl
from jax.experimental.pallas import tpu as pltpu
from jax.sharding import PartitionSpec as P

HEAD_DIM = 64
NORM_EPS = 1e-06
LOGIT_SCALE = 50.0
NEG = -1e30
BF = jnp.bfloat16
F32 = jnp.float32
MESH = pl.DeviceIdType.MESH
VMEM_LIMIT = 63 * 2**20


def dot(a, b):
    return lax.dot_general(a, b, (((1,), (0,)), ((), ())), preferred_element_type=F32)


def dot_nt(a, b):
    return lax.dot_general(a, b, (((1,), (1,)), ((), ())), preferred_element_type=F32)


def dot_tn(a, b):
    return lax.dot_general(a, b, (((0,), (0,)), ((), ())), preferred_element_type=F32)


def norm_stats(values):
    center = jnp.mean(values, -1, keepdims=True)
    shifted = values - center
    spread = jnp.mean(shifted * shifted, -1, keepdims=True)
    rstd = lax.rsqrt(spread + NORM_EPS)
    return shifted * rstd, rstd


def norm_back(grad, hat, rstd, gain):
    scaled = grad * gain
    m1 = jnp.mean(scaled, -1, keepdims=True)
    m2 = jnp.mean(scaled * hat, -1, keepdims=True)
    return rstd * (scaled - m1 - hat * m2)


def rows_sum(values):
    return jnp.sum(values, 0, keepdims=True)


def gelu_pair(u):
    c = 0.7978845608028654
    u2 = u * u
    t = jnp.tanh(c * u * (1.0 + 0.044715 * u2))
    half = 0.5 * (1.0 + t)
    value = u * half
    slope = half + 0.5 * u * (1.0 - t * t) * (c * (1.0 + 3.0 * 0.044715 * u2))
    return value, slope


def head_masks(width, kind):
    lane = lax.broadcasted_iota(jnp.int32, (1, width), 1)
    return [
        jnp.where((lane >= i * HEAD_DIM) & (lane < (i + 1) * HEAD_DIM), 1.0, 0.0).astype(kind)
        for i in range(width // HEAD_DIM)
    ]


class Place:
    def __init__(self):
        self.z = lax.axis_index("dp")
        self.s = lax.axis_index("section")
        h = lax.axis_index("head")
        self.h = h
        self.hi = lax.div(h, 2)
        self.lo = lax.rem(h, 2)
        self.hx = self.block(0, 1)
        self.hy = self.block(1, 0)
        self.hd = self.block(1, 1)

    def block(self, flip_hi, flip_lo):
        return lax.rem(self.hi + flip_hi, 2) * 2 + lax.rem(self.lo + flip_lo, 2)

    def head(self, other):
        return (self.z, self.s, other)

    def greet(self, devices):
        barrier = pltpu.get_barrier_semaphore()
        for device in devices:
            pl.semaphore_signal(barrier, inc=1, device_id=device, device_id_type=MESH)
        return lambda: pl.semaphore_wait(barrier, len(devices))


def remote(src, dst, send_sem, recv_sem, device):
    return pltpu.make_async_remote_copy(
        src_ref=src,
        dst_ref=dst,
        send_sem=send_sem,
        recv_sem=recv_sem,
        device_id=device,
        device_id_type=MESH,
    )


class Gather:
    def __init__(self, at, ref, send, recv, block):
        half = block // 2

        def rows(owner, part):
            return ref.at[pl.ds(pl.multiple_of(owner * block + part * half, half), half)]

        def copy(i, owner, part, target):
            piece = rows(owner, part)
            return remote(piece, piece, send.at[i], recv.at[i], at.head(target))

        self.c = [
            copy(0, at.h, 0, at.hx),
            copy(1, at.h, 1, at.hy),
            copy(2, at.h, 1, at.hx),
            copy(3, at.h, 0, at.hy),
            copy(4, at.hx, 0, at.hy),
            copy(5, at.hy, 1, at.hx),
        ]

    def start(self):
        self.c[0].start()
        self.c[1].start()

    def start_rest(self):
        self.c[2].start()
        self.c[3].start()

    def forward(self):
        self.c[0].wait_recv()
        self.c[4].start()
        self.c[1].wait_recv()
        self.c[5].start()

    def wait_x(self):
        self.c[2].wait_recv()

    def wait_y(self):
        self.c[3].wait_recv()

    def wait_d(self):
        self.c[4].wait_recv()
        self.c[5].wait_recv()

    def finish(self):
        for copy in self.c:
            copy.wait_send()


class Scatter:
    def __init__(self, at, part, got, send, recv, block):
        half = block // 2
        self.at, self.part, self.got, self.half = at, part, got, half

        def piece(owner, side):
            return part.at[owner, pl.ds(side * half, half)]

        def copy(i, owner, side, target):
            return remote(piece(owner, side), got.at[i], send.at[i], recv.at[i], at.head(target))

        self.c = [
            copy(0, at.hd, 0, at.hx),
            copy(1, at.hd, 1, at.hy),
            copy(2, at.hx, 0, at.hx),
            copy(3, at.hy, 1, at.hy),
            copy(4, at.hy, 0, at.hy),
            copy(5, at.hx, 1, at.hx),
        ]

    def send_d(self):
        self.c[0].start()
        self.c[1].start()

    def send_x(self):
        self.c[2].start()

    def send_y(self):
        self.c[3].start()

    def second(self):
        half, part, got, at = self.half, self.part, self.got, self.at
        self.c[0].wait_recv()
        part[at.hy, :half] = (part[at.hy, :half].astype(F32) + got[0].astype(F32)).astype(BF)
        self.c[4].start()
        self.c[1].wait_recv()
        part[at.hx, half:] = (part[at.hx, half:].astype(F32) + got[1].astype(F32)).astype(BF)
        self.c[5].start()

    def wait(self):
        for i in (2, 3, 4, 5):
            self.c[i].wait_recv()

    def total(self):
        half, part, got, at = self.half, self.part, self.got, self.at
        top = part[at.h, :half].astype(F32) + got[2].astype(F32) + got[4].astype(F32)
        low = part[at.h, half:].astype(F32) + got[3].astype(F32) + got[5].astype(F32)
        return jnp.concatenate([top, low], 0)

    def finish(self):
        for copy in self.c:
            copy.wait_send()


class Ledger:
    def __init__(self, at, dp, refs, sems):
        self.at = at
        self.pieces = refs
        self.cs, self.cr, self.ns, self.ar, self.br, self.os, self.fs, self.fr, self.free = sems
        left = at.z < dp // 2
        step = jnp.where(left, 1, -1)
        self.inner = (at.z + step, at.s, at.h)
        self.outer = (at.z - step, at.s, at.h)
        self.core = (at.z, 1 - at.s, at.h)
        self.mid = (at.z == dp // 2 - 1) | (at.z == dp // 2)
        self.outermost = (at.z == 0) | (at.z == dp - 1)

    def rows(self, i, side):
        ref, c, a, b = self.pieces[i]
        half = ref.shape[0] // 2
        return ref.at[pl.ds(pl.multiple_of(side * half, half), half)]

    def swap(self, i):
        c = self.pieces[i][1]
        return remote(self.rows(i, 1 - self.at.s), c, self.cs.at[i], self.cr.at[i], self.core)

    def inward(self, i):
        return remote(
            self.rows(i, self.at.s), self.pieces[i][2], self.ns.at[i], self.ar.at[i], self.inner
        )

    def across(self, i):
        return remote(
            self.rows(i, self.at.s), self.pieces[i][3], self.ns.at[i], self.br.at[i], self.inner
        )

    def outward(self, i):
        return remote(
            self.rows(i, self.at.s), self.pieces[i][3], self.os.at[i], self.br.at[i], self.outer
        )

    def last(self, i):
        mine = self.rows(i, self.at.s)
        return remote(mine, mine, self.fs.at[i], self.fr.at[i], self.core)

    def release(self, i):
        self.swap(i).wait_send()
        pl.semaphore_signal(
            self.free.at[i], inc=1, device_id=self.core, device_id_type=MESH
        )

    def finish(self, i):
        pl.semaphore_wait(self.free.at[i], 1)
        self.last(i).start()

    def add(self, i, *refs):
        mine = self.rows(i, self.at.s)
        total = mine[...].astype(F32)
        for ref in refs:
            total = total + ref[...].astype(F32)
        mine[...] = total.astype(mine.dtype)

    def open(self, *which):
        for i in which:
            self.swap(i).start()

    def step(self, ends=(), middles=(), turns=(), backs=()):
        for i in ends:

            @pl.when(self.outermost)
            def _():
                self.swap(i).wait_recv()
                self.add(i, self.pieces[i][1])
                self.release(i)
                pl.when(self.mid)(lambda: self.across(i).start())
                pl.when(jnp.logical_not(self.mid))(lambda: self.inward(i).start())

        for i in middles:

            @pl.when(jnp.logical_not(self.outermost))
            def _():
                self.swap(i).wait_recv()
                self.inward(i).wait_recv()
                self.add(i, self.pieces[i][1], self.pieces[i][2])
                self.release(i)
                pl.when(self.mid)(lambda: self.across(i).start())
                pl.when(jnp.logical_not(self.mid))(lambda: self.inward(i).start())

        for i in turns:

            @pl.when(self.mid)
            def _():
                self.across(i).wait_recv()
                self.across(i).wait_send()
                self.add(i, self.pieces[i][3])
                pl.when(jnp.logical_not(self.outermost))(lambda: self.outward(i).start())
                self.finish(i)

        for i in backs:

            @pl.when(jnp.logical_not(self.mid))
            def _():
                self.outward(i).wait_recv()
                self.inward(i).wait_send()
                mine = self.rows(i, self.at.s)
                mine[...] = self.pieces[i][3][...]
                pl.when(jnp.logical_not(self.outermost))(lambda: self.outward(i).start())
                self.finish(i)

    def close(self, i):
        self.last(i).wait_recv()
        self.last(i).wait_send()
        pl.when(jnp.logical_not(self.outermost))(lambda: self.outward(i).wait_send())


PIECES = ((0, 0, 2), (0, 2, 2), (1, 0, 2), (1, 2, 2), (2, 0, 2), (2, 2, 2), (3, 0, 2), (3, 2, 2), (4, 0, 2), (4, 2, 2), (5, 0, 1), (5, 1, 1), (5, 2, 1), (5, 3, 1))
RING = 8
HOP_AT, PASS_AT = 2, 2
VECTORS = (14, 15, 18, 19)
SCHEDULE = (
    ((0,), (), (), (), ()),
    ((), (), (), (), ()),
    ((1,), (), (), (), ()),
    ((), (0,), (), (), ()),
    ((2, 3), (1,), (0,), (), ()),
    ((), (), (), (), ()),
    ((), (2,), (1,), (), ()),
    ((), (3,), (), (0,), ()),
    ((4,), (), (), (), ()),
    ((), (), (2,), (), (0,)),
    ((5,), (4,), (), (1,), (1,)),
    ((), (), (3,), (), ()),
    ((6, 7), (5,), (4,), (2, 3), (2,)),
    ((), (6,), (), (), (3,)),
    ((8,), (), (5,), (4,), ()),
    ((9,), (7,), (6,), (), (4,)),
    ((10,), (), (), (5,), ()),
    ((11,), (), (), (), ()),
    ((12, 13), (8, 9), (7,), (), (5,)),
    ((), (10,), (8,), (6,), (6,)),
    ((), (11, 12), (9, 10), (7, 8), (7,)),
    ((), (13,), (11, 12), (9, 10), (8, 9)),
    ((), (), (13,), (11, 12), (10,)),
    ((), (), (), (13,), (11, 12, 13)),
)


def kernel(dp, section, slots, *refs):
    refs = list(refs)

    def take(count):
        out = refs[:count]
        del refs[:count]
        return out

    far_x, lens, image = take(3)
    g1, c1, far_qkv, bqv, far_o, bo, g2, c2, far_u, bu, far_d, bd = take(12)
    tg1, tc1, tqkv, tbqv, two, tbo, tg2, tc2, far_tu, tbu, far_td, tbd = take(12)
    far_dy, far_grads, vec = take(3)
    x, wqkv, wo_all, wu, wd, twu, twd, dy, grads, o_all = take(10)
    n1, q, k, v, p, o, n2, hid, slope, r1, z = take(11)
    w2, b2, images = take(3)
    part, got = take(2)
    ring, arb, stats, scored, dn2b, rsb = take(6)
    f_out, f_in, s_out, s_in, a_in = take(5)
    (da,) = take(1)
    dm = dy
    c_in, l_in, b_in, vh_in, vc_in, vl_in, vb_in, late, late_in, late_all = take(10)
    ag_sems, rs_sems, w_sems, h_sems, i_sems, st_sems, sm_sems, v_sems, sp_sems, o_sems, wo_sems = (
        take(2) for _ in range(11)
    )
    ledger_sems = take(9)
    in_sems, out_sems = take(2)
    assert not refs

    at = Place()
    tokens, width = x.shape
    block = tokens // 4
    local = far_o.shape[0]
    heads = local // HEAD_DIM
    sub = 128
    captions = tokens // slots
    own_caps = block // slots
    caps = captions
    scale = HEAD_DIM ** (-0.5)
    low_masks = head_masks(local, BF)
    masks = head_masks(local, F32)
    other_core = (at.z, 1 - at.s, at.h)
    zs = [(lax.rem(at.z + j, dp), at.s, at.h) for j in range(1, dp)]
    z_pair = (at.z + 1 - 2 * lax.rem(at.z, 2), at.s, at.h)
    head_peers = [at.hx, at.hy, at.hd]
    others = []
    for j in range(dp):
        for i in range(section):
            if i or j:
                others.append((lax.rem(at.z + j, dp), lax.rem(at.s + i, section), at.h))
    own = pl.ds(pl.multiple_of(at.h * block, block), block)

    def vector(ref):
        return ref[...].reshape(1, -1)

    arrive = at.greet([at.head(j) for j in head_peers] + others)
    loads = [
        pltpu.make_async_copy(source, target, in_sems.at[i])
        for i, (source, target) in enumerate(
            (
                (tqkv, w2.at[at.h, 0:3]),
                (two, w2.at[at.h, 3]),
                (far_x, x),
                (far_qkv, wqkv),
                (far_o, wo_all.at[at.h]),
                (far_u, wu),
                (far_d, wd),
                (far_tu, twu),
                (far_td, twd),
            )
        )
    ]
    for copy in loads:
        copy.start()
    pic = image[...].astype(F32)
    pic = pic * lax.rsqrt(jnp.mean(pic * pic, -1, keepdims=True) + NORM_EPS) * width ** (-0.5)
    images[at.z, at.s] = pic.astype(BF)
    b2[at.h] = tbqv[...]

    quarter = local // 4
    mine = lax.rem(at.z, 2) * 2 + at.s
    pair = (1 - lax.rem(at.z, 2)) * 2 + at.s

    def shard_part(owner, which, first=0, many=4):
        rows = pl.ds(pl.multiple_of(which * quarter, quarter), quarter)
        return w2.at[owner, pl.ds(first, many), rows]

    def same_place(ref, sems, i, device):
        return remote(ref, ref, sems[0].at[i], sems[1].at[i], device)

    hop1 = [
        same_place(shard_part(at.h, mine), w_sems, i, at.head(j))
        for i, j in enumerate((at.hx, at.hy))
    ]
    pass1 = [
        same_place(shard_part(at.hx, mine, 0, 2), w_sems, 2, at.head(at.hy)),
        same_place(shard_part(at.hy, mine, 2, 2), w_sems, 3, at.head(at.hx)),
    ]
    hop_b = [same_place(b2.at[at.h], h_sems, i, at.head(j)) for i, j in enumerate(head_peers)]
    hop2 = [
        same_place(shard_part(j, mine), w_sems, 4 + i, z_pair) for i, j in enumerate(head_peers)
    ]
    hop3 = [
        same_place(shard_part(j, which), w_sems, 7 + 3 * n + i, other_core)
        for i, j in enumerate(head_peers)
        for n, which in enumerate((mine, pair))
    ]
    pics = [
        same_place(images.at[at.z, at.s], i_sems, i, device) for i, device in enumerate(zs)
    ]
    core_pics = same_place(images.at[:, at.s], i_sems, dp - 1, other_core)
    half = pl.ds(pl.multiple_of(at.s * (local // 2), local // 2), local // 2)
    wo_hop = [
        same_place(wo_all.at[at.h, half], wo_sems, i, at.head(j))
        for i, j in enumerate((at.hx, at.hy))
    ]

    def wo_part(owner, which):
        piece = local // 4
        first = pl.multiple_of(at.s * (local // 2) + which * piece, piece)
        return wo_all.at[owner, pl.ds(first, piece)]

    wo_pass = [
        same_place(wo_part(at.hx, 0), wo_sems, 2, at.head(at.hy)),
        same_place(wo_part(at.hy, 1), wo_sems, 3, at.head(at.hx)),
    ]
    wo_core = [
        same_place(wo_all.at[j, half], wo_sems, 4 + i, other_core)
        for i, j in enumerate(head_peers)
    ]
    loads[4].wait()
    arrive()
    for copy in wo_hop + hop_b + pics:
        copy.start()
    for copy in loads[:4]:
        copy.wait()

    scatters = [
        Scatter(at, part, got, rs_sems[0].at[i], rs_sems[1].at[i], block) for i in range(3)
    ]
    gathers = [
        Gather(at, ref, ag_sems[0].at[i], ag_sems[1].at[i], block)
        for i, ref in enumerate((n2, dm, da, dy))
    ]

    def block_of(t):
        return lax.rem(at.hi + lax.div(t, 2), 2) * 2 + lax.rem(at.lo + lax.rem(t, 2), 2)

    def limits(first, count):
        cap = lax.broadcasted_iota(jnp.int32, (captions, count), 0)
        slot = lax.broadcasted_iota(jnp.int32, (captions, count), 1)
        chosen = jnp.where(cap == first + slot // slots, 1.0, 0.0).astype(BF)
        row = jnp.broadcast_to(vector(lens).astype(F32), (8, captions)).astype(BF)
        return dot(row, chosen)[:1]

    def key_bias(first, count):
        slot = lax.broadcasted_iota(jnp.int32, (1, count), 1)
        inside = lax.rem(slot, slots).astype(F32) < limits(first, count)
        return jnp.where(inside, 0.0, NEG)

    row_id = lax.broadcasted_iota(jnp.int32, (sub, sub), 0) // slots
    col_id = lax.broadcasted_iota(jnp.int32, (sub, sub), 1) // slots
    same = row_id == col_id
    mixes = [
        remote(
            o.at[pl.ds(pl.multiple_of(j * block, block), block)],
            o_all.at[at.h],
            o_sems[0].at[i],
            o_sems[1].at[i],
            at.head(j),
        )
        for i, j in enumerate((at.hd, at.hy, at.hx))
    ]

    def attend(t, carry):
        blk = block_of(3 - t)
        rows = pl.ds(pl.multiple_of(blk * block, block), block)
        hat, _ = norm_stats(x[rows].astype(F32))
        normed = (hat * vector(g1) + vector(c1)).astype(BF)
        n1[rows] = normed
        query = (dot_nt(normed, wqkv[0]) + bqv[0:1]).astype(BF)
        keys = dot_nt(normed, wqkv[1]).astype(BF)
        values = (dot_nt(normed, wqkv[2]) + bqv[1:2]).astype(BF)
        q[rows] = query
        k[rows] = keys
        v[rows] = values
        mixed = []
        for m in range(block // sub):
            cut = slice(m * sub, (m + 1) * sub)
            index = blk * (block // sub) + m
            bias = jnp.where(same, key_bias(index * (sub // slots), sub), NEG)
            total = jnp.zeros((sub, local), F32)
            for i in range(heads):
                scores = dot_nt(query[cut] * low_masks[i], keys[cut]) * scale + bias
                scores = jnp.exp(scores - jnp.max(scores, -1, keepdims=True))
                probs = (scores * (1.0 / jnp.sum(scores, -1, keepdims=True))).astype(BF)
                p[index, i] = probs
                total = total + dot(probs, values[cut]) * masks[i]
            mixed.append(total.astype(BF))
        mixed = jnp.concatenate(mixed, 0)
        o[rows] = mixed
        for i in range(3):
            pl.when(t == i)(mixes[i].start)

        @pl.when(t == HOP_AT)
        def _():
            for copy in hop1:
                copy.start()

        @pl.when(t == 1)
        def _():
            for copy in wo_hop:
                copy.wait_recv()
            for copy in wo_pass + wo_core[:2]:
                copy.start()

        @pl.when(t == 2)
        def _():
            for copy in wo_pass:
                copy.wait_recv()
            wo_core[2].start()

        @pl.when(t == 3)
        def _():
            o_all[at.h] = mixed

        return carry

    lax.fori_loop(0, 4, attend, 0)
    for copy in mixes + wo_core:
        copy.wait_recv()
    resid = x[own].astype(F32) + vector(bo)
    for j in range(4):
        resid = resid + dot(o_all[j], wo_all[j])
    r1[...] = resid
    hat, _ = norm_stats(resid)
    n2[own] = (hat * vector(g2) + vector(c2)).astype(BF)

    def waits(t, gather):
        @pl.when(t == 1)
        def _():
            gather.forward()
            gather.wait_x()

        pl.when(t == 2)(gather.wait_y)
        pl.when(t == 3)(gather.wait_d)

    def sends(t, scatter):
        pl.when(t == 1)(scatter.send_x)
        pl.when(t == 2)(scatter.send_y)
        pl.when(t == 3)(scatter.send_d)

    gathers[0].start()
    for copy in hop1:
        copy.wait_recv()
    for copy in pass1 + hop2[:2]:
        copy.start()
    for copy in loads[5:7]:
        copy.wait()

    def feed(t, carry):
        waits(t, gathers[0])
        blk = block_of(t)
        rows = pl.ds(pl.multiple_of(blk * block, block), block)
        value, steep = gelu_pair(dot(n2[rows], wu[...]) + vector(bu))
        value = value.astype(BF)
        hid[rows] = value
        slope[rows] = steep.astype(BF)
        part[blk] = dot(value, wd[...]).astype(BF)
        sends(t, scatters[0])
        pl.when(t == 0)(gathers[0].start_rest)

        @pl.when(t == PASS_AT)
        def _():
            for copy in pass1:
                copy.wait_recv()
            hop2[2].start()

        return carry

    lax.fori_loop(0, 4, feed, 0)
    for i in range(3):
        hop2[i].wait_recv()
        hop3[2 * i].start()
        hop3[2 * i + 1].start()
    for copy in pics:
        copy.wait_recv()
    core_pics.start()
    scatters[0].second()
    scatters[0].wait()
    zv = r1[...] + scatters[0].total() + vector(bd)
    scatters[0].finish()
    z[...] = zv
    for copy in hop_b + hop3 + [core_pics]:
        copy.wait_recv()

    per = heads * own_caps

    def stack(values):
        return jnp.concatenate([values * low_masks[i] for i in range(heads)], 0)

    def pick_heads(values):
        total = values[:own_caps] * masks[0]
        for i in range(1, heads):
            total = total + values[i * own_caps : (i + 1) * own_caps] * masks[i]
        return total

    first_cap = at.h * own_caps
    last_slot = limits(first_cap, block) - 1.0
    slot_row = lax.broadcasted_iota(jnp.int32, (own_caps, block), 1)
    cap_row = lax.broadcasted_iota(jnp.int32, (own_caps, block), 0)
    picked = (slot_row // slots == cap_row) & (lax.rem(slot_row, slots).astype(F32) == last_slot)
    pick = jnp.where(picked, 1.0, 0.0).astype(BF)
    cap_of = lax.broadcasted_iota(jnp.int32, (block, captions), 0)
    cap_at = lax.broadcasted_iota(jnp.int32, (block, captions), 1)
    length_col = jnp.sum(
        jnp.where(cap_at == first_cap + cap_of // slots, vector(lens).astype(F32), 0.0),
        1,
        keepdims=True,
    )
    slot_col = lax.rem(lax.broadcasted_iota(jnp.int32, (block, 1), 0), slots).astype(F32)
    pcol = jnp.where(slot_col == length_col - 1.0, 1.0, 0.0)

    hat1, rstd1 = norm_stats(zv)
    normed = (hat1 * vector(tg1) + vector(tc1)).astype(BF)
    pooled_low = dot(pick, normed).astype(BF)
    a_in[at.h, 0] = pooled_low
    z_pool = jnp.sum((zv * pcol).reshape(own_caps, slots, width), 1)
    us = []
    for j in range(4):
        query = (dot_nt(pooled_low, w2[j, 0]) + b2[j, 0:1]).astype(BF)
        s_out[j, 0] = query
        us.append(dot(stack(query), w2[j, 1]).astype(BF))
    u_all = jnp.concatenate(us, 0)
    rows_n = 4 * per
    row_cap = lax.rem(lax.broadcasted_iota(jnp.int32, (rows_n, block), 0), own_caps)
    col_cap = lax.broadcasted_iota(jnp.int32, (rows_n, block), 1) // slots
    bias = jnp.where(row_cap == col_cap, key_bias(first_cap, block), NEG)
    scores = dot_nt(u_all, normed) * scale + bias
    scores = jnp.exp(scores - jnp.max(scores, -1, keepdims=True))
    probs = scores * (1.0 / jnp.sum(scores, -1, keepdims=True))
    probs_low = probs.astype(BF)
    mix = dot(probs_low, normed).astype(BF)
    attended = jnp.zeros((own_caps, width), F32)
    for j in range(4):
        piece = mix[j * per : (j + 1) * per]
        f_out[j, 0] = piece
        out = (pick_heads(dot_nt(piece, w2[j, 2])) + b2[j, 1:2]).astype(BF)
        s_out[j, 3] = out
        attended = attended + dot(out, w2[j, 3])
    ring[at.h] = z_pool + attended + vector(tbo)

    def small(ref, i, j, target=None):
        return remote(
            ref,
            ref if target is None else target,
            sm_sems[0].at[i],
            sm_sems[1].at[i],
            at.head(j),
        )

    for copy in loads[7:]:
        copy.wait()
    rings = [small(ring.at[at.h], i, j) for i, j in enumerate(head_peers)]
    early = [
        small(f_out.at[j, 0], 18 + i, j, f_in.at[at.h, 0]) for i, j in enumerate(head_peers)
    ]
    for copy in rings + early:
        copy.start()
    for copy in rings:
        copy.wait_recv()

    r1_all = ring[...].reshape(caps, width)
    hat2_all, _ = norm_stats(r1_all)
    n2_top = (hat2_all * vector(tg2) + vector(tc2)).astype(BF)
    value, steep = gelu_pair(dot(n2_top, twu[...]) + vector(tbu))
    value = value.astype(BF)
    arb[at.h] = dot(value, twd[...]).astype(BF)
    sums = [small(arb.at[at.h], 3 + i, j) for i, j in enumerate(head_peers)]
    for copy in sums:
        copy.start()
    for copy in sums:
        copy.wait_recv()
    pooled = r1_all + vector(tbd)
    for j in range(4):
        pooled = pooled + arb[j].astype(F32)
    unit_r = lax.rsqrt(jnp.mean(pooled * pooled, -1, keepdims=True) + NORM_EPS)
    text = (pooled * unit_r * width ** (-0.5)).astype(BF)

    everyone = dp * section * caps
    batch = min(dp, 4)
    wide = batch * section * caps
    lanes = wide // 4
    place = at.z * section + at.s

    def chunk_images(n):
        return images[n * batch : (n + 1) * batch].reshape(wide, width)

    def own_columns(n):
        col = lax.broadcasted_iota(jnp.int32, (caps, wide), 1) + n * wide
        row = lax.broadcasted_iota(jnp.int32, (caps, wide), 0) + place * caps
        return col == row

    chunks = [slice(n * wide, (n + 1) * wide) for n in range(dp // batch)]
    row_max = diagonal = None
    for n, cols in enumerate(chunks):
        logits = LOGIT_SCALE * dot_nt(text, chunk_images(n))
        scored[:, cols] = logits
        found = jnp.max(logits, 1, keepdims=True)
        row_max = found if row_max is None else jnp.maximum(row_max, found)
        found = jnp.sum(jnp.where(own_columns(n), logits, 0.0), 1, keepdims=True)
        diagonal = found if diagonal is None else diagonal + found
        col_max = jnp.max(logits, 0, keepdims=True)
        col_sum = jnp.sum(jnp.exp(logits - col_max), 0, keepdims=True)
        for i in range(4):
            stats[place, n, i : i + 1] = col_max[:, i * lanes : (i + 1) * lanes]
            stats[place, n, 4 + i : 5 + i] = col_sum[:, i * lanes : (i + 1) * lanes]
    tells = [
        same_place(stats.at[place], st_sems, i, device) for i, device in enumerate(others)
    ]
    for copy in tells:
        copy.start()
    row_sum = None
    for n, cols in enumerate(chunks):
        found = jnp.sum(jnp.exp(scored[:, cols] - row_max), 1, keepdims=True)
        row_sum = found if row_sum is None else row_sum + found
    row_lse = row_max + jnp.log(row_sum)

    def pull(n, cols, lse):
        steep = jnp.exp(scored[:, cols] - lse) - jnp.where(own_columns(n), 1.0, 0.0)
        return dot((steep * (0.5 / everyone)).astype(BF), chunk_images(n))

    text_grad = None
    for n, cols in enumerate(chunks):
        term = pull(n, cols, row_lse)
        text_grad = term if text_grad is None else text_grad + term
    lost = jnp.sum(row_lse - 2.0 * diagonal, 0, keepdims=True)
    for copy in tells:
        copy.wait_recv()
    for n, cols in enumerate(chunks):
        told = stats[:, n]
        top = jnp.max(told[:, 0:4], 0)
        total = jnp.sum(told[:, 4:8] * jnp.exp(told[:, 0:4] - top[None]), 0)
        lse = top + jnp.log(total)
        col_lse = jnp.concatenate([lse[i : i + 1] for i in range(4)], 1)
        text_grad = text_grad + pull(n, cols, col_lse)
        found = jnp.sum(jnp.where(own_columns(n), col_lse, 0.0), 1, keepdims=True)
        lost = lost + jnp.sum(found, 0, keepdims=True)
    text_grad = LOGIT_SCALE * text_grad
    inner = jnp.mean(pooled * text_grad, -1, keepdims=True)
    d_pool = (unit_r * width ** (-0.5)) * (text_grad - pooled * (unit_r * unit_r * inner))
    z[:caps] = d_pool

    pieces = []
    taken = 0
    for i, (a, first, many) in enumerate(PIECES):
        first, many = first * width // 4, many * width // 4
        here = pl.ds(taken, many // 2)
        lane = pl.ds(0, many // 2)
        pieces.append(
            (grads.at[a, pl.ds(first, many)], c_in.at[here], l_in.at[i % RING, lane], b_in.at[here])
        )
        taken += many // 2
    count = len(pieces)
    pieces.append((vec, vc_in, vl_in, vb_in))
    ledger = Ledger(at, dp, pieces, ledger_sems)

    def flush(i):
        a, first, many = PIECES[i]
        rows = pl.ds(first * width // 4, many * width // 4)
        return pltpu.make_async_copy(grads.at[a, rows], far_grads.at[a, rows], out_sems.at[i])

    def slot(number):
        ends, middles, turns, backs, done = SCHEDULE[number]
        if number in VECTORS:
            chosen = [()] * 4
            chosen[VECTORS.index(number)] = (count,)
            ledger.step(*chosen)
        ledger.step(ends, middles, turns, backs)
        for i in done:
            ledger.close(i)
            flush(i).start()

    low = d_pool.astype(BF)
    du_top = (dot_nt(low, twd[...]) * steep).astype(BF)
    dn2b[...] = dot_nt(du_top, twu[...]).astype(BF)
    own_rows = pl.ds(pl.multiple_of(at.h * own_caps, own_caps), own_caps)
    backs = []
    for i, j in enumerate(head_peers):
        there = pl.ds(pl.multiple_of(j * own_caps, own_caps), own_caps)
        backs.append(small(dn2b.at[there], 6 + i, j, rsb.at[at.h]))
    for copy in backs:
        copy.start()
    grads[0] = dot_tn(value, low).astype(BF)
    ledger.open(0, 1)
    grads[1] = dot_tn(n2_top, du_top).astype(BF)
    ledger.open(2, 3)
    vec[...] = jnp.zeros_like(vec)
    vec[22:23, 0:128] = jnp.broadcast_to(lost, (1, 128))
    vec[17:18] = rows_sum(du_top.astype(F32))
    rsb[at.h] = dn2b[own_rows]
    slot(0)
    for copy in backs:
        copy.wait_recv()
    dn2 = rsb[0].astype(F32)
    for j in range(1, 4):
        dn2 = dn2 + rsb[j].astype(F32)
    hat2, rstd2 = norm_stats(ring[at.h])
    dpool_own = z[own_rows]
    dr1_top = dpool_own + norm_back(dn2, hat2, rstd2, vector(tg2))
    vec[8:9] = rows_sum(dr1_top)
    vec[9:10] = rows_sum(dn2 * hat2)
    vec[10:11] = rows_sum(dn2)
    vec[11:12] = rows_sum(dpool_own)

    slot(1)

    da_top = dr1_top.astype(BF)
    a_in[at.h, 1] = da_top
    ws = []
    for j in range(4):
        d_out = dot_nt(da_top, w2[j, 3]).astype(BF)
        s_out[j, 2] = d_out
        ws.append(dot(stack(d_out), w2[j, 2]).astype(BF))
    w_all = jnp.concatenate(ws, 0)
    d_probs = dot_nt(w_all, normed)
    d_scores = probs * (d_probs - jnp.sum(probs * d_probs, -1, keepdims=True))
    scores_low = d_scores.astype(BF)
    g_rows = (dot(scores_low, normed) * scale).astype(BF)
    slot(2)
    d_pooled_low = jnp.zeros((own_caps, width), F32)
    for j in range(4):
        piece = g_rows[j * per : (j + 1) * per]
        f_out[j, 1] = piece
        d_query = pick_heads(dot_nt(piece, w2[j, 1])).astype(BF)
        s_out[j, 1] = d_query
        d_pooled_low = d_pooled_low + dot(d_query, w2[j, 0])
    facts = []
    for i, j in enumerate(head_peers):
        facts.append(small(f_out.at[j, 1], 9 + i, j, f_in.at[at.h, 1]))
        facts.append(small(s_out.at[j], 12 + i, j, s_in.at[at.h]))
        facts.append(small(a_in.at[at.h], 15 + i, j))
    dn = dot_tn(scores_low, u_all) * scale + dot_tn(probs_low, w_all)

    def widen(values):
        values = jnp.broadcast_to(values[:, None, :], (own_caps, slots, width))
        return values.reshape(block, width)

    dn = dn + pcol * widen(d_pooled_low)
    dz = norm_back(dn, hat1, rstd1, vector(tg1)) + pcol * widen(dr1_top)
    dm[own] = dz.astype(BF)
    gathers[1].start()
    for copy in facts:
        copy.start()
    z[...] = dz
    vec[6:7] = rows_sum(dn * hat1)
    vec[7:8] = rows_sum(dn)
    vec[5:6] = rows_sum(dz)

    f_in[at.h] = f_out[at.h]
    s_in[at.h] = s_out[at.h]
    slot(3)
    scatter_a = scatters[1]

    def feed_back(t, carry):
        waits(t, gathers[1])
        blk = block_of(t)
        rows = pl.ds(pl.multiple_of(blk * block, block), block)
        grad = (dot_nt(dm[rows], wd[...]) * slope[rows].astype(F32)).astype(BF)
        slope[rows] = grad
        part[blk] = dot_nt(grad, wu[...]).astype(BF)
        sends(t, scatter_a)
        pl.when(t == 0)(gathers[1].start_rest)
        for i in range(3):
            pl.when(t == i)(lambda: slot(4 + i))
        return carry

    lax.fori_loop(0, 4, feed_back, 0)
    gathers[1].finish()
    for copy in early + facts:
        copy.wait_recv()
    pooled_all = jnp.concatenate([a_in[j, 0] for j in range(4)], 0)
    da_all = jnp.concatenate([a_in[j, 1] for j in range(4)], 0)
    dq_all = jnp.concatenate([s_in[j, 1] for j in range(4)], 0)
    do_all = jnp.concatenate([s_in[j, 2] for j in range(4)], 0)
    out_all = jnp.concatenate([s_in[j, 3] for j in range(4)], 0)
    grads[2, 0:local] = dot_tn(dq_all, pooled_all).astype(BF)
    grads[2, local : 2 * local] = dot_tn(
        jnp.concatenate([stack(s_in[j, 0]) for j in range(4)], 0),
        jnp.concatenate([f_in[j, 1] for j in range(4)], 0),
    ).astype(BF)
    grads[2, 2 * local : 3 * local] = dot_tn(
        jnp.concatenate([stack(s_in[j, 2]) for j in range(4)], 0),
        jnp.concatenate([f_in[j, 0] for j in range(4)], 0),
    ).astype(BF)
    grads[2, 3 * local :] = dot_tn(out_all, da_all).astype(BF)
    ledger.open(4, 5)
    vec[20:21, 0:local] = rows_sum(dq_all.astype(F32))
    vec[21:22, 0:local] = rows_sum(do_all.astype(F32))
    slot(7)
    grads[3] = dot_tn(hid[...], dm[...]).astype(BF)
    ledger.open(6, 7)
    slot(8)
    grads[4] = dot_tn(n2[...], slope[...]).astype(BF)
    ledger.open(8, 9)
    slot(9)
    scatter_a.second()
    vec[16:17] = rows_sum(slope[...].astype(F32))
    slot(10)
    scatter_a.wait()
    dn2 = scatter_a.total()
    scatter_a.finish()
    hat, rstd = norm_stats(r1[...])
    back = z[...] + norm_back(dn2, hat, rstd, vector(g2))
    r1[...] = back
    da[own] = back.astype(BF)
    gathers[2].start()
    vec[2:3] = rows_sum(back)
    vec[3:4] = rows_sum(dn2 * hat)
    vec[4:5] = rows_sum(dn2)

    vh_in[at.h] = vec[0:16]
    tops = [same_place(vh_in.at[at.h], v_sems, i, at.head(j)) for i, j in enumerate(head_peers)]
    for copy in tops:
        copy.start()
    slot(11)
    scatter_b = scatters[2]

    def attend_back(t, carry):
        waits(t, gathers[2])
        blk = block_of(t)
        rows = pl.ds(pl.multiple_of(blk * block, block), block)
        d_out = dot_nt(da[rows], wo_all[at.h]).astype(BF)
        query, keys, values = q[rows], k[rows], v[rows]
        parts = [[], [], []]
        for m in range(block // sub):
            cut = slice(m * sub, (m + 1) * sub)
            index = blk * (block // sub) + m
            dq = jnp.zeros((sub, local), F32)
            dk = jnp.zeros((sub, local), F32)
            dv = jnp.zeros((sub, local), F32)
            for i in range(heads):
                probs_low = p[index, i]
                probs = probs_low.astype(F32)
                d_probs = dot_nt(d_out[cut] * low_masks[i], values[cut])
                d_scores = probs * (d_probs - jnp.sum(probs * d_probs, -1, keepdims=True))
                d_scores = d_scores.astype(BF)
                dq = dq + dot(d_scores, keys[cut]) * masks[i]
                dk = dk + dot_tn(d_scores, query[cut]) * masks[i]
                dv = dv + dot_tn(probs_low, d_out[cut]) * masks[i]
            parts[0].append((dq * scale).astype(BF))
            parts[1].append((dk * scale).astype(BF))
            parts[2].append(dv.astype(BF))
        total = None
        for i in range(3):
            whole = jnp.concatenate(parts[i], 0)
            (q, k, v)[i][rows] = whole
            term = dot(whole, wqkv[i])
            total = term if total is None else total + term
        part[blk] = total.astype(BF)
        sends(t, scatter_b)
        pl.when(t == 0)(gathers[2].start_rest)
        for i in range(3):
            pl.when(t == i)(lambda: slot(12 + i))

        @pl.when(t == 1)
        def _():
            for copy in tops:
                copy.wait_recv()
            vec[0:16] = vh_in[0] + vh_in[1] + vh_in[2] + vh_in[3]
            ledger.open(count)

        return carry

    lax.fori_loop(0, 4, attend_back, 0)
    grads[5, 0:local] = dot_tn(q[...], n1[...]).astype(BF)
    ledger.open(10)
    grads[5, local : 2 * local] = dot_tn(k[...], n1[...]).astype(BF)
    ledger.open(11)
    slot(15)
    grads[5, 2 * local : 3 * local] = dot_tn(v[...], n1[...]).astype(BF)
    ledger.open(12)
    slot(16)
    grads[5, 3 * local :] = dot_tn(o[...], da[...]).astype(BF)
    ledger.open(13)
    slot(17)
    scatter_b.second()
    late[...] = jnp.zeros_like(late)
    late[2:3, 0:local] = rows_sum(q[...].astype(F32))
    late[3:4, 0:local] = rows_sum(v[...].astype(F32))
    slot(18)
    scatter_b.wait()
    dn1 = scatter_b.total()
    hat, rstd = norm_stats(x[own].astype(F32))
    dy[own] = (r1[...] + norm_back(dn1, hat, rstd, vector(g1))).astype(BF)
    gathers[3].start()
    late[0:1] = rows_sum(dn1 * hat)
    late[1:2] = rows_sum(dn1)

    late_in[at.h] = late[...]
    lates = [
        same_place(late_in.at[at.h], v_sems, 3 + i, at.head(j)) for i, j in enumerate(head_peers)
    ]
    for copy in lates:
        copy.start()
    gathers[3].start_rest()
    slot(19)
    for copy in lates:
        copy.wait_recv()
    late_all[place, 0:2] = late_in[0, 0:2] + late_in[1, 0:2] + late_in[2, 0:2] + late_in[3, 0:2]
    late_all[place, 2:8] = late[2:8]
    spreads = [
        same_place(late_all.at[place], sp_sems, i, device) for i, device in enumerate(others)
    ]
    for copy in spreads:
        copy.start()
    slot(20)
    gathers[3].forward()
    slot(21)
    gathers[3].wait_x()
    gathers[3].wait_y()
    slot(22)
    gathers[3].wait_d()
    spill = pltpu.make_async_copy(dy, far_dy, out_sems.at[count])
    spill.start()
    slot(23)
    for copy in spreads:
        copy.wait_recv()
    total = late_all[0]
    for i in range(1, dp * section):
        total = total + late_all[i]
    ledger.close(count)
    vec[0:2] = total[0:2]
    vec[18:20] = total[2:4]
    for i in range(count):
        flush(i).wait()
    spill.wait()
    scatter_b.finish()
    for i in (0, 2, 3):
        gathers[i].finish()
    for copy in hop1 + pass1 + hop_b + hop2 + hop3 + pics + [core_pics]:
        copy.wait_send()
    for copy in wo_hop + wo_pass + wo_core + mixes:
        copy.wait_send()
    for copy in rings + early + sums + tells + backs + facts + tops + lates + spreads:
        copy.wait_send()


def run_kernel(dp, section, slots, x, lens, image, base, top):
    tokens, width = x.shape
    local = base[4].shape[0]
    ff = base[8].shape[1]
    block = tokens // 4
    heads = local // HEAD_DIM
    captions = image.shape[0]
    own_caps = captions // 4
    per = heads * own_caps
    everyone = dp * section * captions
    batch = min(dp, 4)
    others = dp * section - 1
    vmem = pl.BlockSpec(memory_space=pltpu.VMEM)
    hbm = pl.BlockSpec(memory_space=pl.ANY)
    big = (0, 5, 7, 11, 13, 17, 19, 23, 25)
    shape = jax.ShapeDtypeStruct
    outs = [
        shape((tokens, width), BF),
        shape((6, width, width), BF),
        shape((32, width), F32),
    ]
    assert ff == width and 4 * local == width
    sems = pltpu.SemaphoreType.DMA
    ram = pltpu.VMEM
    count = len(PIECES)
    rows = sum(piece[2] for piece in PIECES) * width // 8
    scratch = [
        ram((tokens, width), BF),
        ram((3, local, width), BF),
        ram((4, local, width), BF),
        ram((width, ff), BF),
        ram((ff, width), BF),
        ram((width, ff), BF),
        ram((ff, width), BF),
        ram((tokens, width), BF),
        ram((6, width, width), BF),
        ram((4, block, local), BF),
        ram((tokens, width), BF),
        ram((tokens, local), BF),
        ram((tokens, local), BF),
        ram((tokens, local), BF),
        ram((tokens // 128, heads, 128, 128), BF),
        ram((tokens, local), BF),
        ram((tokens, width), BF),
        ram((tokens, ff), BF),
        ram((tokens, ff), BF),
        ram((block, width), F32),
        ram((block, width), F32),
        ram((4, 4, local, width), BF),
        ram((4, 2, local), F32),
        ram((dp, section, captions, width), BF),
        ram((4, block, width), BF),
        ram((6, block // 2, width), BF),
        ram((4, own_caps, width), F32),
        ram((4, captions, width), BF),
        ram((dp * section, dp // batch, 8, everyone // (dp // batch) // 4), F32),
        ram((captions, everyone), F32),
        ram((captions, width), BF),
        ram((4, own_caps, width), BF),
        ram((4, 2, per, width), BF),
        ram((4, 2, per, width), BF),
        ram((4, 4, own_caps, local), BF),
        ram((4, 4, own_caps, local), BF),
        ram((4, 2, own_caps, width), BF),
        ram((tokens, width), BF),
        ram((rows, width), BF),
        ram((RING, width // 4, width), BF),
        ram((rows, width), BF),
        ram((4, 16, width), F32),
        ram((16, width), F32),
        ram((16, width), F32),
        ram((16, width), F32),
        ram((8, width), F32),
        ram((4, 8, width), F32),
        ram((dp * section, 8, width), F32),
    ]
    for many in ((4, 6), (3, 6), (13,), (3,), (dp,), (others,), (21,), (6,), (others,), (3,), (7,)):
        scratch += [sems(many), sems(many)]
    scratch += [sems((count + 1,))] * 8 + [pltpu.SemaphoreType.REGULAR((count + 1,))]
    scratch += [sems((9,)), sems((count + 1,))]
    return pl.pallas_call(
        functools.partial(kernel, dp, section, slots),
        out_shape=outs,
        in_specs=[hbm if i in big else vmem for i in range(27)],
        out_specs=[hbm, hbm, vmem],
        scratch_shapes=scratch,
        compiler_params=pltpu.CompilerParams(
            collective_id=0, has_side_effects=True, vmem_limit_bytes=VMEM_LIMIT
        ),
        cost_estimate=pl.CostEstimate(
            flops=14 * 10**9, bytes_accessed=40 * 10**6, transcendentals=4 * 10**6
        ),
    )(x, lens, image, *base, *top)


def widen_kernel(local, scale, far_dy, far_grads, vec, *refs):
    loss, text, base, top = refs[0], refs[1], refs[2:14], refs[14:26]
    near_dy, near_grads, wide_text, wide_grads, dy_in, dy_out, g_in, g_out = refs[26:]
    rows = wide_text.shape[0] // 4
    width = wide_text.shape[1]
    incoming = []
    for a in (3, 4, 5, 0, 1, 2):
        for n in range(4):
            span = pl.ds(n * local, local)
            incoming.append(
                pltpu.make_async_copy(
                    far_grads.at[a, span], near_grads.at[a, span], g_in.at[4 * a + n]
                )
            )
    texts = []
    for n in range(4):
        span = pl.ds(n * rows, rows)
        texts.append(pltpu.make_async_copy(far_dy.at[span], near_dy.at[span], dy_in.at[n]))
    for copy in incoming + texts:
        copy.start()
    loss[...] = vec[22:23, 0:1] * scale
    for layer, row, bu, bqv in ((base, 0, 16, 18), (top, 6, 17, 20)):
        layer[0][...] = vec[row]
        layer[1][...] = vec[row + 1]
        layer[3][...] = vec[bqv : bqv + 2, 0:local]
        layer[5][...] = vec[row + 2]
        layer[6][...] = vec[row + 3]
        layer[7][...] = vec[row + 4]
        layer[9][...] = vec[bu]
        layer[11][...] = vec[row + 5]
    outgoing = []
    for i, copy in enumerate(incoming):
        a, n = (3, 4, 5, 0, 1, 2)[i // 4], i % 4
        layer = base if a >= 3 else top
        span = pl.ds(n * local, local)
        copy.wait()
        wide_grads[a, span] = near_grads[a, span].astype(F32)
        if a % 3 == 2:
            target = layer[2].at[n] if n < 3 else layer[4]
        else:
            target = layer[10 if a % 3 == 0 else 8].at[span]
        outgoing.append(
            pltpu.make_async_copy(wide_grads.at[a, span], target, g_out.at[4 * a + n])
        )
        outgoing[-1].start()
    for n, copy in enumerate(texts):
        span = pl.ds(n * rows, rows)
        copy.wait()
        wide_text[span] = near_dy[span].astype(F32)
        outgoing.append(pltpu.make_async_copy(wide_text.at[span], text.at[span], dy_out.at[n]))
        outgoing[-1].start()
    for copy in outgoing:
        copy.wait()


def widen(local, scale, dy, grads, vec):
    tokens, width = dy.shape
    vmem = pl.BlockSpec(memory_space=pltpu.VMEM)
    hbm = pl.BlockSpec(memory_space=pl.ANY)
    shape = jax.ShapeDtypeStruct
    line = (shape((width,), F32), vmem)
    square = (shape((width, width), F32), hbm)
    layer = [
        line,
        line,
        (shape((3, local, width), F32), hbm),
        (shape((2, local), F32), vmem),
        (shape((local, width), F32), hbm),
        line,
        line,
        line,
        square,
        line,
        square,
        line,
    ]
    outs = [(shape((1, 1), F32), vmem), (shape((tokens, width), F32), hbm)] + layer * 2
    sems = pltpu.SemaphoreType.DMA
    return pl.pallas_call(
        functools.partial(widen_kernel, local, scale),
        out_shape=[item[0] for item in outs],
        in_specs=[hbm, hbm, vmem],
        out_specs=[item[1] for item in outs],
        scratch_shapes=[
            pltpu.VMEM((tokens, width), BF),
            pltpu.VMEM((6, width, width), BF),
            pltpu.VMEM((tokens, width), F32),
            pltpu.VMEM((6, width, width), F32),
            sems((4,)),
            sems((4,)),
            sems((24,)),
            sems((24,)),
        ],
        compiler_params=pltpu.CompilerParams(vmem_limit_bytes=VMEM_LIMIT),
        cost_estimate=pl.CostEstimate(
            flops=10**7, bytes_accessed=26 * 10**6, transcendentals=0
        ),
    )(dy, grads, vec)


def on_device(dp, section, text_in, lengths, image_embed, *params):
    base, top = params[:12], params[12:]
    captions, slots, width = text_in.shape
    tokens = captions * slots
    local = base[4].shape[0]

    def layout(layer):
        return layer[:2] + (layer[2].transpose(1, 2, 0),) + layer[3:]

    dy, grads, vec = run_kernel(
        dp,
        section,
        slots,
        text_in.reshape(tokens, width),
        lengths,
        image_embed,
        layout(base),
        layout(top),
    )
    outs = list(widen(local, 0.5 / (dp * section * captions), dy, grads, vec))
    for i in (4, 16):
        outs[i] = outs[i].transpose(2, 0, 1)
    return (outs[0][0, 0], outs[1].reshape(captions, slots, width)) + tuple(outs[2:])


def solution(mesh):
    layer_in = (
        P(),
        P(),
        P(None, None, "head"),
        P(None, "head"),
        P("head", None),
        P(),
        P(),
        P(),
        P(None, "head"),
        P("head"),
        P("head", None),
        P(),
    )
    rows = P(("dp", "section"), None, None)
    return jax.shard_map(
        functools.partial(on_device, mesh.shape["dp"], mesh.shape["section"]),
        mesh=mesh,
        in_specs=(rows, P(("dp", "section")), P(("dp", "section"), None)) + layer_in * 2,
        out_specs=(P(), rows) + layer_in * 2,
        check_vma=False,
    )
```

```python
import functools

import jax
import jax.numpy as jnp
from jax import lax
from jax.experimental import pallas as pl
from jax.experimental.pallas import tpu as pltpu
from jax.sharding import PartitionSpec as P

HEAD_DIM = 64
NORM_EPS = 1e-06
LOGIT_SCALE = 50.0
NEG = -1e30
BF = jnp.bfloat16
F32 = jnp.float32
MESH = pl.DeviceIdType.MESH
VMEM_LIMIT = 63 * 2**20


def dot(a, b):
    return lax.dot_general(a, b, (((1,), (0,)), ((), ())), preferred_element_type=F32)


def dot_nt(a, b):
    return lax.dot_general(a, b, (((1,), (1,)), ((), ())), preferred_element_type=F32)


def dot_tn(a, b):
    return lax.dot_general(a, b, (((0,), (0,)), ((), ())), preferred_element_type=F32)


def norm_stats(values):
    center = jnp.mean(values, -1, keepdims=True)
    shifted = values - center
    spread = jnp.mean(shifted * shifted, -1, keepdims=True)
    rstd = lax.rsqrt(spread + NORM_EPS)
    return shifted * rstd, rstd


def norm_back(grad, hat, rstd, gain):
    scaled = grad * gain
    m1 = jnp.mean(scaled, -1, keepdims=True)
    m2 = jnp.mean(scaled * hat, -1, keepdims=True)
    return rstd * (scaled - m1 - hat * m2)


def rows_sum(values):
    return jnp.sum(values, 0, keepdims=True)


def gelu_pair(u):
    c = 0.7978845608028654
    u2 = u * u
    t = jnp.tanh(c * u * (1.0 + 0.044715 * u2))
    half = 0.5 * (1.0 + t)
    value = u * half
    slope = half + 0.5 * u * (1.0 - t * t) * (c * (1.0 + 3.0 * 0.044715 * u2))
    return value, slope


def head_masks(width, kind):
    lane = lax.broadcasted_iota(jnp.int32, (1, width), 1)
    return [
        jnp.where((lane >= i * HEAD_DIM) & (lane < (i + 1) * HEAD_DIM), 1.0, 0.0).astype(kind)
        for i in range(width // HEAD_DIM)
    ]


class Place:
    def __init__(self):
        self.z = lax.axis_index("dp")
        self.s = lax.axis_index("section")
        h = lax.axis_index("head")
        self.h = h
        self.hi = lax.div(h, 2)
        self.lo = lax.rem(h, 2)
        self.hx = self.block(0, 1)
        self.hy = self.block(1, 0)
        self.hd = self.block(1, 1)

    def block(self, flip_hi, flip_lo):
        return lax.rem(self.hi + flip_hi, 2) * 2 + lax.rem(self.lo + flip_lo, 2)

    def head(self, other):
        return (self.z, self.s, other)

    def greet(self, devices):
        barrier = pltpu.get_barrier_semaphore()
        for device in devices:
            pl.semaphore_signal(barrier, inc=1, device_id=device, device_id_type=MESH)
        return lambda: pl.semaphore_wait(barrier, len(devices))


def remote(src, dst, send_sem, recv_sem, device):
    return pltpu.make_async_remote_copy(
        src_ref=src,
        dst_ref=dst,
        send_sem=send_sem,
        recv_sem=recv_sem,
        device_id=device,
        device_id_type=MESH,
    )


class Gather:
    def __init__(self, at, ref, send, recv, block):
        half = block // 2

        def rows(owner, part):
            return ref.at[pl.ds(pl.multiple_of(owner * block + part * half, half), half)]

        def copy(i, owner, part, target):
            piece = rows(owner, part)
            return remote(piece, piece, send.at[i], recv.at[i], at.head(target))

        self.c = [
            copy(0, at.h, 0, at.hx),
            copy(1, at.h, 1, at.hy),
            copy(2, at.h, 1, at.hx),
            copy(3, at.h, 0, at.hy),
            copy(4, at.hx, 0, at.hy),
            copy(5, at.hy, 1, at.hx),
        ]

    def start(self):
        self.c[0].start()
        self.c[1].start()

    def start_rest(self):
        self.c[2].start()
        self.c[3].start()

    def forward(self):
        self.c[0].wait_recv()
        self.c[4].start()
        self.c[1].wait_recv()
        self.c[5].start()

    def wait_x(self):
        self.c[2].wait_recv()

    def wait_y(self):
        self.c[3].wait_recv()

    def wait_d(self):
        self.c[4].wait_recv()
        self.c[5].wait_recv()

    def finish(self):
        for copy in self.c:
            copy.wait_send()


class Scatter:
    def __init__(self, at, part, got, send, recv, block):
        half = block // 2
        self.at, self.part, self.got, self.half = at, part, got, half

        def piece(owner, side):
            return part.at[owner, pl.ds(side * half, half)]

        def copy(i, owner, side, target):
            return remote(piece(owner, side), got.at[i], send.at[i], recv.at[i], at.head(target))

        self.c = [
            copy(0, at.hd, 0, at.hx),
            copy(1, at.hd, 1, at.hy),
            copy(2, at.hx, 0, at.hx),
            copy(3, at.hy, 1, at.hy),
            copy(4, at.hy, 0, at.hy),
            copy(5, at.hx, 1, at.hx),
        ]

    def send_d(self):
        self.c[0].start()
        self.c[1].start()

    def send_x(self):
        self.c[2].start()

    def send_y(self):
        self.c[3].start()

    def second(self):
        half, part, got, at = self.half, self.part, self.got, self.at
        self.c[0].wait_recv()
        part[at.hy, :half] = (part[at.hy, :half].astype(F32) + got[0].astype(F32)).astype(BF)
        self.c[4].start()
        self.c[1].wait_recv()
        part[at.hx, half:] = (part[at.hx, half:].astype(F32) + got[1].astype(F32)).astype(BF)
        self.c[5].start()

    def wait(self):
        for i in (2, 3, 4, 5):
            self.c[i].wait_recv()

    def total(self):
        half, part, got, at = self.half, self.part, self.got, self.at
        top = part[at.h, :half].astype(F32) + got[2].astype(F32) + got[4].astype(F32)
        low = part[at.h, half:].astype(F32) + got[3].astype(F32) + got[5].astype(F32)
        return jnp.concatenate([top, low], 0)

    def finish(self):
        for copy in self.c:
            copy.wait_send()


class Ledger:
    def __init__(self, at, dp, refs, sems):
        self.at = at
        self.pieces = refs
        self.cs, self.cr, self.ns, self.ar, self.br, self.os, self.fs, self.fr, self.free = sems
        left = at.z < dp // 2
        step = jnp.where(left, 1, -1)
        self.inner = (at.z + step, at.s, at.h)
        self.outer = (at.z - step, at.s, at.h)
        self.core = (at.z, 1 - at.s, at.h)
        self.mid = (at.z == dp // 2 - 1) | (at.z == dp // 2)
        self.outermost = (at.z == 0) | (at.z == dp - 1)

    def rows(self, i, side):
        ref, c, a, b = self.pieces[i]
        half = ref.shape[0] // 2
        return ref.at[pl.ds(pl.multiple_of(side * half, half), half)]

    def swap(self, i):
        c = self.pieces[i][1]
        return remote(self.rows(i, 1 - self.at.s), c, self.cs.at[i], self.cr.at[i], self.core)

    def inward(self, i):
        return remote(
            self.rows(i, self.at.s), self.pieces[i][2], self.ns.at[i], self.ar.at[i], self.inner
        )

    def across(self, i):
        return remote(
            self.rows(i, self.at.s), self.pieces[i][3], self.ns.at[i], self.br.at[i], self.inner
        )

    def outward(self, i):
        return remote(
            self.rows(i, self.at.s), self.pieces[i][3], self.os.at[i], self.br.at[i], self.outer
        )

    def last(self, i):
        mine = self.rows(i, self.at.s)
        return remote(mine, mine, self.fs.at[i], self.fr.at[i], self.core)

    def release(self, i):
        self.swap(i).wait_send()
        pl.semaphore_signal(
            self.free.at[i], inc=1, device_id=self.core, device_id_type=MESH
        )

    def finish(self, i):
        pl.semaphore_wait(self.free.at[i], 1)
        self.last(i).start()

    def add(self, i, *refs):
        mine = self.rows(i, self.at.s)
        total = mine[...].astype(F32)
        for ref in refs:
            total = total + ref[...].astype(F32)
        mine[...] = total.astype(mine.dtype)

    def open(self, *which):
        for i in which:
            self.swap(i).start()

    def step(self, ends=(), middles=(), turns=(), backs=()):
        for i in ends:

            @pl.when(self.outermost)
            def _():
                self.swap(i).wait_recv()
                self.add(i, self.pieces[i][1])
                self.release(i)
                pl.when(self.mid)(lambda: self.across(i).start())
                pl.when(jnp.logical_not(self.mid))(lambda: self.inward(i).start())

        for i in middles:

            @pl.when(jnp.logical_not(self.outermost))
            def _():
                self.swap(i).wait_recv()
                self.inward(i).wait_recv()
                self.add(i, self.pieces[i][1], self.pieces[i][2])
                self.release(i)
                pl.when(self.mid)(lambda: self.across(i).start())
                pl.when(jnp.logical_not(self.mid))(lambda: self.inward(i).start())

        for i in turns:

            @pl.when(self.mid)
            def _():
                self.across(i).wait_recv()
                self.across(i).wait_send()
                self.add(i, self.pieces[i][3])
                pl.when(jnp.logical_not(self.outermost))(lambda: self.outward(i).start())
                self.finish(i)

        for i in backs:

            @pl.when(jnp.logical_not(self.mid))
            def _():
                self.outward(i).wait_recv()
                self.inward(i).wait_send()
                mine = self.rows(i, self.at.s)
                mine[...] = self.pieces[i][3][...]
                pl.when(jnp.logical_not(self.outermost))(lambda: self.outward(i).start())
                self.finish(i)

    def close(self, i):
        self.last(i).wait_recv()
        self.last(i).wait_send()
        pl.when(jnp.logical_not(self.outermost))(lambda: self.outward(i).wait_send())


PIECES = ((0, 0, 2), (0, 2, 2), (1, 0, 2), (1, 2, 2), (2, 0, 2), (2, 2, 2), (3, 0, 2), (3, 2, 2), (4, 0, 2), (4, 2, 2), (5, 0, 1), (5, 1, 1), (5, 2, 1), (5, 3, 1))
RING = 8
HOP_AT, PASS_AT = 2, 2
VECTORS = (14, 15, 18, 19)
SCHEDULE = (
    ((0,), (), (), (), ()),
    ((), (), (), (), ()),
    ((1,), (), (), (), ()),
    ((), (0,), (), (), ()),
    ((2, 3), (1,), (0,), (), ()),
    ((), (), (), (), ()),
    ((), (2,), (1,), (), ()),
    ((), (3,), (), (0,), ()),
    ((4,), (), (), (), ()),
    ((), (), (2,), (), (0,)),
    ((5,), (4,), (), (1,), (1,)),
    ((), (), (3,), (), ()),
    ((6, 7), (5,), (4,), (2, 3), (2,)),
    ((), (6,), (), (), (3,)),
    ((8,), (), (5,), (4,), ()),
    ((9,), (7,), (6,), (), (4,)),
    ((10,), (), (), (5,), ()),
    ((11,), (), (), (), ()),
    ((12, 13), (8, 9), (7,), (), (5,)),
    ((), (10,), (8,), (6,), (6,)),
    ((), (11, 12), (9, 10), (7, 8), (7,)),
    ((), (13,), (11, 12), (9, 10), (8, 9)),
    ((), (), (13,), (11, 12), (10,)),
    ((), (), (), (13,), (11, 12, 13)),
)


def kernel(dp, section, slots, *refs):
    refs = list(refs)

    def take(count):
        out = refs[:count]
        del refs[:count]
        return out

    far_x, lens, image = take(3)
    g1, c1, far_qkv, bqv, far_o, bo, g2, c2, far_u, bu, far_d, bd = take(12)
    tg1, tc1, tqkv, tbqv, two, tbo, tg2, tc2, far_tu, tbu, far_td, tbd = take(12)
    far_dy, far_grads, vec = take(3)
    x, wqkv, wo_all, wu, wd, twu, twd, dy, grads, o_all = take(10)
    n1, q, k, v, p, o, n2, hid, slope, r1, z = take(11)
    w2, b2, images = take(3)
    part, got = take(2)
    ring, arb, stats, scored, dn2b, rsb = take(6)
    f_out, f_in, s_out, s_in, a_in = take(5)
    (da,) = take(1)
    dm = dy
    c_in, l_in, b_in, vh_in, vc_in, vl_in, vb_in, late, late_in, late_all = take(10)
    ag_sems, rs_sems, w_sems, h_sems, i_sems, st_sems, sm_sems, v_sems, sp_sems, o_sems, wo_sems = (
        take(2) for _ in range(11)
    )
    ledger_sems = take(9)
    in_sems, out_sems = take(2)
    assert not refs

    at = Place()
    tokens, width = x.shape
    block = tokens // 4
    local = far_o.shape[0]
    heads = local // HEAD_DIM
    sub = 128
    captions = tokens // slots
    own_caps = block // slots
    caps = captions
    scale = HEAD_DIM ** (-0.5)
    low_masks = head_masks(local, BF)
    masks = head_masks(local, F32)
    other_core = (at.z, 1 - at.s, at.h)
    zs = [(lax.rem(at.z + j, dp), at.s, at.h) for j in range(1, dp)]
    z_pair = (at.z + 1 - 2 * lax.rem(at.z, 2), at.s, at.h)
    head_peers = [at.hx, at.hy, at.hd]
    others = []
    for j in range(dp):
        for i in range(section):
            if i or j:
                others.append((lax.rem(at.z + j, dp), lax.rem(at.s + i, section), at.h))
    own = pl.ds(pl.multiple_of(at.h * block, block), block)

    def vector(ref):
        return ref[...].reshape(1, -1)

    arrive = at.greet([at.head(j) for j in head_peers] + others)
    loads = [
        pltpu.make_async_copy(source, target, in_sems.at[i])
        for i, (source, target) in enumerate(
            (
                (tqkv, w2.at[at.h, 0:3]),
                (two, w2.at[at.h, 3]),
                (far_x, x),
                (far_qkv, wqkv),
                (far_o, wo_all.at[at.h]),
                (far_u, wu),
                (far_d, wd),
                (far_tu, twu),
                (far_td, twd),
            )
        )
    ]
    for copy in loads:
        copy.start()
    pic = image[...].astype(F32)
    pic = pic * lax.rsqrt(jnp.mean(pic * pic, -1, keepdims=True) + NORM_EPS) * width ** (-0.5)
    images[at.z, at.s] = pic.astype(BF)
    b2[at.h] = tbqv[...]

    quarter = local // 4
    mine = lax.rem(at.z, 2) * 2 + at.s
    pair = (1 - lax.rem(at.z, 2)) * 2 + at.s

    def shard_part(owner, which, first=0, many=4):
        rows = pl.ds(pl.multiple_of(which * quarter, quarter), quarter)
        return w2.at[owner, pl.ds(first, many), rows]

    def same_place(ref, sems, i, device):
        return remote(ref, ref, sems[0].at[i], sems[1].at[i], device)

    hop1 = [
        same_place(shard_part(at.h, mine), w_sems, i, at.head(j))
        for i, j in enumerate((at.hx, at.hy))
    ]
    pass1 = [
        same_place(shard_part(at.hx, mine, 0, 2), w_sems, 2, at.head(at.hy)),
        same_place(shard_part(at.hy, mine, 2, 2), w_sems, 3, at.head(at.hx)),
    ]
    hop_b = [same_place(b2.at[at.h], h_sems, i, at.head(j)) for i, j in enumerate(head_peers)]
    hop2 = [
        same_place(shard_part(j, mine), w_sems, 4 + i, z_pair) for i, j in enumerate(head_peers)
    ]
    hop3 = [
        same_place(shard_part(j, which), w_sems, 7 + 3 * n + i, other_core)
        for i, j in enumerate(head_peers)
        for n, which in enumerate((mine, pair))
    ]
    pics = [
        same_place(images.at[at.z, at.s], i_sems, i, device) for i, device in enumerate(zs)
    ]
    core_pics = same_place(images.at[:, at.s], i_sems, dp - 1, other_core)
    half = pl.ds(pl.multiple_of(at.s * (local // 2), local // 2), local // 2)
    wo_hop = [
        same_place(wo_all.at[at.h, half], wo_sems, i, at.head(j))
        for i, j in enumerate((at.hx, at.hy))
    ]

    def wo_part(owner, which):
        piece = local // 4
        first = pl.multiple_of(at.s * (local // 2) + which * piece, piece)
        return wo_all.at[owner, pl.ds(first, piece)]

    wo_pass = [
        same_place(wo_part(at.hx, 0), wo_sems, 2, at.head(at.hy)),
        same_place(wo_part(at.hy, 1), wo_sems, 3, at.head(at.hx)),
    ]
    wo_core = [
        same_place(wo_all.at[j, half], wo_sems, 4 + i, other_core)
        for i, j in enumerate(head_peers)
    ]
    loads[4].wait()
    arrive()
    for copy in wo_hop + hop_b + pics:
        copy.start()
    for copy in loads[:4]:
        copy.wait()

    scatters = [
        Scatter(at, part, got, rs_sems[0].at[i], rs_sems[1].at[i], block) for i in range(3)
    ]
    gathers = [
        Gather(at, ref, ag_sems[0].at[i], ag_sems[1].at[i], block)
        for i, ref in enumerate((n2, dm, da, dy))
    ]

    def block_of(t):
        return lax.rem(at.hi + lax.div(t, 2), 2) * 2 + lax.rem(at.lo + lax.rem(t, 2), 2)

    def limits(first, count):
        cap = lax.broadcasted_iota(jnp.int32, (captions, count), 0)
        slot = lax.broadcasted_iota(jnp.int32, (captions, count), 1)
        chosen = jnp.where(cap == first + slot // slots, 1.0, 0.0).astype(BF)
        row = jnp.broadcast_to(vector(lens).astype(F32), (8, captions)).astype(BF)
        return dot(row, chosen)[:1]

    def key_bias(first, count):
        slot = lax.broadcasted_iota(jnp.int32, (1, count), 1)
        inside = lax.rem(slot, slots).astype(F32) < limits(first, count)
        return jnp.where(inside, 0.0, NEG)

    row_id = lax.broadcasted_iota(jnp.int32, (sub, sub), 0) // slots
    col_id = lax.broadcasted_iota(jnp.int32, (sub, sub), 1) // slots
    same = row_id == col_id
    mixes = [
        remote(
            o.at[pl.ds(pl.multiple_of(j * block, block), block)],
            o_all.at[at.h],
            o_sems[0].at[i],
            o_sems[1].at[i],
            at.head(j),
        )
        for i, j in enumerate((at.hd, at.hy, at.hx))
    ]

    def attend(t, carry):
        blk = block_of(3 - t)
        rows = pl.ds(pl.multiple_of(blk * block, block), block)
        hat, _ = norm_stats(x[rows].astype(F32))
        normed = (hat * vector(g1) + vector(c1)).astype(BF)
        n1[rows] = normed
        query = (dot_nt(normed, wqkv[0]) + bqv[0:1]).astype(BF)
        keys = dot_nt(normed, wqkv[1]).astype(BF)
        values = (dot_nt(normed, wqkv[2]) + bqv[1:2]).astype(BF)
        q[rows] = query
        k[rows] = keys
        v[rows] = values
        mixed = []
        for m in range(block // sub):
            cut = slice(m * sub, (m + 1) * sub)
            index = blk * (block // sub) + m
            bias = jnp.where(same, key_bias(index * (sub // slots), sub), NEG)
            total = jnp.zeros((sub, local), F32)
            for i in range(heads):
                scores = dot_nt(query[cut] * low_masks[i], keys[cut]) * scale + bias
                scores = jnp.exp(scores - jnp.max(scores, -1, keepdims=True))
                probs = (scores * (1.0 / jnp.sum(scores, -1, keepdims=True))).astype(BF)
                p[index, i] = probs
                total = total + dot(probs, values[cut]) * masks[i]
            mixed.append(total.astype(BF))
        mixed = jnp.concatenate(mixed, 0)
        o[rows] = mixed
        for i in range(3):
            pl.when(t == i)(mixes[i].start)

        @pl.when(t == HOP_AT)
        def _():
            for copy in hop1:
                copy.start()

        @pl.when(t == 1)
        def _():
            for copy in wo_hop:
                copy.wait_recv()
            for copy in wo_pass + wo_core[:2]:
                copy.start()

        @pl.when(t == 2)
        def _():
            for copy in wo_pass:
                copy.wait_recv()
            wo_core[2].start()

        @pl.when(t == 3)
        def _():
            o_all[at.h] = mixed

        return carry

    lax.fori_loop(0, 4, attend, 0)
    for copy in mixes + wo_core:
        copy.wait_recv()
    resid = x[own].astype(F32) + vector(bo)
    for j in range(4):
        resid = resid + dot(o_all[j], wo_all[j])
    r1[...] = resid
    hat, _ = norm_stats(resid)
    n2[own] = (hat * vector(g2) + vector(c2)).astype(BF)

    def waits(t, gather):
        @pl.when(t == 1)
        def _():
            gather.forward()
            gather.wait_x()

        pl.when(t == 2)(gather.wait_y)
        pl.when(t == 3)(gather.wait_d)

    def sends(t, scatter):
        pl.when(t == 1)(scatter.send_x)
        pl.when(t == 2)(scatter.send_y)
        pl.when(t == 3)(scatter.send_d)

    gathers[0].start()
    for copy in hop1:
        copy.wait_recv()
    for copy in pass1 + hop2[:2]:
        copy.start()
    for copy in loads[5:7]:
        copy.wait()

    def feed(t, carry):
        waits(t, gathers[0])
        blk = block_of(t)
        rows = pl.ds(pl.multiple_of(blk * block, block), block)
        value, steep = gelu_pair(dot(n2[rows], wu[...]) + vector(bu))
        value = value.astype(BF)
        hid[rows] = value
        slope[rows] = steep.astype(BF)
        part[blk] = dot(value, wd[...]).astype(BF)
        sends(t, scatters[0])
        pl.when(t == 0)(gathers[0].start_rest)

        @pl.when(t == PASS_AT)
        def _():
            for copy in pass1:
                copy.wait_recv()
            hop2[2].start()

        return carry

    lax.fori_loop(0, 4, feed, 0)
    for i in range(3):
        hop2[i].wait_recv()
        hop3[2 * i].start()
        hop3[2 * i + 1].start()
    for copy in pics:
        copy.wait_recv()
    core_pics.start()
    scatters[0].second()
    scatters[0].wait()
    zv = r1[...] + scatters[0].total() + vector(bd)
    scatters[0].finish()
    z[...] = zv
    for copy in hop_b + hop3 + [core_pics]:
        copy.wait_recv()

    per = heads * own_caps

    def stack(values):
        return jnp.concatenate([values * low_masks[i] for i in range(heads)], 0)

    def pick_heads(values):
        total = values[:own_caps] * masks[0]
        for i in range(1, heads):
            total = total + values[i * own_caps : (i + 1) * own_caps] * masks[i]
        return total

    first_cap = at.h * own_caps
    last_slot = limits(first_cap, block) - 1.0
    slot_row = lax.broadcasted_iota(jnp.int32, (own_caps, block), 1)
    cap_row = lax.broadcasted_iota(jnp.int32, (own_caps, block), 0)
    picked = (slot_row // slots == cap_row) & (lax.rem(slot_row, slots).astype(F32) == last_slot)
    pick = jnp.where(picked, 1.0, 0.0).astype(BF)
    cap_of = lax.broadcasted_iota(jnp.int32, (block, captions), 0)
    cap_at = lax.broadcasted_iota(jnp.int32, (block, captions), 1)
    length_col = jnp.sum(
        jnp.where(cap_at == first_cap + cap_of // slots, vector(lens).astype(F32), 0.0),
        1,
        keepdims=True,
    )
    slot_col = lax.rem(lax.broadcasted_iota(jnp.int32, (block, 1), 0), slots).astype(F32)
    pcol = jnp.where(slot_col == length_col - 1.0, 1.0, 0.0)

    hat1, rstd1 = norm_stats(zv)
    normed = (hat1 * vector(tg1) + vector(tc1)).astype(BF)
    pooled_low = dot(pick, normed).astype(BF)
    a_in[at.h, 0] = pooled_low
    z_pool = jnp.sum((zv * pcol).reshape(own_caps, slots, width), 1)
    us = []
    for j in range(4):
        query = (dot_nt(pooled_low, w2[j, 0]) + b2[j, 0:1]).astype(BF)
        s_out[j, 0] = query
        us.append(dot(stack(query), w2[j, 1]).astype(BF))
    u_all = jnp.concatenate(us, 0)
    rows_n = 4 * per
    row_cap = lax.rem(lax.broadcasted_iota(jnp.int32, (rows_n, block), 0), own_caps)
    col_cap = lax.broadcasted_iota(jnp.int32, (rows_n, block), 1) // slots
    bias = jnp.where(row_cap == col_cap, key_bias(first_cap, block), NEG)
    scores = dot_nt(u_all, normed) * scale + bias
    scores = jnp.exp(scores - jnp.max(scores, -1, keepdims=True))
    probs = scores * (1.0 / jnp.sum(scores, -1, keepdims=True))
    probs_low = probs.astype(BF)
    mix = dot(probs_low, normed).astype(BF)
    attended = jnp.zeros((own_caps, width), F32)
    for j in range(4):
        piece = mix[j * per : (j + 1) * per]
        f_out[j, 0] = piece
        out = (pick_heads(dot_nt(piece, w2[j, 2])) + b2[j, 1:2]).astype(BF)
        s_out[j, 1] = out
        attended = attended + dot(out, w2[j, 3])
    ring[at.h] = z_pool + attended + vector(tbo)

    def small(ref, i, j, target=None):
        return remote(
            ref,
            ref if target is None else target,
            sm_sems[0].at[i],
            sm_sems[1].at[i],
            at.head(j),
        )

    for copy in loads[7:]:
        copy.wait()
    rings = [small(ring.at[at.h], i, j) for i, j in enumerate(head_peers)]
    early = [
        small(f_out.at[j, 0], 18 + i, j, f_in.at[at.h, 0]) for i, j in enumerate(head_peers)
    ]
    for i, j in enumerate(head_peers):
        early.append(small(s_out.at[j, pl.ds(0, 2)], 21 + i, j, s_in.at[at.h, pl.ds(0, 2)]))
        early.append(small(a_in.at[at.h, 0], 24 + i, j))
    for copy in rings + early:
        copy.start()
    for copy in rings:
        copy.wait_recv()

    r1_all = ring[...].reshape(caps, width)
    hat2_all, _ = norm_stats(r1_all)
    n2_top = (hat2_all * vector(tg2) + vector(tc2)).astype(BF)
    value, steep = gelu_pair(dot(n2_top, twu[...]) + vector(tbu))
    value = value.astype(BF)
    arb[at.h] = dot(value, twd[...]).astype(BF)
    sums = [small(arb.at[at.h], 3 + i, j) for i, j in enumerate(head_peers)]
    for copy in sums:
        copy.start()
    for copy in sums:
        copy.wait_recv()
    pooled = r1_all + vector(tbd)
    for j in range(4):
        pooled = pooled + arb[j].astype(F32)
    unit_r = lax.rsqrt(jnp.mean(pooled * pooled, -1, keepdims=True) + NORM_EPS)
    text = (pooled * unit_r * width ** (-0.5)).astype(BF)

    everyone = dp * section * caps
    batch = min(dp, 4)
    wide = batch * section * caps
    lanes = wide // 4
    place = at.z * section + at.s

    def chunk_images(n):
        return images[n * batch : (n + 1) * batch].reshape(wide, width)

    def own_columns(n):
        col = lax.broadcasted_iota(jnp.int32, (caps, wide), 1) + n * wide
        row = lax.broadcasted_iota(jnp.int32, (caps, wide), 0) + place * caps
        return col == row

    chunks = [slice(n * wide, (n + 1) * wide) for n in range(dp // batch)]
    row_max = diagonal = None
    for n, cols in enumerate(chunks):
        logits = LOGIT_SCALE * dot_nt(text, chunk_images(n))
        scored[:, cols] = logits
        found = jnp.max(logits, 1, keepdims=True)
        row_max = found if row_max is None else jnp.maximum(row_max, found)
        found = jnp.sum(jnp.where(own_columns(n), logits, 0.0), 1, keepdims=True)
        diagonal = found if diagonal is None else diagonal + found
        col_max = jnp.max(logits, 0, keepdims=True)
        col_sum = jnp.sum(jnp.exp(logits - col_max), 0, keepdims=True)
        for i in range(4):
            stats[place, n, i : i + 1] = col_max[:, i * lanes : (i + 1) * lanes]
            stats[place, n, 4 + i : 5 + i] = col_sum[:, i * lanes : (i + 1) * lanes]
    tells = [
        same_place(stats.at[place], st_sems, i, device) for i, device in enumerate(others)
    ]
    for copy in tells:
        copy.start()
    row_sum = None
    for n, cols in enumerate(chunks):
        found = jnp.sum(jnp.exp(scored[:, cols] - row_max), 1, keepdims=True)
        row_sum = found if row_sum is None else row_sum + found
    row_lse = row_max + jnp.log(row_sum)

    def pull(n, cols, lse):
        steep = jnp.exp(scored[:, cols] - lse) - jnp.where(own_columns(n), 1.0, 0.0)
        return dot((steep * (0.5 / everyone)).astype(BF), chunk_images(n))

    text_grad = None
    for n, cols in enumerate(chunks):
        term = pull(n, cols, row_lse)
        text_grad = term if text_grad is None else text_grad + term
    lost = jnp.sum(row_lse - 2.0 * diagonal, 0, keepdims=True)
    for copy in tells:
        copy.wait_recv()
    for n, cols in enumerate(chunks):
        told = stats[:, n]
        top = jnp.max(told[:, 0:4], 0)
        total = jnp.sum(told[:, 4:8] * jnp.exp(told[:, 0:4] - top[None]), 0)
        lse = top + jnp.log(total)
        col_lse = jnp.concatenate([lse[i : i + 1] for i in range(4)], 1)
        text_grad = text_grad + pull(n, cols, col_lse)
        found = jnp.sum(jnp.where(own_columns(n), col_lse, 0.0), 1, keepdims=True)
        lost = lost + jnp.sum(found, 0, keepdims=True)
    text_grad = LOGIT_SCALE * text_grad
    inner = jnp.mean(pooled * text_grad, -1, keepdims=True)
    d_pool = (unit_r * width ** (-0.5)) * (text_grad - pooled * (unit_r * unit_r * inner))
    z[:caps] = d_pool

    pieces = []
    taken = 0
    for i, (a, first, many) in enumerate(PIECES):
        first, many = first * width // 4, many * width // 4
        here = pl.ds(taken, many // 2)
        lane = pl.ds(0, many // 2)
        pieces.append(
            (grads.at[a, pl.ds(first, many)], c_in.at[here], l_in.at[i % RING, lane], b_in.at[here])
        )
        taken += many // 2
    count = len(pieces)
    pieces.append((vec, vc_in, vl_in, vb_in))
    ledger = Ledger(at, dp, pieces, ledger_sems)

    def flush(i):
        a, first, many = PIECES[i]
        rows = pl.ds(first * width // 4, many * width // 4)
        return pltpu.make_async_copy(grads.at[a, rows], far_grads.at[a, rows], out_sems.at[i])

    def slot(number):
        ends, middles, turns, backs, done = SCHEDULE[number]
        if number in VECTORS:
            chosen = [()] * 4
            chosen[VECTORS.index(number)] = (count,)
            ledger.step(*chosen)
        ledger.step(ends, middles, turns, backs)
        for i in done:
            ledger.close(i)
            flush(i).start()

    low = d_pool.astype(BF)
    du_top = (dot_nt(low, twd[...]) * steep).astype(BF)
    dn2b[...] = dot_nt(du_top, twu[...]).astype(BF)
    own_rows = pl.ds(pl.multiple_of(at.h * own_caps, own_caps), own_caps)
    backs = []
    for i, j in enumerate(head_peers):
        there = pl.ds(pl.multiple_of(j * own_caps, own_caps), own_caps)
        backs.append(small(dn2b.at[there], 6 + i, j, rsb.at[at.h]))
    for copy in backs:
        copy.start()
    grads[0] = dot_tn(value, low).astype(BF)
    ledger.open(0, 1)
    grads[1] = dot_tn(n2_top, du_top).astype(BF)
    ledger.open(2, 3)
    vec[...] = jnp.zeros_like(vec)
    vec[22:23, 0:128] = jnp.broadcast_to(lost, (1, 128))
    vec[17:18] = rows_sum(du_top.astype(F32))
    rsb[at.h] = dn2b[own_rows]
    slot(0)
    for copy in backs:
        copy.wait_recv()
    dn2 = rsb[0].astype(F32)
    for j in range(1, 4):
        dn2 = dn2 + rsb[j].astype(F32)
    hat2, rstd2 = norm_stats(ring[at.h])
    dpool_own = z[own_rows]
    dr1_top = dpool_own + norm_back(dn2, hat2, rstd2, vector(tg2))
    vec[8:9] = rows_sum(dr1_top)
    vec[9:10] = rows_sum(dn2 * hat2)
    vec[10:11] = rows_sum(dn2)
    vec[11:12] = rows_sum(dpool_own)

    slot(1)

    da_top = dr1_top.astype(BF)
    a_in[at.h, 1] = da_top
    ws = []
    for j in range(4):
        d_out = dot_nt(da_top, w2[j, 3]).astype(BF)
        s_out[j, 3] = d_out
        ws.append(dot(stack(d_out), w2[j, 2]).astype(BF))
    w_all = jnp.concatenate(ws, 0)
    d_probs = dot_nt(w_all, normed)
    d_scores = probs * (d_probs - jnp.sum(probs * d_probs, -1, keepdims=True))
    scores_low = d_scores.astype(BF)
    g_rows = (dot(scores_low, normed) * scale).astype(BF)
    slot(2)
    d_pooled_low = jnp.zeros((own_caps, width), F32)
    for j in range(4):
        piece = g_rows[j * per : (j + 1) * per]
        f_out[j, 1] = piece
        d_query = pick_heads(dot_nt(piece, w2[j, 1])).astype(BF)
        s_out[j, 2] = d_query
        d_pooled_low = d_pooled_low + dot(d_query, w2[j, 0])
    facts = []
    for i, j in enumerate(head_peers):
        facts.append(small(f_out.at[j, 1], 9 + i, j, f_in.at[at.h, 1]))
        facts.append(small(s_out.at[j, pl.ds(2, 2)], 12 + i, j, s_in.at[at.h, pl.ds(2, 2)]))
        facts.append(small(a_in.at[at.h, 1], 15 + i, j))
    dn = dot_tn(scores_low, u_all) * scale + dot_tn(probs_low, w_all)

    def widen(values):
        values = jnp.broadcast_to(values[:, None, :], (own_caps, slots, width))
        return values.reshape(block, width)

    dn = dn + pcol * widen(d_pooled_low)
    dz = norm_back(dn, hat1, rstd1, vector(tg1)) + pcol * widen(dr1_top)
    dm[own] = dz.astype(BF)
    gathers[1].start()
    for copy in facts:
        copy.start()
    z[...] = dz
    vec[6:7] = rows_sum(dn * hat1)
    vec[7:8] = rows_sum(dn)
    vec[5:6] = rows_sum(dz)

    f_in[at.h] = f_out[at.h]
    s_in[at.h] = s_out[at.h]
    slot(3)
    scatter_a = scatters[1]

    def feed_back(t, carry):
        waits(t, gathers[1])
        blk = block_of(t)
        rows = pl.ds(pl.multiple_of(blk * block, block), block)
        grad = (dot_nt(dm[rows], wd[...]) * slope[rows].astype(F32)).astype(BF)
        slope[rows] = grad
        part[blk] = dot_nt(grad, wu[...]).astype(BF)
        sends(t, scatter_a)
        pl.when(t == 0)(gathers[1].start_rest)
        for i in range(3):
            pl.when(t == i)(lambda: slot(4 + i))
        return carry

    lax.fori_loop(0, 4, feed_back, 0)
    gathers[1].finish()
    for copy in early + facts:
        copy.wait_recv()
    pooled_all = jnp.concatenate([a_in[j, 0] for j in range(4)], 0)
    da_all = jnp.concatenate([a_in[j, 1] for j in range(4)], 0)
    dq_all = jnp.concatenate([s_in[j, 2] for j in range(4)], 0)
    do_all = jnp.concatenate([s_in[j, 3] for j in range(4)], 0)
    out_all = jnp.concatenate([s_in[j, 1] for j in range(4)], 0)
    grads[2, 0:local] = dot_tn(dq_all, pooled_all).astype(BF)
    grads[2, local : 2 * local] = dot_tn(
        jnp.concatenate([stack(s_in[j, 0]) for j in range(4)], 0),
        jnp.concatenate([f_in[j, 1] for j in range(4)], 0),
    ).astype(BF)
    grads[2, 2 * local : 3 * local] = dot_tn(
        jnp.concatenate([stack(s_in[j, 3]) for j in range(4)], 0),
        jnp.concatenate([f_in[j, 0] for j in range(4)], 0),
    ).astype(BF)
    grads[2, 3 * local :] = dot_tn(out_all, da_all).astype(BF)
    ledger.open(4, 5)
    vec[20:21, 0:local] = rows_sum(dq_all.astype(F32))
    vec[21:22, 0:local] = rows_sum(do_all.astype(F32))
    slot(7)
    grads[3] = dot_tn(hid[...], dm[...]).astype(BF)
    ledger.open(6, 7)
    slot(8)
    grads[4] = dot_tn(n2[...], slope[...]).astype(BF)
    ledger.open(8, 9)
    slot(9)
    scatter_a.second()
    vec[16:17] = rows_sum(slope[...].astype(F32))
    slot(10)
    scatter_a.wait()
    dn2 = scatter_a.total()
    scatter_a.finish()
    hat, rstd = norm_stats(r1[...])
    back = z[...] + norm_back(dn2, hat, rstd, vector(g2))
    r1[...] = back
    da[own] = back.astype(BF)
    gathers[2].start()
    vec[2:3] = rows_sum(back)
    vec[3:4] = rows_sum(dn2 * hat)
    vec[4:5] = rows_sum(dn2)

    vh_in[at.h] = vec[0:16]
    tops = [same_place(vh_in.at[at.h], v_sems, i, at.head(j)) for i, j in enumerate(head_peers)]
    for copy in tops:
        copy.start()
    slot(11)
    scatter_b = scatters[2]

    def attend_back(t, carry):
        waits(t, gathers[2])
        blk = block_of(t)
        rows = pl.ds(pl.multiple_of(blk * block, block), block)
        d_out = dot_nt(da[rows], wo_all[at.h]).astype(BF)
        query, keys, values = q[rows], k[rows], v[rows]
        parts = [[], [], []]
        for m in range(block // sub):
            cut = slice(m * sub, (m + 1) * sub)
            index = blk * (block // sub) + m
            dq = jnp.zeros((sub, local), F32)
            dk = jnp.zeros((sub, local), F32)
            dv = jnp.zeros((sub, local), F32)
            for i in range(heads):
                probs_low = p[index, i]
                probs = probs_low.astype(F32)
                d_probs = dot_nt(d_out[cut] * low_masks[i], values[cut])
                d_scores = probs * (d_probs - jnp.sum(probs * d_probs, -1, keepdims=True))
                d_scores = d_scores.astype(BF)
                dq = dq + dot(d_scores, keys[cut]) * masks[i]
                dk = dk + dot_tn(d_scores, query[cut]) * masks[i]
                dv = dv + dot_tn(probs_low, d_out[cut]) * masks[i]
            parts[0].append((dq * scale).astype(BF))
            parts[1].append((dk * scale).astype(BF))
            parts[2].append(dv.astype(BF))
        total = None
        for i in range(3):
            whole = jnp.concatenate(parts[i], 0)
            (q, k, v)[i][rows] = whole
            term = dot(whole, wqkv[i])
            total = term if total is None else total + term
        part[blk] = total.astype(BF)
        sends(t, scatter_b)
        pl.when(t == 0)(gathers[2].start_rest)
        for i in range(3):
            pl.when(t == i)(lambda: slot(12 + i))

        @pl.when(t == 1)
        def _():
            for copy in tops:
                copy.wait_recv()
            vec[0:16] = vh_in[0] + vh_in[1] + vh_in[2] + vh_in[3]
            ledger.open(count)

        return carry

    lax.fori_loop(0, 4, attend_back, 0)
    grads[5, 0:local] = dot_tn(q[...], n1[...]).astype(BF)
    ledger.open(10)
    grads[5, local : 2 * local] = dot_tn(k[...], n1[...]).astype(BF)
    ledger.open(11)
    slot(15)
    grads[5, 2 * local : 3 * local] = dot_tn(v[...], n1[...]).astype(BF)
    ledger.open(12)
    slot(16)
    grads[5, 3 * local :] = dot_tn(o[...], da[...]).astype(BF)
    ledger.open(13)
    slot(17)
    scatter_b.second()
    late[...] = jnp.zeros_like(late)
    late[2:3, 0:local] = rows_sum(q[...].astype(F32))
    late[3:4, 0:local] = rows_sum(v[...].astype(F32))
    slot(18)
    scatter_b.wait()
    dn1 = scatter_b.total()
    hat, rstd = norm_stats(x[own].astype(F32))
    dy[own] = (r1[...] + norm_back(dn1, hat, rstd, vector(g1))).astype(BF)
    gathers[3].start()
    late[0:1] = rows_sum(dn1 * hat)
    late[1:2] = rows_sum(dn1)

    late_in[at.h] = late[...]
    lates = [
        same_place(late_in.at[at.h], v_sems, 3 + i, at.head(j)) for i, j in enumerate(head_peers)
    ]
    for copy in lates:
        copy.start()
    gathers[3].start_rest()
    slot(19)
    for copy in lates:
        copy.wait_recv()
    late_all[place, 0:2] = late_in[0, 0:2] + late_in[1, 0:2] + late_in[2, 0:2] + late_in[3, 0:2]
    late_all[place, 2:8] = late[2:8]
    spreads = [
        same_place(late_all.at[place], sp_sems, i, device) for i, device in enumerate(others)
    ]
    for copy in spreads:
        copy.start()
    slot(20)
    gathers[3].forward()
    slot(21)
    gathers[3].wait_x()
    gathers[3].wait_y()
    slot(22)
    gathers[3].wait_d()
    spill = pltpu.make_async_copy(dy, far_dy, out_sems.at[count])
    spill.start()
    slot(23)
    for copy in spreads:
        copy.wait_recv()
    total = late_all[0]
    for i in range(1, dp * section):
        total = total + late_all[i]
    ledger.close(count)
    vec[0:2] = total[0:2]
    vec[18:20] = total[2:4]
    for i in range(count):
        flush(i).wait()
    spill.wait()
    scatter_b.finish()
    for i in (0, 2, 3):
        gathers[i].finish()
    for copy in hop1 + pass1 + hop_b + hop2 + hop3 + pics + [core_pics]:
        copy.wait_send()
    for copy in wo_hop + wo_pass + wo_core + mixes:
        copy.wait_send()
    for copy in rings + early + sums + tells + backs + facts + tops + lates + spreads:
        copy.wait_send()


def run_kernel(dp, section, slots, x, lens, image, base, top):
    tokens, width = x.shape
    local = base[4].shape[0]
    ff = base[8].shape[1]
    block = tokens // 4
    heads = local // HEAD_DIM
    captions = image.shape[0]
    own_caps = captions // 4
    per = heads * own_caps
    everyone = dp * section * captions
    batch = min(dp, 4)
    others = dp * section - 1
    vmem = pl.BlockSpec(memory_space=pltpu.VMEM)
    hbm = pl.BlockSpec(memory_space=pl.ANY)
    big = (0, 5, 7, 11, 13, 17, 19, 23, 25)
    shape = jax.ShapeDtypeStruct
    outs = [
        shape((tokens, width), BF),
        shape((6, width, width), BF),
        shape((32, width), F32),
    ]
    assert ff == width and 4 * local == width
    sems = pltpu.SemaphoreType.DMA
    ram = pltpu.VMEM
    count = len(PIECES)
    rows = sum(piece[2] for piece in PIECES) * width // 8
    scratch = [
        ram((tokens, width), BF),
        ram((3, local, width), BF),
        ram((4, local, width), BF),
        ram((width, ff), BF),
        ram((ff, width), BF),
        ram((width, ff), BF),
        ram((ff, width), BF),
        ram((tokens, width), BF),
        ram((6, width, width), BF),
        ram((4, block, local), BF),
        ram((tokens, width), BF),
        ram((tokens, local), BF),
        ram((tokens, local), BF),
        ram((tokens, local), BF),
        ram((tokens // 128, heads, 128, 128), BF),
        ram((tokens, local), BF),
        ram((tokens, width), BF),
        ram((tokens, ff), BF),
        ram((tokens, ff), BF),
        ram((block, width), F32),
        ram((block, width), F32),
        ram((4, 4, local, width), BF),
        ram((4, 2, local), F32),
        ram((dp, section, captions, width), BF),
        ram((4, block, width), BF),
        ram((6, block // 2, width), BF),
        ram((4, own_caps, width), F32),
        ram((4, captions, width), BF),
        ram((dp * section, dp // batch, 8, everyone // (dp // batch) // 4), F32),
        ram((captions, everyone), F32),
        ram((captions, width), BF),
        ram((4, own_caps, width), BF),
        ram((4, 2, per, width), BF),
        ram((4, 2, per, width), BF),
        ram((4, 4, own_caps, local), BF),
        ram((4, 4, own_caps, local), BF),
        ram((4, 2, own_caps, width), BF),
        ram((tokens, width), BF),
        ram((rows, width), BF),
        ram((RING, width // 4, width), BF),
        ram((rows, width), BF),
        ram((4, 16, width), F32),
        ram((16, width), F32),
        ram((16, width), F32),
        ram((16, width), F32),
        ram((8, width), F32),
        ram((4, 8, width), F32),
        ram((dp * section, 8, width), F32),
    ]
    for many in ((4, 6), (3, 6), (13,), (3,), (dp,), (others,), (27,), (6,), (others,), (3,), (7,)):
        scratch += [sems(many), sems(many)]
    scratch += [sems((count + 1,))] * 8 + [pltpu.SemaphoreType.REGULAR((count + 1,))]
    scratch += [sems((9,)), sems((count + 1,))]
    return pl.pallas_call(
        functools.partial(kernel, dp, section, slots),
        out_shape=outs,
        in_specs=[hbm if i in big else vmem for i in range(27)],
        out_specs=[hbm, hbm, vmem],
        scratch_shapes=scratch,
        compiler_params=pltpu.CompilerParams(
            collective_id=0, has_side_effects=True, vmem_limit_bytes=VMEM_LIMIT
        ),
        cost_estimate=pl.CostEstimate(
            flops=14 * 10**9, bytes_accessed=40 * 10**6, transcendentals=4 * 10**6
        ),
    )(x, lens, image, *base, *top)


def widen_kernel(local, scale, far_dy, far_grads, vec, *refs):
    loss, text, base, top = refs[0], refs[1], refs[2:14], refs[14:26]
    near_dy, near_grads, wide_text, wide_grads, dy_in, dy_out, g_in, g_out = refs[26:]
    rows = wide_text.shape[0] // 4
    width = wide_text.shape[1]
    incoming = []
    for a in (3, 4, 5, 0, 1, 2):
        for n in range(4):
            span = pl.ds(n * local, local)
            incoming.append(
                pltpu.make_async_copy(
                    far_grads.at[a, span], near_grads.at[a, span], g_in.at[4 * a + n]
                )
            )
    texts = []
    for n in range(4):
        span = pl.ds(n * rows, rows)
        texts.append(pltpu.make_async_copy(far_dy.at[span], near_dy.at[span], dy_in.at[n]))
    for copy in incoming + texts:
        copy.start()
    loss[...] = vec[22:23, 0:1] * scale
    for layer, row, bu, bqv in ((base, 0, 16, 18), (top, 6, 17, 20)):
        layer[0][...] = vec[row]
        layer[1][...] = vec[row + 1]
        layer[3][...] = vec[bqv : bqv + 2, 0:local]
        layer[5][...] = vec[row + 2]
        layer[6][...] = vec[row + 3]
        layer[7][...] = vec[row + 4]
        layer[9][...] = vec[bu]
        layer[11][...] = vec[row + 5]
    outgoing = []
    for i, copy in enumerate(incoming):
        a, n = (3, 4, 5, 0, 1, 2)[i // 4], i % 4
        layer = base if a >= 3 else top
        span = pl.ds(n * local, local)
        copy.wait()
        wide_grads[a, span] = near_grads[a, span].astype(F32)
        if a % 3 == 2:
            target = layer[2].at[n] if n < 3 else layer[4]
        else:
            target = layer[10 if a % 3 == 0 else 8].at[span]
        outgoing.append(
            pltpu.make_async_copy(wide_grads.at[a, span], target, g_out.at[4 * a + n])
        )
        outgoing[-1].start()
    for n, copy in enumerate(texts):
        span = pl.ds(n * rows, rows)
        copy.wait()
        wide_text[span] = near_dy[span].astype(F32)
        outgoing.append(pltpu.make_async_copy(wide_text.at[span], text.at[span], dy_out.at[n]))
        outgoing[-1].start()
    for copy in outgoing:
        copy.wait()


def widen(local, scale, dy, grads, vec):
    tokens, width = dy.shape
    vmem = pl.BlockSpec(memory_space=pltpu.VMEM)
    hbm = pl.BlockSpec(memory_space=pl.ANY)
    shape = jax.ShapeDtypeStruct
    line = (shape((width,), F32), vmem)
    square = (shape((width, width), F32), hbm)
    layer = [
        line,
        line,
        (shape((3, local, width), F32), hbm),
        (shape((2, local), F32), vmem),
        (shape((local, width), F32), hbm),
        line,
        line,
        line,
        square,
        line,
        square,
        line,
    ]
    outs = [(shape((1, 1), F32), vmem), (shape((tokens, width), F32), hbm)] + layer * 2
    sems = pltpu.SemaphoreType.DMA
    return pl.pallas_call(
        functools.partial(widen_kernel, local, scale),
        out_shape=[item[0] for item in outs],
        in_specs=[hbm, hbm, vmem],
        out_specs=[item[1] for item in outs],
        scratch_shapes=[
            pltpu.VMEM((tokens, width), BF),
            pltpu.VMEM((6, width, width), BF),
            pltpu.VMEM((tokens, width), F32),
            pltpu.VMEM((6, width, width), F32),
            sems((4,)),
            sems((4,)),
            sems((24,)),
            sems((24,)),
        ],
        compiler_params=pltpu.CompilerParams(vmem_limit_bytes=VMEM_LIMIT),
        cost_estimate=pl.CostEstimate(
            flops=10**7, bytes_accessed=26 * 10**6, transcendentals=0
        ),
    )(dy, grads, vec)


def on_device(dp, section, text_in, lengths, image_embed, *params):
    base, top = params[:12], params[12:]
    captions, slots, width = text_in.shape
    tokens = captions * slots
    local = base[4].shape[0]

    def layout(layer):
        return layer[:2] + (layer[2].transpose(1, 2, 0),) + layer[3:]

    dy, grads, vec = run_kernel(
        dp,
        section,
        slots,
        text_in.reshape(tokens, width),
        lengths,
        image_embed,
        layout(base),
        layout(top),
    )
    outs = list(widen(local, 0.5 / (dp * section * captions), dy, grads, vec))
    for i in (4, 16):
        outs[i] = outs[i].transpose(2, 0, 1)
    return (outs[0][0, 0], outs[1].reshape(captions, slots, width)) + tuple(outs[2:])


def solution(mesh):
    layer_in = (
        P(),
        P(),
        P(None, None, "head"),
        P(None, "head"),
        P("head", None),
        P(),
        P(),
        P(),
        P(None, "head"),
        P("head"),
        P("head", None),
        P(),
    )
    rows = P(("dp", "section"), None, None)
    return jax.shard_map(
        functools.partial(on_device, mesh.shape["dp"], mesh.shape["section"]),
        mesh=mesh,
        in_specs=(rows, P(("dp", "section")), P(("dp", "section"), None)) + layer_in * 2,
        out_specs=(P(), rows) + layer_in * 2,
        check_vma=False,
    )
```
